32 devices in a mesh: along: 8 (over y, x, core), cross: 4 (over z).
Axes of the slice: x: 2, y: 2, z: 4, core: 2. Of those that a mesh axis runs over, the one named last changes fastest.
Arguments:
- nadir_view: bfloat16 [2048, 6144], P('along', 'cross'), may hold values from -36 to 36
- forward: bfloat16 [2048, 6144], P('along', 'cross'), may hold values from -36 to 36
- backward: bfloat16 [2048, 6144], P('along', 'cross'), may hold values from -36 to 36
- along_weights: bfloat16 [2, 4, 2048], replicated, may hold values from 0.049804688 to 0.5
- cross_weights: bfloat16 [2, 4, 6144], P(None, None, 'cross'), may hold values from 0.049804688 to 0.5
- band_offsets: int32 [2, 2048], replicated, may hold values from -6 to 6, as said below
- col_offsets: int32 [2, 6144], P(None, 'cross'), may hold values from -6 to 6, as said below
- lag_lines: int32 [2048], replicated, may hold values from 21504 to 21519, as said below
- window_start: int32 [1], replicated, may hold values from 0 to 2095104
Outputs:
- parallax: bfloat16 [2, 2048, 6144], P(None, 'along', 'cross')
- normal_gram: float32 [8, 256, 256], P('along', 'cross')
- normal_rhs: float32 [8, 256], P('along', 'cross')
The draws below stay inside these ranges and needn't reach their ends.
Inputs may be any that keep to these rules, and one draw needn't show every extreme that they name: `lag_lines`: every value in the range occurs in each draw. `band_offsets`: both ends of the range occur in each draw. `col_offsets`: both ends of the range occur in each draw.
All inputs are finite; a program needn't handle non-finite values.
Results may differ from the reference program's by a relative error of at most 0.0065.
Values may be sent and summed in bfloat16 or wider, within the bound.
No kernel may reach another device: no remote copies, remote signals or barrier semaphores. Data moves between devices by JAX's collectives and lax.ppermute only.
A program may use at most 64 MiB of HBM per device.

```python
import jax
import jax.numpy as jnp
from jax import lax

LD = 256
TAPS = 4
OFFA = 6
OFFC = 6
LAG_SPAN = 16
BOX = 4
MODES = 64
STRIP_LINES = 2097152
LINES = 2048
COLS = 6144
LAG_MIN = 21504
COL_RIM = 9
N_ALONG = 8


def image_draw(key, salt):
    seeded = jax.random.fold_in(key, salt)
    noise_key, row_key, col_key = jax.random.split(seeded, 3)
    noise = jnp.clip(jax.random.normal(noise_key, (LINES, COLS), jnp.float32), -4.0, 4.0)
    row_scale = jnp.exp(jax.random.uniform(row_key, (LINES, 1), jnp.float32, jnp.log(0.3), jnp.log(3.0)))
    col_scale = jnp.exp(jax.random.uniform(col_key, (1, COLS), jnp.float32, jnp.log(0.3), jnp.log(3.0)))
    return (noise * row_scale * col_scale).astype(jnp.bfloat16)


def forced_ints(key, count, lowest, highest):
    values = jax.random.randint(key, (count,), lowest, highest + 1, dtype=jnp.int32)
    order = jax.random.permutation(jax.random.fold_in(key, 7), count)
    values = values.at[order[0]].set(highest)
    return values.at[order[1]].set(lowest)


def draw_nadir_view(key, part):
    return image_draw(key, 11)


def draw_forward(key, part):
    return image_draw(key, 12)


def draw_backward(key, part):
    return image_draw(key, 13)


def draw_lag_lines(key, part):
    seeded = jax.random.fold_in(key, 21)
    values = forced_ints(seeded, LINES, LAG_MIN, LAG_MIN + LAG_SPAN - 1)
    order = jax.random.permutation(jax.random.fold_in(seeded, 9), LINES)
    every = LAG_MIN + jnp.arange(LAG_SPAN, dtype=jnp.int32)
    return values.at[order[2:2 + LAG_SPAN]].set(every)


def draw_band_offsets(key, part):
    return forced_ints(jax.random.fold_in(key, 22), 2 * LINES, -OFFA, OFFA).reshape(2, LINES)


def draw_col_offsets(key, part):
    return forced_ints(jax.random.fold_in(key, 23), 2 * COLS, -OFFC, OFFC).reshape(2, COLS)


def shard_levels(stream_key, dims, cuts, least, top_value):
    gain, own = 1.0, jax.random.fold_in(stream_key, 6)
    for axis_at, shards_of in cuts:
        heights = jnp.exp(jax.random.uniform(jax.random.fold_in(own, axis_at), (shards_of,), jnp.float32, least / len(cuts), top_value / len(cuts)))
        gain = gain * jnp.repeat(heights, dims[axis_at] // shards_of).reshape([-1 if axis == axis_at else 1 for axis in range(len(dims))])
    return gain


def setup_inputs(seed: int = 0) -> dict:
    arg_keys = jax.random.split(jax.random.key(seed), 10)
    nadir_view = draw_nadir_view(jax.random.fold_in(arg_keys[9], 71), 0)
    forward = draw_forward(jax.random.fold_in(arg_keys[9], 71), 0)
    backward = draw_backward(jax.random.fold_in(arg_keys[9], 71), 0)
    along_weights = jnp.clip(jax.random.uniform(arg_keys[3], (2, TAPS, LINES), jnp.float32, 0.049804688, 0.5), 0.049804688, 0.5).astype(jnp.bfloat16)
    cross_weights = jnp.clip(0.049804688 + 0.4501953 * jax.random.uniform(arg_keys[4], (2, TAPS, COLS), jnp.float32) ** shard_levels(arg_keys[4], (2, TAPS, COLS), ((2, 4),), -0.2, 0.2), 0.049804688, 0.5).astype(jnp.bfloat16)
    band_offsets = draw_band_offsets(jax.random.fold_in(arg_keys[9], 71), 0)
    col_offsets = draw_col_offsets(jax.random.fold_in(arg_keys[9], 71), 0)
    lag_lines = draw_lag_lines(jax.random.fold_in(arg_keys[9], 71), 0)
    window_start = jax.random.randint(arg_keys[8], (1,), 0, STRIP_LINES - LINES + 1).astype(jnp.int32)
    return {"nadir_view": nadir_view, "forward": forward, "backward": backward, "along_weights": along_weights, "cross_weights": cross_weights, "band_offsets": band_offsets, "col_offsets": col_offsets, "lag_lines": lag_lines, "window_start": window_start}


def harmonics(absolute):
    period = 4 * MODES
    factor = 2 * jnp.arange(MODES, dtype=jnp.int32) + 1
    phases = ((absolute % period)[:, None] * factor[None, :]) % period
    angles = phases.astype(jnp.float32) * (2.0 * jnp.pi / period)
    return jnp.concatenate([jnp.cos(angles), jnp.sin(angles)], axis=1)


def box_mean(values):
    running = values[0:LD]
    for offset in range(1, 2 * BOX + 1):
        running = running + values[offset:offset + LD]
    return running / (2 * BOX + 1)


def resample_slab(slab, sign, weights_along, offsets_along, weights_cross, offsets_cross, lag_lines, lines_ext):
    wrapped = lines_ext % LINES
    source = lines_ext + sign * jnp.take(lag_lines, wrapped) + jnp.take(offsets_along, wrapped)
    tap_range = jnp.arange(TAPS, dtype=jnp.int32)
    row_index = ((source[:, None] + tap_range[None, :]) % LINES).reshape(-1)
    gathered = jnp.take(slab, row_index, axis=0).reshape(lines_ext.shape[0], TAPS, COLS).astype(jnp.float32)
    tap_weights = jnp.take(weights_along, wrapped, axis=1).T.astype(jnp.float32)
    along = jnp.sum(gathered * tap_weights[:, :, None], axis=1).astype(jnp.bfloat16)
    padded = jnp.pad(along, ((0, 0), (COL_RIM, COL_RIM)))
    columns = jnp.arange(COLS, dtype=jnp.int32)
    result = jnp.zeros((lines_ext.shape[0], COLS), jnp.float32)
    for tap_index in range(TAPS):
        picked = jnp.take(padded, columns + offsets_cross + tap_index + COL_RIM, axis=1)
        result = result + picked.astype(jnp.float32) * weights_cross[tap_index].astype(jnp.float32)[None, :]
    return result.astype(jnp.bfloat16)


def reference(nadir_view, forward, backward, along_weights, cross_weights, band_offsets, col_offsets, lag_lines, window_start):
    columns = jnp.arange(COLS, dtype=jnp.int32)
    position = (columns.astype(jnp.float32) + 0.5) / COLS + 0.25
    lever_two = position * position
    lever_three = lever_two * position
    lever_four = lever_two * lever_two
    scale_sum = 1.0 / (LD * COLS)
    scale_pull = 1.0 / (LD * COLS) ** 0.5

    def one_block(block):
        first_line = block * LD
        lines_ext = first_line + jnp.arange(-BOX, LD + BOX, dtype=jnp.int32)
        lead_res = resample_slab(forward, -1, along_weights[0], band_offsets[0], cross_weights[0], col_offsets[0], lag_lines, lines_ext)
        trail_res = resample_slab(backward, 1, along_weights[1], band_offsets[1], cross_weights[1], col_offsets[1], lag_lines, lines_ext)
        nadir_rows = (first_line + jnp.arange(-BOX - 1, LD + BOX + 1, dtype=jnp.int32)) % LINES
        framed = jnp.pad(jnp.take(nadir_view, nadir_rows, axis=0).astype(jnp.float32), ((0, 0), (1, 1)))
        slopes = (framed[2:, :-2] + 2.0 * framed[2:, 1:-1] + framed[2:, 2:] - framed[:-2, :-2] - 2.0 * framed[:-2, 1:-1] - framed[:-2, 2:]) / 4.0
        center = framed[1:-1, 1:-1]
        texture = box_mean(slopes * slopes)
        divisor = jnp.maximum(texture, 0.4)
        lead_est = -box_mean(slopes * (lead_res.astype(jnp.float32) - center)) / divisor
        trail_est = -box_mean(slopes * (trail_res.astype(jnp.float32) - center)) / divisor
        disagree = lead_est + trail_est
        second = jnp.sum(texture * lever_two[None, :], axis=1) * scale_sum
        third = jnp.sum(texture * lever_three[None, :], axis=1) * scale_sum
        fourth = jnp.sum(texture * lever_four[None, :], axis=1) * scale_sum
        pull_one = jnp.sum(texture * disagree * position[None, :], axis=1) * scale_pull
        pull_two = jnp.sum(texture * disagree * lever_two[None, :], axis=1) * scale_pull
        basis_lines = harmonics(window_start[0] + first_line + jnp.arange(LD, dtype=jnp.int32))

        def weighted(coefs):
            return jnp.dot((basis_lines * coefs[:, None]).T, basis_lines, precision=lax.Precision.HIGHEST)

        gram_block = jnp.concatenate([
            jnp.concatenate([weighted(second), weighted(third)], axis=1),
            jnp.concatenate([weighted(third), weighted(fourth)], axis=1)], axis=0)
        rhs_block = jnp.concatenate([
            jnp.dot(basis_lines.T, pull_one, precision=lax.Precision.HIGHEST),
            jnp.dot(basis_lines.T, pull_two, precision=lax.Precision.HIGHEST)])
        parallax_block = jnp.stack([lead_est, trail_est]).astype(jnp.bfloat16)
        return parallax_block, gram_block, rhs_block

    parallax_all, normal_gram, normal_rhs = lax.map(one_block, jnp.arange(N_ALONG, dtype=jnp.int32))
    parallax = jnp.transpose(parallax_all, (1, 0, 2, 3)).reshape(2, LINES, COLS)
    return parallax, normal_gram, normal_rhs
```

```python
import functools

import jax
import jax.numpy as jnp
from jax import lax
from jax.experimental import pallas as pl
from jax.experimental.pallas import tpu as pltpu
from jax.sharding import PartitionSpec as P

TAPS = 4
CAMERA_LAG = 20480
BOX = 4
MODES = 64
LINE_RIM = 32
NADIR_RIM = 16
TILE = 128
WIDE = 256


def pairs_of(count, step):
    return [(i, i + step) for i in range(count) if 0 <= i + step < count]


def harmonics(absolute):
    period = 4 * MODES
    factor = 2 * jnp.arange(MODES, dtype=jnp.int32) + 1
    phases = (absolute % period)[:, None] * factor[None, :] % period
    angles = phases.astype(jnp.float32) * (2.0 * jnp.pi / period)
    return jnp.concatenate([jnp.cos(angles), jnp.sin(angles)], axis=1)


def box_sum(x, lines):
    rows = x.shape[0]
    two = x + pltpu.roll(x, rows - 1, 0)
    four = two + pltpu.roll(two, rows - 2, 0)
    eight = four + pltpu.roll(four, rows - 4, 0)
    return eight[:lines] + x[2 * BOX : lines + 2 * BOX]


def lane_fold(x):
    folded = x[:, :TILE]
    for at in range(TILE, x.shape[1], TILE):
        folded = folded + x[:, at : at + TILE]
    return folded


def prep_kernel(
    lines, cols, nadir, left, right, above, below, line_params, pos,
    slopes, center, texture, inverse, sums, bands, framed,
):
    tall = lines + 2 * NADIR_RIM
    rows = lines + 16
    framed[0:NADIR_RIM, :] = above[...]
    framed[NADIR_RIM + lines : tall, :] = below[...]
    framed[NADIR_RIM : NADIR_RIM + lines, 0:TILE] = left[...]
    framed[NADIR_RIM : NADIR_RIM + lines, TILE : TILE + cols] = nadir[...]
    framed[NADIR_RIM : NADIR_RIM + lines, TILE + cols :] = right[...]
    row = lax.broadcasted_iota(jnp.int32, (2 * WIDE, WIDE), 0)
    col = lax.broadcasted_iota(jnp.int32, (2 * WIDE, WIDE), 1)
    gap = jnp.abs(row - TILE - col)
    smear = jnp.where(gap == 0, 2.0, jnp.where(gap == 1, 1.0, 0.0)).astype(jnp.bfloat16)
    totals = [jnp.zeros((lines, TILE), jnp.float32) for _ in range(3)]
    for at in range(0, cols, WIDE):
        across = jnp.dot(
            framed[:, at : at + 2 * WIDE], smear, preferred_element_type=jnp.float32
        )
        change = pltpu.roll(across, tall - 5, 0) - pltpu.roll(across, tall - 3, 0)
        slope = change[8 : 8 + rows] * 0.25
        slopes[:, at : at + WIDE] = slope
        middle = framed[:, TILE + at : TILE + at + WIDE].astype(jnp.float32)
        center[:, at : at + WIDE] = pltpu.roll(middle, tall - 4, 0)[8 : 8 + rows]
        level = box_sum(slope * slope, lines) * (1.0 / (2 * BOX + 1))
        texture[:, at : at + WIDE] = level
        inverse[:, at : at + WIDE] = (-1.0 / (2 * BOX + 1)) / jnp.maximum(level, 0.4)
        for k in range(3):
            totals[k] = totals[k] + lane_fold(level * pos[k + 1 : k + 2, at : at + WIDE])
    lane = lax.broadcasted_iota(jnp.int32, (lines, TILE), 1)
    packed = jnp.zeros((lines, TILE), jnp.float32)
    for k in range(3):
        packed = jnp.where(lane == k, jnp.sum(totals[k], axis=1, keepdims=True), packed)
    sums[...] = packed
    half = lines // 2
    depth = half + 2 * LINE_RIM
    for s in range(2):
        for first, last in ((0, half), (half, rows)):
            at = lax.broadcasted_iota(jnp.int32, (last - first, depth), 1).astype(jnp.float32)
            distance = at + float(first) - line_params[first:last, 5 * s : 5 * s + 1]
            band = jnp.zeros((last - first, depth), jnp.float32)
            for tap in range(TAPS):
                weight = line_params[first:last, 5 * s + 1 + tap : 5 * s + 2 + tap]
                band = jnp.where(distance == float(tap), weight, band)
            bands[s, first:last, :] = band.astype(jnp.bfloat16)


def slab_kernel(
    lines, cols, s, first, width, spans, fresh,
    slopes, center, texture, inverse, bands, col_params, pos, basis, earlier,
    above, below, left, right, edges, ends, *rest,
):
    count = len(spans)
    interiors = rest[:count]
    rest = rest[count + (0 if fresh else 1) :]
    parallax, pulled, ext, along, slope_v, center_v, texture_v, inverse_v, result, sem = rest
    rows = lines + 16
    half = lines // 2
    depth = half + 2 * LINE_RIM
    low, high = first, first + width + 2 * TILE
    copies = []

    def fetch(source, target):
        copy = pltpu.make_async_copy(source, target, sem.at[len(copies)])
        copy.start()
        copies.append(copy)

    def place(ref, lead, row, span, height, begin, end):
        a, b = max(begin, low), min(end, high)
        if a < b:
            fetch(
                ref.at[lead + (pl.ds(row, height), pl.ds(a - begin + span[0], b - a))],
                ext.at[pl.ds(span[1], height), pl.ds(a - low, b - a)],
            )

    whole = cols + 2 * TILE
    place(above, (s,), 0, (0, 0), LINE_RIM, 0, whole)
    place(below, (s,), 0, (0, LINE_RIM + lines), LINE_RIM, 0, whole)
    place(left, (s,), 0, (0, LINE_RIM), lines, 0, TILE)
    place(edges, (s,), 0, (0, LINE_RIM), lines, TILE, 2 * TILE)
    place(ends, (s,), 0, (0, LINE_RIM), LINE_RIM, 2 * TILE, cols)
    place(ends, (s,), LINE_RIM, (0, lines), LINE_RIM, 2 * TILE, cols)
    place(edges, (s,), 0, (TILE, LINE_RIM), lines, cols, cols + TILE)
    place(right, (s,), 0, (0, LINE_RIM), lines, cols + TILE, whole)
    for ref, (begin, end) in zip(interiors, spans):
        place(ref, (), 0, (0, 2 * LINE_RIM), lines - 2 * LINE_RIM, begin, end)
    loaded = len(copies)
    columns = pl.ds(first, width)
    fetch(slopes.at[:, columns], slope_v)
    fetch(center.at[:, columns], center_v)
    fetch(inverse.at[:, columns], inverse_v)
    fetch(texture.at[:, columns], texture_v)
    for copy in copies[:loaded]:
        copy.wait()
    for at in range(0, width + 2 * TILE, WIDE):
        end = min(at + WIDE, width + 2 * TILE)
        for start, stop in ((0, half), (half, rows)):
            along[start:stop, at:end] = jnp.dot(
                bands[s, start:stop, :],
                ext[start : start + depth, at:end],
                preferred_element_type=jnp.float32,
            ).astype(jnp.bfloat16)
    for copy in copies[loaded:]:
        copy.wait()
    pulls = [jnp.zeros((lines, TILE), jnp.float32) for _ in range(2)]
    for at in range(0, width, WIDE):
        span = min(WIDE, width - at)
        place_of = slice(first + at, first + at + span)
        row = lax.broadcasted_iota(jnp.int32, (span + 2 * TILE, span), 0)
        col = lax.broadcasted_iota(jnp.int32, (span + 2 * TILE, span), 1)
        distance = (row - col - TILE).astype(jnp.float32) - col_params[8 * s : 8 * s + 1, place_of]
        band = jnp.zeros((span + 2 * TILE, span), jnp.float32)
        for tap in range(TAPS):
            weight = col_params[8 * s + 1 + tap : 8 * s + 2 + tap, place_of]
            band = jnp.where(distance == float(tap), weight, band)
        resampled = jnp.dot(
            along[:, at : at + span + 2 * TILE],
            band.astype(jnp.bfloat16),
            preferred_element_type=jnp.float32,
        ).astype(jnp.bfloat16)
        here = slice(at, at + span)
        mismatch = resampled.astype(jnp.float32) - center_v[:, here]
        estimate = box_sum(slope_v[:, here] * mismatch, lines) * inverse_v[:, here]
        result[:, here] = estimate.astype(jnp.bfloat16)
        weighted = texture_v[:, here] * estimate
        for k in range(2):
            pulls[k] = pulls[k] + lane_fold(weighted * pos[k : k + 1, place_of])
    out = pltpu.make_async_copy(result, parallax.at[s, :, columns], sem.at[len(copies)])
    out.start()
    pulled[...] = earlier[...]
    for k in range(2):
        per_line = jnp.sum(pulls[k], axis=1, keepdims=True)
        pulled[k : k + 1, :] += jnp.sum(basis[...] * per_line, axis=0, keepdims=True)
    out.wait()


def local(
    nadir_view, forward, backward, along_weights, cross_weights, band_offsets, col_offsets,
    lag_lines, window_start,
):
    lines, cols = nadir_view.shape
    along_count = lax.axis_size("along")
    cross_count = lax.axis_size("cross")
    along_index = lax.axis_index("along")
    cross_index = lax.axis_index("cross")
    total_lines = lines * along_count
    total_cols = cols * cross_count
    half_ring = along_count // 2
    lag_floor = CAMERA_LAG // total_lines * total_lines + half_ring * lines
    rows = lines + 16
    whole = cols + 2 * TILE
    low_z, high_z = pairs_of(cross_count, -1), pairs_of(cross_count, 1)
    ring_down = [(i, (i - 1) % along_count) for i in range(along_count)]
    ring_up = [(i, (i + 1) % along_count) for i in range(along_count)]
    half_down, half_up = [], []
    for i in range(along_count):
        base = i // half_ring * half_ring
        half_down.append((i, base + (i - base - 1) % half_ring))
        half_up.append((i, base + (i - base + 1) % half_ring))
    across = [(i, (i + half_ring) % along_count) for i in range(along_count)]

    def over(value):
        return lax.ppermute(value, "along", across)

    inner = slice(TILE, cols - TILE)
    slabs = (forward, backward)
    edges = over(
        jnp.stack([jnp.concatenate([v[:, :TILE], v[:, cols - TILE :]], axis=1) for v in slabs])
    )
    ends = over(
        jnp.stack(
            [
                jnp.concatenate([v[:LINE_RIM, inner], v[lines - LINE_RIM :, inner]], axis=0)
                for v in slabs
            ]
        )
    )
    tiles = cols // TILE - 2
    cuts = [tiles - 6, tiles - 3, tiles - 1, tiles] if tiles > 6 else [tiles]
    body = slice(LINE_RIM, lines - LINE_RIM)

    def after(value, *others):
        return lax.optimization_barrier((value, *others))[0]

    lead_inner = over(after(forward[body, inner], edges))
    trail_spans, trail_parts, begin = [], [], 0
    for n, cut in enumerate(cuts):
        start, stop = TILE + begin * TILE, TILE + cut * TILE
        piece = backward[body, start:stop]
        if n == 0:
            piece = after(piece, ends)
        elif n < 3:
            piece = after(piece, lead_inner)
        else:
            piece = after(piece, trail_parts[n - 3])
        trail_parts.append(over(piece))
        trail_spans.append((start + TILE, stop + TILE))
        begin = cut

    def rim(v):
        return jnp.concatenate([v[:LINE_RIM], v[lines - LINE_RIM :]], axis=0)

    raw_left = jnp.concatenate([v[:, :TILE] for v in (nadir_view, rim(forward), rim(backward))])
    raw_right = jnp.concatenate(
        [v[:, cols - TILE :] for v in (nadir_view, rim(forward), rim(backward))]
    )
    from_right = lax.ppermute(raw_left, "cross", low_z)
    from_left = lax.ppermute(raw_right, "cross", high_z)
    nadir_left, nadir_right = from_left[:lines], from_right[:lines]

    def widened(v, left, right):
        return jnp.concatenate([left, v, right], axis=-1)

    first_lines = widened(nadir_view[:NADIR_RIM], nadir_left[:NADIR_RIM], nadir_right[:NADIR_RIM])
    last_lines = widened(
        nadir_view[lines - NADIR_RIM :],
        nadir_left[lines - NADIR_RIM :],
        nadir_right[lines - NADIR_RIM :],
    )
    nadir_below = lax.ppermute(first_lines, "along", ring_down)
    nadir_above = lax.ppermute(last_lines, "along", ring_up)

    def window(v):
        padded = jnp.concatenate([v[..., total_lines - BOX :], v, v[..., : rows - lines]], axis=-1)
        return lax.dynamic_slice_in_dim(padded, along_index * lines, rows, v.ndim - 1)

    excess = lag_lines - lag_floor
    own = jnp.arange(rows, dtype=jnp.int32) + (LINE_RIM - BOX)
    starts = own[None] + window(jnp.stack([band_offsets[0] - excess, band_offsets[1] + excess]))
    tap_rows = window(along_weights).astype(jnp.float32)
    starts = starts.astype(jnp.float32)
    line_params = jnp.concatenate(
        [starts[0:1], tap_rows[0], starts[1:2], tap_rows[1], jnp.zeros((6, rows), jnp.float32)]
    ).T
    gap = jnp.zeros((3, cols), jnp.float32)
    shift = col_offsets.astype(jnp.float32)
    taps = cross_weights.astype(jnp.float32)
    col_params = jnp.concatenate([shift[0:1], taps[0], gap, shift[1:2], taps[1], gap])
    columns = cross_index * cols + jnp.arange(cols, dtype=jnp.int32)
    position = (columns.astype(jnp.float32) + 0.5) / total_cols + 0.25
    square = position * position
    pos = jnp.stack([position, square, square * position, square * square] + [position] * 4)
    basis = harmonics(window_start[0] + along_index * lines + jnp.arange(lines, dtype=jnp.int32))

    f32, bf16 = jnp.float32, jnp.bfloat16
    depth = lines // 2 + 2 * LINE_RIM
    limit = pltpu.CompilerParams(vmem_limit_bytes=40 * 1024 * 1024)
    slopes, center, texture, inverse, sums, bands = pl.pallas_call(
        functools.partial(prep_kernel, lines, cols),
        out_shape=(
            jax.ShapeDtypeStruct((rows, cols), f32),
            jax.ShapeDtypeStruct((rows, cols), f32),
            jax.ShapeDtypeStruct((lines, cols), f32),
            jax.ShapeDtypeStruct((lines, cols), f32),
            jax.ShapeDtypeStruct((lines, TILE), f32),
            jax.ShapeDtypeStruct((2, rows, depth), bf16),
        ),
        scratch_shapes=[pltpu.VMEM((lines + 2 * NADIR_RIM, whole), bf16)],
        compiler_params=limit,
        cost_estimate=pl.CostEstimate(
            flops=2 * rows * cols * 512, bytes_accessed=12 * rows * cols, transcendentals=0
        ),
        name="prep",
    )(nadir_view, nadir_left, nadir_right, nadir_above, nadir_below, line_params, pos)

    scale_sum = 1.0 / (lines * total_cols)
    scale_pull = 1.0 / (lines * total_cols) ** 0.5
    line_sums = sums[:, :8].T * scale_sum
    step = 1
    while step < cross_count:
        line_sums = line_sums + lax.ppermute(
            line_sums, "cross", [(i, i ^ step) for i in range(cross_count)]
        )
        step *= 2
    row_count = 4 * MODES // cross_count
    row_first = cross_index * row_count
    upper = row_first + jnp.arange(row_count, dtype=jnp.int32) >= 2 * MODES
    doubled = jnp.concatenate([basis, basis], axis=1)
    basis_rows = lax.dynamic_slice_in_dim(doubled, row_first, row_count, 1)
    left_coef = jnp.where(upper[None, :], line_sums[1][:, None], line_sums[0][:, None])
    right_coef = jnp.where(upper[None, :], line_sums[2][:, None], line_sums[1][:, None])
    weighted = jnp.concatenate([basis_rows * left_coef, basis_rows * right_coef], axis=1)
    grams = jnp.dot(weighted.T, basis, precision=lax.Precision.HIGHEST)
    normal_gram = jnp.concatenate([grams[:row_count], grams[row_count:]], axis=1)[None]

    slab_right = lax.ppermute(edges[:, :, :TILE], "cross", low_z)
    slab_left = lax.ppermute(edges[:, :, TILE:], "cross", high_z)

    def full_lines(at, ends_at):
        span = slice(at, at + LINE_RIM)
        crossed = jnp.concatenate(
            [
                slab_left[:, span],
                edges[:, span, :TILE],
                ends[:, ends_at : ends_at + LINE_RIM],
                edges[:, span, TILE:],
                slab_right[:, span],
            ],
            axis=2,
        )
        raw = []
        for s, slab in enumerate(slabs):
            halo = slice(
                lines + 2 * LINE_RIM * s + ends_at, lines + 2 * LINE_RIM * s + ends_at + LINE_RIM
            )
            raw.append(widened(slab[span], from_left[halo], from_right[halo]))
        return crossed, jnp.stack(raw)

    in_half = along_index % half_ring
    crossed_top, raw_top = full_lines(0, 0)
    crossed_bottom, raw_bottom = full_lines(lines - LINE_RIM, LINE_RIM)
    send_down = jnp.where(in_half == 0, raw_top, crossed_top)
    send_up = jnp.where(in_half == half_ring - 1, raw_bottom, crossed_bottom)
    slab_below = lax.ppermute(send_down, "along", half_down)
    slab_above = lax.ppermute(send_up, "along", half_up)

    def run(s, first, width, parts, spans, earlier, parallax):
        fresh = parallax is None
        any_space = pl.BlockSpec(memory_space=pl.ANY)
        vmem = pl.BlockSpec(memory_space=pltpu.VMEM)
        operands = [
            slopes, center, texture, inverse, bands, col_params, pos, basis, earlier,
            slab_above, slab_below, slab_left, slab_right, edges, ends, *parts,
        ]
        specs = [any_space] * 4 + [vmem] * 5 + [any_space] * (6 + len(parts))
        aliases = {}
        if not fresh:
            aliases = {len(operands): 0}
            operands.append(parallax)
            specs.append(any_space)
        return pl.pallas_call(
            functools.partial(slab_kernel, lines, cols, s, first, width, spans, fresh),
            out_shape=(
                jax.ShapeDtypeStruct((2, lines, cols), bf16),
                jax.ShapeDtypeStruct((8, TILE), f32),
            ),
            in_specs=specs,
            out_specs=(any_space, vmem),
            scratch_shapes=[
                pltpu.VMEM((lines + 2 * LINE_RIM, width + 2 * TILE), bf16),
                pltpu.VMEM((rows, width + 2 * TILE), bf16),
                pltpu.VMEM((rows, width), f32),
                pltpu.VMEM((rows, width), f32),
                pltpu.VMEM((lines, width), f32),
                pltpu.VMEM((lines, width), f32),
                pltpu.VMEM((lines, width), bf16),
                pltpu.SemaphoreType.DMA((16 + len(parts),)),
            ],
            input_output_aliases=aliases,
            compiler_params=limit,
            cost_estimate=pl.CostEstimate(
                flops=2 * rows * (width + 256) * 900,
                bytes_accessed=20 * rows * width,
                transcendentals=0,
            ),
            name=f"slab{s}_{first}",
        )(*operands)

    nothing = jnp.zeros((8, TILE), f32)
    lead_span = (2 * TILE, cols)
    parallax, pulled = run(0, 0, cols, [lead_inner], [lead_span], nothing, None)
    done = 0
    for n, cut in enumerate(cuts):
        upto = cols if n == len(cuts) - 1 else cut * TILE
        parts, spans = [], []
        for part, span in zip(trail_parts[: n + 1], trail_spans):
            if span[1] > done:
                parts.append(part)
                spans.append(span)
        parallax, pulled = run(1, done, upto - done, parts, spans, pulled, parallax)
        done = upto

    total = pulled
    for shift_by in range(1, cross_count):
        total = total + lax.ppermute(
            pulled, "cross", [(i, (i + shift_by) % cross_count) for i in range(cross_count)]
        )
    flat = total[:2].reshape(1, 4 * MODES) * scale_pull
    normal_rhs = lax.dynamic_slice_in_dim(flat, row_first, row_count, 1)
    return parallax, normal_gram, normal_rhs


def solution(mesh):
    placed = (
        P("along", "cross"),
        P("along", "cross"),
        P("along", "cross"),
        P(),
        P(None, None, "cross"),
        P(),
        P(None, "cross"),
        P(),
        P(),
    )
    return jax.shard_map(
        local,
        mesh=mesh,
        in_specs=placed,
        out_specs=(P(None, "along", "cross"), P("along", "cross", None), P("along", "cross")),
        check_vma=False,
    )
```

```python
import functools
import math

import jax
import jax.numpy as jnp
from jax import lax
from jax.experimental import pallas as pl
from jax.experimental.pallas import tpu as pltpu
from jax.sharding import PartitionSpec as P

TAPS = 4
CAMERA_LAG = 20480
BOX = 4
MODES = 64
LINE_RIM = 32
NADIR_RIM = 16
TILE = 128
WIDE = 256
EDGE = 16


def pairs_of(count, step):
    return [(i, i + step) for i in range(count) if 0 <= i + step < count]


def harmonics(absolute):
    period = 4 * MODES
    factor = 2 * jnp.arange(MODES, dtype=jnp.int32) + 1
    phases = (absolute % period)[:, None] * factor[None, :] % period
    angles = phases.astype(jnp.float32) * (2.0 * jnp.pi / period)
    return jnp.concatenate([jnp.cos(angles), jnp.sin(angles)], axis=1)


def box_sum(x, lines):
    rows = x.shape[0]
    two = x + pltpu.roll(x, rows - 1, 0)
    four = two + pltpu.roll(two, rows - 2, 0)
    eight = four + pltpu.roll(four, rows - 4, 0)
    return eight[:lines] + x[2 * BOX : lines + 2 * BOX]


def lane_fold(x):
    folded = x[:, :TILE]
    for at in range(TILE, x.shape[1], TILE):
        folded = folded + x[:, at : at + TILE]
    return folded


def copy_all(moves, sem):
    copies = [pltpu.make_async_copy(a, b, sem.at[n]) for n, (a, b) in enumerate(moves)]
    for copy in copies:
        copy.start()
    for copy in copies:
        copy.wait()


def pack_kernel(lines, cols, nadir, forward, backward, first, last, near_first, near_last, side, sem):
    moves = []
    for n, (begin, near) in enumerate(((0, near_first), (cols - TILE, near_last))):
        moves.append((nadir.at[:, pl.ds(begin, TILE)], near.at[pl.ds(0, lines), :]))
        for s, slab in enumerate((forward, backward)):
            moves.append((slab.at[:, pl.ds(begin, TILE)], side.at[s, n]))
    copy_all(moves, sem)
    for n, (row, packed, near) in enumerate(((0, first, near_first), (TILE - EDGE, last, near_last))):
        for s in range(2):
            turned = side[s, n].astype(jnp.float32).T[row : row + EDGE].astype(jnp.bfloat16)
            packed[:, s * lines : (s + 1) * lines] = turned
            for k in range(lines // TILE):
                at = lines + (s * (lines // TILE) + k) * EDGE
                near[at : at + EDGE, :] = turned[:, k * TILE : (k + 1) * TILE]


def cut_kernel(lines, spans, backward, ends, *rest):
    moves = []
    for n, row in enumerate((0, lines - LINE_RIM)):
        moves.append((backward.at[pl.ds(row, LINE_RIM), :], ends.at[pl.ds(n * LINE_RIM, LINE_RIM), :]))
    body = pl.ds(LINE_RIM, lines - 2 * LINE_RIM)
    for (begin, end), part in zip(spans, rest):
        moves.append((backward.at[body, pl.ds(begin, end - begin)], part))
    copy_all(moves, rest[-1])


def nadir_lines_kernel(lines, cols, nadir, from_left, from_right, first, last, sem):
    moves = []
    for out, row in ((first, 0), (last, lines - NADIR_RIM)):
        span = pl.ds(row, NADIR_RIM)
        moves.append((from_left.at[span, :], out.at[:, pl.ds(0, TILE)]))
        moves.append((nadir.at[span, :], out.at[:, pl.ds(TILE, cols)]))
        moves.append((from_right.at[span, :], out.at[:, pl.ds(TILE + cols, TILE)]))
    copy_all(moves, sem)


def lines_kernel(
    lines, cols, half_ring, place, forward, backward, near_left, near_right,
    lead, ends, left, right, down, up, sem,
):
    in_half = lax.rem(place[0], half_ring)
    packed = pl.ds(2 * LINE_RIM, EDGE)
    for out, row, n, raw_place in (
        (down, 0, 0, 0),
        (up, lines - LINE_RIM, 1, half_ring - 1),
    ):
        span = pl.ds(row, LINE_RIM)
        out[2 * LINE_RIM :, 4 * lines :] = jnp.zeros((EDGE, cols - 4 * lines), jnp.bfloat16)

        @pl.when(in_half == raw_place)
        def _(out=out, span=span):
            moves = [(slab.at[span, :], out.at[pl.ds(s * LINE_RIM, LINE_RIM), :]) for s, slab in enumerate((forward, backward))]
            for n, near in enumerate((near_left, near_right)):
                for k in range(2 * lines // TILE):
                    moves.append(
                        (
                            near.at[pl.ds(lines + k * EDGE, EDGE), :],
                            out.at[packed, pl.ds(2 * n * lines + k * TILE, TILE)],
                        )
                    )
            copy_all(moves, sem)

        @pl.when(in_half != raw_place)
        def _(out=out, span=span, n=n):
            moves = [
                (lead.at[span, :], out.at[pl.ds(0, LINE_RIM), :]),
                (ends.at[pl.ds(n * LINE_RIM, LINE_RIM), :], out.at[pl.ds(LINE_RIM, LINE_RIM), :]),
                (left, out.at[packed, pl.ds(0, 2 * lines)]),
                (right, out.at[packed, pl.ds(2 * lines, 2 * lines)]),
            ]
            copy_all(moves, sem)


def positions(place, cols, total_cols, at, span):
    column = lax.broadcasted_iota(jnp.int32, (1, span), 1) + (place[1] * cols + at)
    position = (column.astype(jnp.float32) + 0.5) / total_cols + 0.25
    return position, position * position


def prep_kernel(
    lines, cols, total_lines, total_cols, lag_floor, place,
    nadir, left, right, above, below, lag, offsets, weights,
    slopes, center, texture, sums, bands, framed, slope_v, center_v, texture_v, bands_v, sem,
):
    tall = lines + 2 * NADIR_RIM
    rows = lines + 16
    framed[0:NADIR_RIM, :] = above[...]
    framed[NADIR_RIM + lines : tall, :] = below[...]
    framed[NADIR_RIM : NADIR_RIM + lines, 0:TILE] = left[0:lines, :]
    framed[NADIR_RIM : NADIR_RIM + lines, TILE : TILE + cols] = nadir[...]
    framed[NADIR_RIM : NADIR_RIM + lines, TILE + cols :] = right[0:lines, :]
    row = lax.broadcasted_iota(jnp.int32, (2 * WIDE, WIDE), 0)
    col = lax.broadcasted_iota(jnp.int32, (2 * WIDE, WIDE), 1)
    gap = jnp.abs(row - TILE - col)
    smear = jnp.where(gap == 0, 2.0, jnp.where(gap == 1, 1.0, 0.0)).astype(jnp.bfloat16)
    totals = [jnp.zeros((lines, TILE), jnp.float32) for _ in range(3)]
    copies = []
    for at in range(0, cols, WIDE):
        across = jnp.dot(
            framed[:, at : at + 2 * WIDE], smear, preferred_element_type=jnp.float32
        )
        change = pltpu.roll(across, tall - 5, 0) - pltpu.roll(across, tall - 3, 0)
        slope = change[8 : 8 + rows] * 0.25
        slope_v[:, at : at + WIDE] = slope
        middle = framed[:, TILE + at : TILE + at + WIDE].astype(jnp.float32)
        middle = pltpu.roll(middle, tall - 4, 0)[8 : 8 + rows]
        center_v[:, at : at + WIDE] = middle.astype(jnp.bfloat16)
        level = box_sum(slope * slope, lines) * (1.0 / (2 * BOX + 1))
        texture_v[:, at : at + WIDE] = level
        for source, target in ((slope_v, slopes), (center_v, center), (texture_v, texture)):
            window = (slice(None), pl.ds(at, WIDE))
            copy = pltpu.make_async_copy(source.at[window], target.at[window], sem.at[len(copies)])
            copy.start()
            copies.append(copy)
        position, square = positions(place, cols, total_cols, at, WIDE)
        for k, lever in enumerate((square, square * position, square * square)):
            totals[k] = totals[k] + lane_fold(level * lever)
    lane = lax.broadcasted_iota(jnp.int32, (lines, TILE), 1)
    packed = jnp.zeros((lines, TILE), jnp.float32)
    for k in range(3):
        packed = jnp.where(lane == k, jnp.sum(totals[k], axis=1, keepdims=True), packed)
    sums[...] = packed.T[0:8, :] * (1.0 / (lines * total_cols))
    begin = place[0] * lines
    ahead = pl.multiple_of(lax.rem(begin + total_lines - TILE, total_lines), TILE)
    behind = pl.multiple_of(lax.rem(begin + lines, total_lines), TILE)
    begin = pl.multiple_of(begin, TILE)

    def window(ref, lead):
        parts = [
            ref[lead + (slice(None), pl.ds(start, size))].astype(jnp.float32)
            for start, size in ((ahead, TILE), (begin, lines), (behind, TILE))
        ]
        return jnp.concatenate(parts, axis=1)

    wide = lines + 2 * TILE
    lags = window(lag, ()) - float(lag_floor)
    shifts = window(offsets, ())
    stacked = jnp.concatenate(
        [
            jnp.broadcast_to(shifts[0:1] - lags, (8, wide)),
            jnp.broadcast_to(shifts[1:2] + lags, (8, wide)),
            window(weights, (0,)),
            window(weights, (1,)),
            jnp.zeros((TILE - 24, wide), jnp.float32),
        ],
        axis=0,
    )
    as_columns = pltpu.roll(stacked.T, wide - (TILE - BOX), 0)[0:rows]
    half = lines // 2
    depth = half + 2 * LINE_RIM
    for s in range(2):
        for first, last in ((0, half), (half, rows)):
            at = lax.broadcasted_iota(jnp.int32, (last - first, depth), 1)
            own = lax.broadcasted_iota(jnp.int32, (last - first, depth), 0)
            distance = (at - own - (LINE_RIM - BOX)).astype(jnp.float32)
            distance = distance - as_columns[first:last, 8 * s : 8 * s + 1]
            band = jnp.zeros((last - first, depth), jnp.float32)
            for tap in range(TAPS):
                weight = as_columns[first:last, 16 + 4 * s + tap : 17 + 4 * s + tap]
                band = jnp.where(distance == float(tap), weight, band)
            bands_v[s, first:last, :] = band.astype(jnp.bfloat16)
    copy = pltpu.make_async_copy(bands_v, bands, sem.at[len(copies)])
    copy.start()
    for waited in (*copies, copy):
        waited.wait()


def slab_kernel(
    lines, cols, s, first, width, spans, fresh,
    slopes, center, texture, bands, params, basis, earlier, above, below, left, right, *rest,
):
    sources = rest[: len(spans)]
    rest = rest[len(spans) + (0 if fresh else 1) :]
    (
        parallax, pulled, ext, along, slope_v, center_v, texture_v, bands_v, params_v, basis_v,
        earlier_v, packed, result, sem,
    ) = rest
    rows = lines + 16
    half = lines // 2
    depth = half + 2 * LINE_RIM
    low, high = first - TILE, first + width + TILE
    copies = []

    def fetch(source, target):
        copy = pltpu.make_async_copy(source, target, sem.at[len(copies)])
        copy.start()
        copies.append(copy)

    def place(ref, row, target, height, begin, end):
        a, b = max(begin, low), min(end, high)
        if a < b:
            fetch(
                ref.at[pl.ds(row, height), pl.ds(a - begin, b - a)],
                ext.at[pl.ds(target, height), pl.ds(a - low, b - a)],
            )

    fetch(bands.at[s], bands_v)
    place(above, s * LINE_RIM, 0, LINE_RIM, 0, cols)
    place(below, s * LINE_RIM, LINE_RIM + lines, LINE_RIM, 0, cols)
    for ref, (row, target, height, begin, end) in zip(sources, spans):
        place(ref, row, target, height, begin, end)
    sides = [n for n in range(2) if (low < 0, high > cols)[n]]
    for n in sides:
        window = pl.ds((2 * n + s) * lines, lines)
        for k, ref in enumerate((above, below)):
            fetch(ref.at[pl.ds(2 * LINE_RIM, EDGE), window], packed.at[n, k])
        fetch((left, right)[n].at[:, pl.ds(s * lines, lines)], packed.at[n, 2])
    loaded = len(copies)
    columns = pl.ds(first, width)
    fetch(params.at[:, columns], params_v)
    fetch(slopes.at[:, columns], slope_v)
    fetch(center.at[:, columns], center_v)
    fetch(texture.at[:, columns], texture_v)
    fetch(basis, basis_v)
    fetch(earlier, earlier_v)
    for copy in copies[:loaded]:
        copy.wait()
    for n in sides:
        at = 0 if n == 0 else width + TILE
        blank = jnp.zeros((TILE - EDGE, lines), jnp.float32)
        for k, (source, target, height) in enumerate(
            ((lines - LINE_RIM, 0, LINE_RIM), (0, LINE_RIM + lines, LINE_RIM), (0, LINE_RIM, lines))
        ):
            piece = packed[n, k].astype(jnp.float32)
            piece = jnp.concatenate([blank, piece] if n == 0 else [piece, blank], axis=0)
            turned = piece.T[source : source + height].astype(jnp.bfloat16)
            ext[target : target + height, at : at + TILE] = turned
    for at in range(0, width + 2 * TILE, WIDE):
        end = min(at + WIDE, width + 2 * TILE)
        for start, stop in ((0, half), (half, rows)):
            along[start:stop, at:end] = jnp.dot(
                bands_v[start:stop, :],
                ext[start : start + depth, at:end],
                preferred_element_type=jnp.float32,
            ).astype(jnp.bfloat16)
    for copy in copies[loaded:]:
        copy.wait()
    pulls = [jnp.zeros((lines, TILE), jnp.float32) for _ in range(2)]
    for at in range(0, width, WIDE):
        span = min(WIDE, width - at)
        here = slice(at, at + span)
        row = lax.broadcasted_iota(jnp.int32, (span + 2 * EDGE, span), 0)
        col = lax.broadcasted_iota(jnp.int32, (span + 2 * EDGE, span), 1)
        distance = (row - col - EDGE).astype(jnp.float32) - params_v[8 * s : 8 * s + 1, here]
        band = jnp.zeros((span + 2 * EDGE, span), jnp.float32)
        for tap in range(TAPS):
            weight = params_v[8 * s + 1 + tap : 8 * s + 2 + tap, here]
            band = jnp.where(distance == float(tap), weight, band)
        blank = jnp.zeros((TILE - EDGE, span), jnp.bfloat16)
        resampled = jnp.dot(
            along[:, at : at + span + 2 * TILE],
            jnp.concatenate([blank, band.astype(jnp.bfloat16), blank], axis=0),
            preferred_element_type=jnp.float32,
        ).astype(jnp.bfloat16)
        mismatch = resampled.astype(jnp.float32) - center_v[:, here].astype(jnp.float32)
        level = texture_v[:, here]
        inverse = (-1.0 / (2 * BOX + 1)) / jnp.maximum(level, 0.4)
        estimate = box_sum(slope_v[:, here] * mismatch, lines) * inverse
        result[:, here] = estimate.astype(jnp.bfloat16)
        weighted = level * estimate
        for k in range(2):
            pulls[k] = pulls[k] + lane_fold(weighted * params_v[16 + k : 17 + k, here])
    out = pltpu.make_async_copy(result, parallax.at[s, :, columns], sem.at[len(copies)])
    out.start()
    pulled[...] = earlier_v[...]
    for k in range(2):
        per_line = jnp.sum(pulls[k], axis=1, keepdims=True)
        pulled[k : k + 1, :] += jnp.sum(basis_v[...] * per_line, axis=0, keepdims=True)
    out.wait()


def local(
    nadir_view, forward, backward, along_weights, cross_weights, band_offsets, col_offsets,
    lag_lines, window_start,
):
    lines, cols = nadir_view.shape
    along_count = lax.axis_size("along")
    cross_count = lax.axis_size("cross")
    along_index = lax.axis_index("along")
    cross_index = lax.axis_index("cross")
    total_lines = lines * along_count
    total_cols = cols * cross_count
    half_ring = along_count // 2
    lag_floor = CAMERA_LAG // total_lines * total_lines + half_ring * lines
    rows = lines + 16
    whole = cols + 2 * TILE
    low_z, high_z = pairs_of(cross_count, -1), pairs_of(cross_count, 1)
    ring_down = [(i, (i - 1) % along_count) for i in range(along_count)]
    ring_up = [(i, (i + 1) % along_count) for i in range(along_count)]
    half_down, half_up = [], []
    for i in range(along_count):
        base = i // half_ring * half_ring
        half_down.append((i, base + (i - base - 1) % half_ring))
        half_up.append((i, base + (i - base + 1) % half_ring))
    across = [(i, (i + half_ring) % along_count) for i in range(along_count)]

    def aslant(pairs):
        return [(a * cross_count + c, b * cross_count + d) for a, b in across for c, d in pairs]

    def over(value):
        return lax.ppermute(value, "along", across)

    def after(value, *others):
        return lax.optimization_barrier((value, *others))[0]

    def hbm(value):
        return pltpu.with_memory_space_constraint(value, pltpu.HBM)

    f32, bf16 = jnp.float32, jnp.bfloat16
    any_space = pl.BlockSpec(memory_space=pl.ANY)
    vmem = pl.BlockSpec(memory_space=pltpu.VMEM)
    smem = pl.BlockSpec(memory_space=pltpu.SMEM)
    limit = pltpu.CompilerParams(vmem_limit_bytes=24 * 1024 * 1024)

    def mover(kernel, name, shapes, operands, copies, scalars=0, scratch=()):
        return pl.pallas_call(
            kernel,
            out_shape=tuple(jax.ShapeDtypeStruct(shape, bf16) for shape in shapes),
            in_specs=[smem] * scalars + [any_space] * (len(operands) - scalars),
            out_specs=(vmem,) * len(shapes),
            scratch_shapes=[*scratch, pltpu.SemaphoreType.DMA((copies,))],
            compiler_params=limit,
            cost_estimate=pl.CostEstimate(
                flops=0, bytes_accessed=4 * sum(math.prod(s) for s in shapes), transcendentals=0
            ),
            name=name,
        )(*operands[:scalars], *(hbm(v) for v in operands[scalars:]))

    lead = over(forward)
    near = lines + 2 * EDGE * lines // TILE
    first, last, near_first, near_last = mover(
        functools.partial(pack_kernel, lines, cols),
        "pack",
        ((EDGE, 2 * lines), (EDGE, 2 * lines), (near, TILE), (near, TILE)),
        (nadir_view, forward, backward),
        6,
        scratch=[pltpu.VMEM((2, 2, lines, TILE), bf16)],
    )
    slab_right = lax.ppermute(first, ("along", "cross"), aslant(low_z))
    slab_left = lax.ppermute(last, ("along", "cross"), aslant(high_z))
    from_right = lax.ppermute(near_first, "cross", low_z)
    from_left = lax.ppermute(near_last, "cross", high_z)

    cuts = [0, cols - 3 * TILE, cols]
    spans = list(zip(cuts[:-1], cuts[1:]))
    height = lines - 2 * LINE_RIM
    ends, *parts = mover(
        functools.partial(cut_kernel, lines, spans),
        "cut",
        ((2 * LINE_RIM, cols), *((height, end - begin) for begin, end in spans)),
        (after(backward, first),),
        2 + len(spans),
    )
    ends = over(ends)

    place = jnp.stack([along_index, cross_index]).astype(jnp.int32)
    gap = jnp.zeros((3, cols), f32)
    shift = col_offsets.astype(f32)
    taps = cross_weights.astype(f32)
    columns = cross_index * cols + jnp.arange(cols, dtype=jnp.int32)
    position = ((columns.astype(f32) + 0.5) / total_cols + 0.25)[None]
    params = jnp.concatenate(
        [shift[0:1], taps[0], gap, shift[1:2], taps[1], gap, position, position * position, gap, gap]
    )
    basis = harmonics(window_start[0] + along_index * lines + jnp.arange(lines, dtype=jnp.int32))

    first_lines, last_lines = mover(
        functools.partial(nadir_lines_kernel, lines, cols),
        "nadir_lines",
        ((NADIR_RIM, whole), (NADIR_RIM, whole)),
        (nadir_view, from_left, from_right),
        6,
    )
    nadir_below = lax.ppermute(first_lines, "along", ring_down)
    nadir_above = lax.ppermute(last_lines, "along", ring_up)
    depth = lines // 2 + 2 * LINE_RIM
    slopes, center, texture, sums, bands = pl.pallas_call(
        functools.partial(prep_kernel, lines, cols, total_lines, total_cols, lag_floor),
        out_shape=(
            pltpu.HBM((rows, cols), f32),
            pltpu.HBM((rows, cols), bf16),
            pltpu.HBM((lines, cols), f32),
            jax.ShapeDtypeStruct((8, lines), f32),
            pltpu.HBM((2, rows, depth), bf16),
        ),
        in_specs=[smem] + [vmem] * 8,
        out_specs=(any_space, any_space, any_space, vmem, any_space),
        scratch_shapes=[
            pltpu.VMEM((lines + 2 * NADIR_RIM, whole), bf16),
            pltpu.VMEM((rows, cols), f32),
            pltpu.VMEM((rows, cols), bf16),
            pltpu.VMEM((lines, cols), f32),
            pltpu.VMEM((2, rows, depth), bf16),
            pltpu.SemaphoreType.DMA((3 * (cols // WIDE) + 1,)),
        ],
        compiler_params=limit,
        cost_estimate=pl.CostEstimate(
            flops=2 * rows * cols * 512, bytes_accessed=12 * rows * cols, transcendentals=0
        ),
        name="prep",
    )(
        place, hbm(after(nadir_view, params, basis, parts[0])), hbm(from_left), hbm(from_right),
        hbm(nadir_above), hbm(nadir_below), lag_lines[None], hbm(band_offsets), hbm(along_weights),
    )

    down, up = mover(
        functools.partial(lines_kernel, lines, cols, half_ring),
        "lines",
        ((2 * LINE_RIM + EDGE, cols), (2 * LINE_RIM + EDGE, cols)),
        (
            place, forward, backward, from_left, from_right, after(lead, sums), ends,
            slab_left, slab_right,
        ),
        2 + 4 * lines // TILE,
        1,
    )
    slab_below = lax.ppermute(down, "along", half_down)
    slab_above = lax.ppermute(up, "along", half_up)
    for n in range(len(parts)):
        parts[n] = over(after(parts[n], from_left if n == 0 else ends))

    def run(s, begin, end, sources, spans, earlier, parallax):
        fresh = parallax is None
        width = end - begin
        operands = [
            slopes, center, texture, bands, params, basis, earlier, slab_above, slab_below,
            slab_left, slab_right, *sources,
        ]
        aliases = {}
        if not fresh:
            aliases = {len(operands): 0}
            operands.append(parallax)
        return pl.pallas_call(
            functools.partial(slab_kernel, lines, cols, s, begin, width, spans, fresh),
            out_shape=(
                pltpu.HBM((2, lines, cols), bf16),
                jax.ShapeDtypeStruct((8, TILE), f32),
            ),
            in_specs=[any_space] * len(operands),
            out_specs=(any_space, vmem),
            scratch_shapes=[
                pltpu.VMEM((lines + 2 * LINE_RIM, width + 2 * TILE), bf16),
                pltpu.VMEM((rows, width + 2 * TILE), bf16),
                pltpu.VMEM((rows, width), f32),
                pltpu.VMEM((rows, width), bf16),
                pltpu.VMEM((lines, width), f32),
                pltpu.VMEM((rows, depth), bf16),
                pltpu.VMEM((24, width), f32),
                pltpu.VMEM((lines, TILE), f32),
                pltpu.VMEM((8, TILE), f32),
                pltpu.VMEM((2, 3, EDGE, lines), bf16),
                pltpu.VMEM((lines, width), bf16),
                pltpu.SemaphoreType.DMA((20 + len(sources),)),
            ],
            input_output_aliases=aliases,
            compiler_params=limit,
            cost_estimate=pl.CostEstimate(
                flops=2 * rows * (width + 256) * 900,
                bytes_accessed=20 * rows * width,
                transcendentals=0,
            ),
            name=f"slab{s}_{begin}",
        )(*(hbm(v) for v in operands))

    nothing = jnp.zeros((8, TILE), f32)
    lead_span = (0, LINE_RIM, lines, 0, cols)
    parallax, pulled = run(0, 0, cols, [lead], [lead_span], nothing, None)
    ends_spans = [(0, LINE_RIM, LINE_RIM, 0, cols), (LINE_RIM, lines, LINE_RIM, 0, cols)]
    done = 0
    for n, (_, cut) in enumerate(spans):
        upto = cols if cut == cols else cut - TILE
        use = [k for k in range(n + 1) if spans[k][1] > done - TILE]
        held = [(0, 2 * LINE_RIM, height, *spans[k]) for k in use]
        parallax, pulled = run(
            1, done, upto, [ends, ends, *(parts[k] for k in use)], ends_spans + held, pulled, parallax
        )
        done = upto

    share = jnp.concatenate([sums, pulled], axis=1)
    total = share
    for shift_by in range(1, cross_count):
        total = total + lax.ppermute(
            share, "cross", [(i, (i + shift_by) % cross_count) for i in range(cross_count)]
        )
    scale_pull = 1.0 / (lines * total_cols) ** 0.5
    line_sums = total[:, :lines]
    row_count = 4 * MODES // cross_count
    row_first = cross_index * row_count
    upper = row_first + jnp.arange(row_count, dtype=jnp.int32) >= 2 * MODES
    doubled = jnp.concatenate([basis, basis], axis=1)
    basis_rows = lax.dynamic_slice_in_dim(doubled, row_first, row_count, 1)
    left_coef = jnp.where(upper[None, :], line_sums[1][:, None], line_sums[0][:, None])
    right_coef = jnp.where(upper[None, :], line_sums[2][:, None], line_sums[1][:, None])
    weighted = jnp.concatenate([basis_rows * left_coef, basis_rows * right_coef], axis=1)
    grams = jnp.dot(weighted.T, basis, precision=lax.Precision.HIGHEST)
    normal_gram = jnp.concatenate([grams[:row_count], grams[row_count:]], axis=1)[None]
    flat = total[:2, lines:].reshape(1, 4 * MODES) * scale_pull
    normal_rhs = lax.dynamic_slice_in_dim(flat, row_first, row_count, 1)
    return parallax, normal_gram, normal_rhs


def solution(mesh):
    placed = (
        P("along", "cross"),
        P("along", "cross"),
        P("along", "cross"),
        P(),
        P(None, None, "cross"),
        P(),
        P(None, "cross"),
        P(),
        P(),
    )
    return jax.shard_map(
        local,
        mesh=mesh,
        in_specs=placed,
        out_specs=(P(None, "along", "cross"), P("along", "cross", None), P("along", "cross")),
        check_vma=False,
    )
```

```python
import functools
import math

import jax
import jax.numpy as jnp
from jax import lax
from jax.experimental import pallas as pl
from jax.experimental.pallas import tpu as pltpu
from jax.sharding import PartitionSpec as P

TAPS = 4
CAMERA_LAG = 20480
BOX = 4
MODES = 64
LINE_RIM = 32
NADIR_RIM = 16
TILE = 128
WIDE = 256
EDGE = 16


def pairs_of(count, step):
    return [(i, i + step) for i in range(count) if 0 <= i + step < count]


def harmonics(absolute):
    period = 4 * MODES
    factor = 2 * jnp.arange(MODES, dtype=jnp.int32) + 1
    phases = (absolute % period)[:, None] * factor[None, :] % period
    angles = phases.astype(jnp.float32) * (2.0 * jnp.pi / period)
    return jnp.concatenate([jnp.cos(angles), jnp.sin(angles)], axis=1)


def box_sum(x, lines):
    rows = x.shape[0]
    two = x + pltpu.roll(x, rows - 1, 0)
    four = two + pltpu.roll(two, rows - 2, 0)
    eight = four + pltpu.roll(four, rows - 4, 0)
    return eight[:lines] + x[2 * BOX : lines + 2 * BOX]


def lane_fold(x):
    folded = x[:, :TILE]
    for at in range(TILE, x.shape[1], TILE):
        folded = folded + x[:, at : at + TILE]
    return folded


def copy_all(moves, sem):
    copies = [pltpu.make_async_copy(a, b, sem.at[n]) for n, (a, b) in enumerate(moves)]
    for copy in copies:
        copy.start()
    for copy in copies:
        copy.wait()


def pack_kernel(
    lines, cols, nadir, forward, backward, crossing, near_first, near_last, side, sem
):
    moves = []
    for n, (begin, near) in enumerate(((0, near_first), (cols - TILE, near_last))):
        moves.append((nadir.at[:, pl.ds(begin, TILE)], near.at[pl.ds(0, lines), :]))
        for s, slab in enumerate((forward, backward)):
            moves.append((slab.at[:, pl.ds(begin, TILE)], side.at[s, n]))
    copy_all(moves, sem)
    for n, (row, near) in enumerate(((0, near_first), (TILE - EDGE, near_last))):
        for s in range(2):
            turned = side[s, n].astype(jnp.float32).T[row : row + EDGE].astype(jnp.bfloat16)
            for k in range(lines // TILE):
                at = lines + (s * (lines // TILE) + k) * EDGE
                near[at : at + EDGE, :] = turned[:, k * TILE : (k + 1) * TILE]


def cross_kernel(lines, forward, backward, crossing, sem):
    moves = [(forward, crossing.at[pl.ds(0, lines), :])]
    for n, row in enumerate((0, lines - LINE_RIM)):
        target = pl.ds(lines + n * LINE_RIM, LINE_RIM)
        moves.append((backward.at[pl.ds(row, LINE_RIM), :], crossing.at[target, :]))
    copy_all(moves, sem)


def nadir_lines_kernel(lines, cols, nadir, from_left, from_right, params, basis, first, last, sem):
    moves = []
    for out, row in ((first, 0), (last, lines - NADIR_RIM)):
        span, top = pl.ds(row, NADIR_RIM), pl.ds(0, NADIR_RIM)
        moves.append((from_left.at[span, :], out.at[top, pl.ds(0, TILE)]))
        moves.append((nadir.at[span, :], out.at[top, pl.ds(TILE, cols)]))
        moves.append((from_right.at[span, :], out.at[top, pl.ds(TILE + cols, TILE)]))
        for n, near in enumerate((from_left, from_right)):
            for k in range(2 * lines // TILE):
                moves.append(
                    (
                        near.at[pl.ds(lines + k * EDGE, EDGE), :],
                        out.at[pl.ds(NADIR_RIM, EDGE), pl.ds(2 * n * lines + k * TILE, TILE)],
                    )
                )
        out[NADIR_RIM:, 4 * lines :] = jnp.zeros((EDGE, cols + 2 * TILE - 4 * lines), jnp.bfloat16)
    copy_all(moves, sem)


def middle_kernel(lines, cols, backward, own, above, below, middle, sem):
    height = lines - 2 * LINE_RIM
    row, packed = pl.ds(height, EDGE), slice(NADIR_RIM, NADIR_RIM + EDGE)
    moves = [
        (backward.at[pl.ds(LINE_RIM, height), :], middle.at[pl.ds(0, height), :]),
        (
            own.at[pl.ds(NADIR_RIM, EDGE), pl.ds(0, 4 * lines)],
            middle.at[row, pl.ds(0, 4 * lines)],
        ),
    ]
    lane = lax.broadcasted_iota(jnp.int32, (EDGE, TILE), 1)
    for k in range(4):
        ahead = above[packed, (k + 1) * lines - TILE : (k + 1) * lines].astype(jnp.float32)
        behind = below[packed, k * lines : k * lines + TILE].astype(jnp.float32)
        both = jnp.where(lane < TILE // 2, behind, ahead).astype(jnp.bfloat16)
        middle[height : height + EDGE, 4 * lines + k * TILE : 4 * lines + (k + 1) * TILE] = both
    copy_all(moves, sem)


def lines_kernel(lines, half_ring, place, forward, backward, crossed, down, up, sem):
    in_half = lax.rem(place[0], half_ring)
    most, least = LINE_RIM, LINE_RIM // 2
    for out, counts, raw_place in ((down, (least, most), 0), (up, (most, least), half_ring - 1)):
        starts = (0, 0) if out is down else (lines - counts[0], lines - counts[1])
        ended = lines if out is down else lines + 2 * LINE_RIM - counts[1]
        tops = pl.ds(0, counts[0]), pl.ds(counts[0], counts[1])

        @pl.when(in_half == raw_place)
        def _(out=out, counts=counts, starts=starts, tops=tops):
            copy_all(
                [
                    (slab.at[pl.ds(start, count), :], out.at[top, :])
                    for slab, start, count, top in zip((forward, backward), starts, counts, tops)
                ],
                sem,
            )

        @pl.when(in_half != raw_place)
        def _(out=out, counts=counts, starts=starts, ended=ended, tops=tops):
            copy_all(
                [
                    (crossed.at[pl.ds(starts[0], counts[0]), :], out.at[tops[0], :]),
                    (crossed.at[pl.ds(ended, counts[1]), :], out.at[tops[1], :]),
                ],
                sem,
            )


def positions(place, cols, total_cols, at, span):
    column = lax.broadcasted_iota(jnp.int32, (1, span), 1) + (place[1] * cols + at)
    position = (column.astype(jnp.float32) + 0.5) / total_cols + 0.25
    return position, position * position


def prep_kernel(
    lines, cols, total_lines, total_cols, lag_floor, place,
    nadir, left, right, above, below, lag, offsets, weights, down,
    slopes, center, texture, sums, bands, framed, slope_v, center_v, texture_v, bands_v, sem,
):
    tall = lines + 2 * NADIR_RIM
    rows = lines + 16
    framed[0:NADIR_RIM, :] = above[0:NADIR_RIM, :]
    framed[NADIR_RIM + lines : tall, :] = below[0:NADIR_RIM, :]
    framed[NADIR_RIM : NADIR_RIM + lines, 0:TILE] = left[0:lines, :]
    framed[NADIR_RIM : NADIR_RIM + lines, TILE : TILE + cols] = nadir[...]
    framed[NADIR_RIM : NADIR_RIM + lines, TILE + cols :] = right[0:lines, :]
    row = lax.broadcasted_iota(jnp.int32, (2 * WIDE, WIDE), 0)
    col = lax.broadcasted_iota(jnp.int32, (2 * WIDE, WIDE), 1)
    gap = jnp.abs(row - TILE - col)
    smear = jnp.where(gap == 0, 2.0, jnp.where(gap == 1, 1.0, 0.0)).astype(jnp.bfloat16)
    totals = [jnp.zeros((lines, TILE), jnp.float32) for _ in range(3)]
    copies = []
    for at in range(0, cols, WIDE):
        across = jnp.dot(
            framed[:, at : at + 2 * WIDE], smear, preferred_element_type=jnp.float32
        )
        change = pltpu.roll(across, tall - 5, 0) - pltpu.roll(across, tall - 3, 0)
        slope = change[8 : 8 + rows] * 0.25
        slope_v[:, at : at + WIDE] = slope
        middle = framed[:, TILE + at : TILE + at + WIDE].astype(jnp.float32)
        middle = pltpu.roll(middle, tall - 4, 0)[8 : 8 + rows]
        center_v[:, at : at + WIDE] = middle.astype(jnp.bfloat16)
        level = box_sum(slope * slope, lines) * (1.0 / (2 * BOX + 1))
        texture_v[:, at : at + WIDE] = level
        for source, target in ((slope_v, slopes), (center_v, center), (texture_v, texture)):
            window = (slice(None), pl.ds(at, WIDE))
            copy = pltpu.make_async_copy(source.at[window], target.at[window], sem.at[len(copies)])
            copy.start()
            copies.append(copy)
        position, square = positions(place, cols, total_cols, at, WIDE)
        for k, lever in enumerate((square, square * position, square * square)):
            totals[k] = totals[k] + lane_fold(level * lever)
    lane = lax.broadcasted_iota(jnp.int32, (lines, TILE), 1)
    packed = jnp.zeros((lines, TILE), jnp.float32)
    for k in range(3):
        packed = jnp.where(lane == k, jnp.sum(totals[k], axis=1, keepdims=True), packed)
    sums[...] = packed.T[0:8, :] * (1.0 / (lines * total_cols))
    begin = place[0] * lines
    ahead = pl.multiple_of(lax.rem(begin + total_lines - TILE, total_lines), TILE)
    behind = pl.multiple_of(lax.rem(begin + lines, total_lines), TILE)
    begin = pl.multiple_of(begin, TILE)

    def window(ref, lead):
        parts = [
            ref[lead + (slice(None), pl.ds(start, size))].astype(jnp.float32)
            for start, size in ((ahead, TILE), (begin, lines), (behind, TILE))
        ]
        return jnp.concatenate(parts, axis=1)

    wide = lines + 2 * TILE
    lags = window(lag, ()) - float(lag_floor)
    shifts = window(offsets, ())
    stacked = jnp.concatenate(
        [
            jnp.broadcast_to(shifts[0:1] - lags, (8, wide)),
            jnp.broadcast_to(shifts[1:2] + lags, (8, wide)),
            window(weights, (0,)),
            window(weights, (1,)),
            jnp.zeros((TILE - 24, wide), jnp.float32),
        ],
        axis=0,
    )
    as_columns = pltpu.roll(stacked.T, wide - (TILE - BOX), 0)[0:rows]
    half = lines // 2
    depth = half + 2 * LINE_RIM
    for s in range(2):
        for first, last in ((0, half), (half, rows)):
            at = lax.broadcasted_iota(jnp.int32, (last - first, depth), 1)
            own = lax.broadcasted_iota(jnp.int32, (last - first, depth), 0)
            distance = (at - own - (LINE_RIM - BOX)).astype(jnp.float32)
            distance = distance - as_columns[first:last, 8 * s : 8 * s + 1]
            band = jnp.zeros((last - first, depth), jnp.float32)
            for tap in range(TAPS):
                weight = as_columns[first:last, 16 + 4 * s + tap : 17 + 4 * s + tap]
                band = jnp.where(distance == float(tap), weight, band)
            bands_v[s, first:last, :] = band.astype(jnp.bfloat16)
    copy = pltpu.make_async_copy(bands_v, bands, sem.at[len(copies)])
    copy.start()
    for waited in (*copies, copy):
        waited.wait()


def slab_kernel(
    lines, cols, jobs, fresh,
    slopes, center, texture, bands, params, basis, earlier, above, below, crossed, *rest,
):
    middle = None
    if not fresh:
        middle, rest = rest[0], rest[2:]
    parallax, pulled, bands_v, params_v, basis_v, earlier_v, sem, *scratch = rest
    rows = lines + 16
    half = lines // 2
    depth = half + 2 * LINE_RIM
    height = lines - 2 * LINE_RIM
    most, least = LINE_RIM, LINE_RIM // 2
    copies = []

    def fetch(source, target):
        copy = pltpu.make_async_copy(source, target, sem.at[len(copies)])
        copy.start()
        copies.append(copy)

    fetch(bands, bands_v)
    fetch(params, params_v)
    loads = []
    for n, (s, first, width) in enumerate(jobs):
        ext, along, slope_v, center_v, texture_v, packed, result = scratch[7 * n : 7 * n + 7]
        low, high = first - TILE, first + width + TILE
        over, under = ((most, least), (least, most))[s]
        begin, end = max(low, 0), min(high, cols)
        columns, inside = pl.ds(begin, end - begin), pl.ds(begin - low, end - begin)
        pieces = [
            (above, (0, most)[s], LINE_RIM - over, over),
            (below, (0, least)[s], LINE_RIM + lines, under),
        ]
        if s == 0:
            pieces.append((crossed, 0, LINE_RIM, lines))
        else:
            pieces.append((crossed, lines, LINE_RIM, LINE_RIM))
            pieces.append((crossed, lines + LINE_RIM, lines, LINE_RIM))
            pieces.append((middle, 0, 2 * LINE_RIM, height))
        for ref, row, target, count in pieces:
            fetch(ref.at[pl.ds(row, count), columns], ext.at[pl.ds(target, count), inside])
        for side in range(2):
            if (low < 0, high > cols)[side]:
                kind = 2 * side + s
                row = pl.ds(height, EDGE)
                fetch(middle.at[row, pl.ds(kind * lines, lines)], packed.at[side, :, pl.ds(0, lines)])
                fetch(
                    middle.at[row, pl.ds(4 * lines + kind * TILE, TILE)],
                    packed.at[side, :, pl.ds(lines, TILE)],
                )
        loaded = len(copies)
        columns = pl.ds(first, width)
        fetch(slopes.at[:, columns], slope_v)
        fetch(center.at[:, columns], center_v)
        fetch(texture.at[:, columns], texture_v)
        loads.append((loaded, len(copies)))
    fetch(basis, basis_v)
    fetch(earlier, earlier_v)
    waited, writes = 0, []
    pulls = [jnp.zeros((lines, TILE), jnp.float32) for _ in range(2)]
    for n, (s, first, width) in enumerate(jobs):
        ext, along, slope_v, center_v, texture_v, packed, result = scratch[7 * n : 7 * n + 7]
        low, high = first - TILE, first + width + TILE
        over, under = ((most, least), (least, most))[s]
        blank = jnp.zeros((least, width + 2 * TILE), jnp.bfloat16)
        if s == 0:
            ext[2 * LINE_RIM + lines - least :, :] = blank
        else:
            ext[:least, :] = blank
        for copy in copies[waited : loads[n][0]]:
            copy.wait()
        for side in range(2):
            if (low < 0, high > cols)[side]:
                at = 0 if side == 0 else width + TILE
                piece = packed[side].astype(jnp.float32)
                gap = jnp.zeros((TILE - EDGE, lines + TILE), jnp.float32)
                piece = jnp.concatenate([gap, piece] if side == 0 else [piece, gap], axis=0)
                turned = piece.T.astype(jnp.bfloat16)
                ext[LINE_RIM : LINE_RIM + lines, at : at + TILE] = turned[:lines]
                ext[LINE_RIM - over : LINE_RIM, at : at + TILE] = turned[lines + TILE - over :]
                ext[LINE_RIM + lines : LINE_RIM + lines + under, at : at + TILE] = turned[
                    lines : lines + under
                ]
        for at in range(0, width + 2 * TILE, WIDE):
            end = min(at + WIDE, width + 2 * TILE)
            for start, stop in ((0, half), (half, rows)):
                along[start:stop, at:end] = jnp.dot(
                    bands_v[s, start:stop, :],
                    ext[start : start + depth, at:end],
                    preferred_element_type=jnp.float32,
                ).astype(jnp.bfloat16)
        for copy in copies[loads[n][0] : loads[n][1]]:
            copy.wait()
        waited = loads[n][1]
        for at in range(0, width, WIDE):
            span = min(WIDE, width - at)
            place_of = slice(first + at, first + at + span)
            row = lax.broadcasted_iota(jnp.int32, (span + 2 * EDGE, span), 0)
            col = lax.broadcasted_iota(jnp.int32, (span + 2 * EDGE, span), 1)
            distance = (row - col - EDGE).astype(jnp.float32) - params_v[8 * s : 8 * s + 1, place_of]
            band = jnp.zeros((span + 2 * EDGE, span), jnp.float32)
            for tap in range(TAPS):
                weight = params_v[8 * s + 1 + tap : 8 * s + 2 + tap, place_of]
                band = jnp.where(distance == float(tap), weight, band)
            blank = jnp.zeros((TILE - EDGE, span), jnp.bfloat16)
            resampled = jnp.dot(
                along[:, at : at + span + 2 * TILE],
                jnp.concatenate([blank, band.astype(jnp.bfloat16), blank], axis=0),
                preferred_element_type=jnp.float32,
            ).astype(jnp.bfloat16)
            for part in range(0, span, TILE):
                here = slice(at + part, at + part + TILE)
                there = slice(first + at + part, first + at + part + TILE)
                mismatch = resampled[:, part : part + TILE].astype(jnp.float32)
                mismatch = mismatch - center_v[:, here].astype(jnp.float32)
                level = texture_v[:, here]
                inverse = (-1.0 / (2 * BOX + 1)) / jnp.maximum(level, 0.4)
                estimate = box_sum(slope_v[:, here] * mismatch, lines) * inverse
                result[:, here] = estimate.astype(jnp.bfloat16)
                weighted = level * estimate
                for k in range(2):
                    pulls[k] = pulls[k] + weighted * params_v[16 + k : 17 + k, there]
        write = pltpu.make_async_copy(
            result, parallax.at[s, :, pl.ds(first, width)], sem.at[len(copies) + n]
        )
        write.start()
        writes.append(write)
    for copy in copies[waited:]:
        copy.wait()
    pulled[...] = earlier_v[...]
    for k in range(2):
        per_line = jnp.sum(pulls[k], axis=1, keepdims=True)
        pulled[k : k + 1, :] += jnp.sum(basis_v[...] * per_line, axis=0, keepdims=True)
    for write in writes:
        write.wait()


def local(
    nadir_view, forward, backward, along_weights, cross_weights, band_offsets, col_offsets,
    lag_lines, window_start,
):
    lines, cols = nadir_view.shape
    along_count = lax.axis_size("along")
    cross_count = lax.axis_size("cross")
    along_index = lax.axis_index("along")
    cross_index = lax.axis_index("cross")
    total_lines = lines * along_count
    total_cols = cols * cross_count
    half_ring = along_count // 2
    lag_floor = CAMERA_LAG // total_lines * total_lines + half_ring * lines
    rows = lines + 16
    whole = cols + 2 * TILE
    low_z, high_z = pairs_of(cross_count, -1), pairs_of(cross_count, 1)
    ring_down = [(i, (i - 1) % along_count) for i in range(along_count)]
    ring_up = [(i, (i + 1) % along_count) for i in range(along_count)]
    half_down, half_up = [], []
    for i in range(along_count):
        base = i // half_ring * half_ring
        half_down.append((i, base + (i - base - 1) % half_ring))
        half_up.append((i, base + (i - base + 1) % half_ring))
    across = [(i, (i + half_ring) % along_count) for i in range(along_count)]

    def over(value):
        return lax.ppermute(value, "along", across)

    def hbm(value):
        return pltpu.with_memory_space_constraint(value, pltpu.HBM)

    f32, bf16 = jnp.float32, jnp.bfloat16
    any_space = pl.BlockSpec(memory_space=pl.ANY)
    vmem = pl.BlockSpec(memory_space=pltpu.VMEM)
    smem = pl.BlockSpec(memory_space=pltpu.SMEM)
    limit = pltpu.CompilerParams(vmem_limit_bytes=24 * 1024 * 1024)

    def mover(kernel, name, shapes, operands, copies, scalars=0, scratch=()):
        return pl.pallas_call(
            kernel,
            out_shape=tuple(jax.ShapeDtypeStruct(shape, bf16) for shape in shapes),
            in_specs=[smem] * scalars + [any_space] * (len(operands) - scalars),
            out_specs=(vmem,) * len(shapes),
            scratch_shapes=[*scratch, pltpu.SemaphoreType.DMA((copies,))],
            compiler_params=limit,
            cost_estimate=pl.CostEstimate(
                flops=0, bytes_accessed=4 * sum(math.prod(s) for s in shapes), transcendentals=0
            ),
            name=name,
        )(*operands)

    place = jnp.stack([along_index, cross_index]).astype(jnp.int32)
    gap = jnp.zeros((3, cols), f32)
    shift = col_offsets.astype(f32)
    taps = cross_weights.astype(f32)
    columns = cross_index * cols + jnp.arange(cols, dtype=jnp.int32)
    position = ((columns.astype(f32) + 0.5) / total_cols + 0.25)[None]
    params = jnp.concatenate(
        [shift[0:1], taps[0], gap, shift[1:2], taps[1], gap, position, position * position, gap, gap]
    )
    basis = harmonics(window_start[0] + along_index * lines + jnp.arange(lines, dtype=jnp.int32))

    (crossing,) = mover(
        functools.partial(cross_kernel, lines),
        "cross",
        ((lines + 2 * LINE_RIM, cols),),
        (hbm(forward), hbm(backward)),
        3,
    )
    crossed = over(crossing)

    near = lines + 2 * EDGE * lines // TILE
    near_first, near_last = mover(
        functools.partial(pack_kernel, lines, cols),
        "pack",
        ((near, TILE), (near, TILE)),
        (hbm(nadir_view), hbm(forward), hbm(backward), crossing),
        6,
        scratch=[pltpu.VMEM((2, 2, lines, TILE), bf16)],
    )
    from_right = lax.ppermute(near_first, "cross", low_z)
    from_left = lax.ppermute(near_last, "cross", high_z)
    first_lines, last_lines = mover(
        functools.partial(nadir_lines_kernel, lines, cols),
        "nadir_lines",
        ((NADIR_RIM + EDGE, whole), (NADIR_RIM + EDGE, whole)),
        (hbm(nadir_view), from_left, from_right, params, basis),
        6 + 8 * lines // TILE,
    )
    nadir_below = lax.ppermute(first_lines, "along", ring_down)
    nadir_above = lax.ppermute(last_lines, "along", ring_up)

    (middle,) = pl.pallas_call(
        functools.partial(middle_kernel, lines, cols),
        out_shape=(jax.ShapeDtypeStruct((lines - 2 * LINE_RIM + EDGE, cols), bf16),),
        in_specs=[any_space, any_space, vmem, vmem],
        out_specs=(vmem,),
        scratch_shapes=[pltpu.SemaphoreType.DMA((2,))],
        compiler_params=limit,
        cost_estimate=pl.CostEstimate(
            flops=0, bytes_accessed=4 * lines * cols, transcendentals=0
        ),
        name="middle",
    )(hbm(backward), first_lines, nadir_above, nadir_below)
    middle = over(middle)

    down, up = mover(
        functools.partial(lines_kernel, lines, half_ring),
        "lines",
        ((3 * LINE_RIM // 2, cols), (3 * LINE_RIM // 2, cols)),
        (place, hbm(forward), hbm(backward), crossed),
        2,
        1,
    )
    slab_below = lax.ppermute(down, "along", half_down)
    slab_above = lax.ppermute(up, "along", half_up)

    depth = lines // 2 + 2 * LINE_RIM
    slopes, center, texture, sums, bands = pl.pallas_call(
        functools.partial(prep_kernel, lines, cols, total_lines, total_cols, lag_floor),
        out_shape=(
            pltpu.HBM((rows, cols), f32),
            pltpu.HBM((rows, cols), bf16),
            pltpu.HBM((lines, cols), f32),
            jax.ShapeDtypeStruct((8, lines), f32),
            pltpu.HBM((2, rows, depth), bf16),
        ),
        in_specs=[smem] + [vmem] * 8 + [any_space],
        out_specs=(any_space, any_space, any_space, vmem, any_space),
        scratch_shapes=[
            pltpu.VMEM((lines + 2 * NADIR_RIM, whole), bf16),
            pltpu.VMEM((rows, cols), f32),
            pltpu.VMEM((rows, cols), bf16),
            pltpu.VMEM((lines, cols), f32),
            pltpu.VMEM((2, rows, depth), bf16),
            pltpu.SemaphoreType.DMA((3 * (cols // WIDE) + 1,)),
        ],
        compiler_params=limit,
        cost_estimate=pl.CostEstimate(
            flops=2 * rows * cols * 512, bytes_accessed=12 * rows * cols, transcendentals=0
        ),
        name="prep",
    )(
        place, hbm(nadir_view), from_left, from_right, nadir_above,
        nadir_below, lag_lines[None], hbm(band_offsets), hbm(along_weights), down,
    )

    def run(jobs, earlier, middle, parallax):
        fresh = parallax is None
        operands = [
            slopes, center, texture, bands, params, basis, earlier, slab_above, slab_below, crossed,
        ]
        aliases = {}
        if not fresh:
            operands += [middle, parallax]
            aliases = {len(operands) - 1: 0}
        scratch = []
        for _, _, width in jobs:
            scratch += [
                pltpu.VMEM((lines + 2 * LINE_RIM, width + 2 * TILE), bf16),
                pltpu.VMEM((rows, width + 2 * TILE), bf16),
                pltpu.VMEM((rows, width), f32),
                pltpu.VMEM((rows, width), bf16),
                pltpu.VMEM((lines, width), f32),
                pltpu.VMEM((2, EDGE, lines + TILE), bf16),
                pltpu.VMEM((lines, width), bf16),
            ]
        done = sum(width for _, _, width in jobs)
        return pl.pallas_call(
            functools.partial(slab_kernel, lines, cols, jobs, fresh),
            out_shape=(
                pltpu.HBM((2, lines, cols), bf16),
                jax.ShapeDtypeStruct((8, TILE), f32),
            ),
            in_specs=[any_space] * len(operands),
            out_specs=(any_space, vmem),
            scratch_shapes=[
                pltpu.VMEM((2, rows, depth), bf16),
                pltpu.VMEM((24, cols), f32),
                pltpu.VMEM((lines, TILE), f32),
                pltpu.VMEM((8, TILE), f32),
                pltpu.SemaphoreType.DMA((4 + 14 * len(jobs),)),
                *scratch,
            ],
            input_output_aliases=aliases,
            compiler_params=limit,
            cost_estimate=pl.CostEstimate(
                flops=2 * rows * (done + 256) * 900, bytes_accessed=20 * rows * done, transcendentals=0
            ),
            name="inner" if fresh else "rest",
        )(*(hbm(v) if n < 4 else v for n, v in enumerate(operands)))

    nothing = jnp.zeros((8, TILE), f32)
    parallax, pulled = run([(0, TILE, cols - 2 * TILE)], nothing, None, None)
    jobs = [(0, 0, TILE), (0, cols - TILE, TILE), (1, 0, cols)]
    parallax, pulled = run(jobs, pulled, middle, parallax)

    share = jnp.concatenate([sums, pulled], axis=1)
    total = share
    for shift_by in range(1, cross_count):
        total = total + lax.ppermute(
            share, "cross", [(i, (i + shift_by) % cross_count) for i in range(cross_count)]
        )
    scale_pull = 1.0 / (lines * total_cols) ** 0.5
    line_sums = total[:, :lines]
    row_count = 4 * MODES // cross_count
    row_first = cross_index * row_count
    assert 2 * MODES % row_count == 0
    upper = row_first >= 2 * MODES
    doubled = jnp.concatenate([basis, basis], axis=1)
    basis_rows = lax.dynamic_slice_in_dim(doubled, row_first, row_count, 1)
    left_coef = jnp.where(upper, line_sums[1], line_sums[0])
    right_coef = jnp.where(upper, line_sums[2], line_sums[1])
    weighted = jnp.concatenate([basis * left_coef[:, None], basis * right_coef[:, None]], axis=1)
    normal_gram = jnp.dot(basis_rows.T, weighted, precision=lax.Precision.HIGHEST)[None]
    flat = total[:2, lines:].reshape(1, 4 * MODES) * scale_pull
    normal_rhs = lax.dynamic_slice_in_dim(flat, row_first, row_count, 1)
    return parallax, normal_gram, normal_rhs


def solution(mesh):
    placed = (
        P("along", "cross"),
        P("along", "cross"),
        P("along", "cross"),
        P(),
        P(None, None, "cross"),
        P(),
        P(None, "cross"),
        P(),
        P(),
    )
    return jax.shard_map(
        local,
        mesh=mesh,
        in_specs=placed,
        out_specs=(P(None, "along", "cross"), P("along", "cross", None), P("along", "cross")),
        check_vma=False,
    )
```

```python
import functools
import math

import jax
import jax.numpy as jnp
from jax import lax
from jax.experimental import pallas as pl
from jax.experimental.pallas import tpu as pltpu
from jax.sharding import PartitionSpec as P

TAPS = 4
CAMERA_LAG = 20480
BOX = 4
MODES = 64
LINE_RIM = 32
NADIR_RIM = 16
TILE = 128
WIDE = 256
EDGE = 16


def pairs_of(count, step):
    return [(i, i + step) for i in range(count) if 0 <= i + step < count]


def box_sum(x, lines):
    rows = x.shape[0]
    two = x + pltpu.roll(x, rows - 1, 0)
    four = two + pltpu.roll(two, rows - 2, 0)
    eight = four + pltpu.roll(four, rows - 4, 0)
    return eight[:lines] + x[2 * BOX : lines + 2 * BOX]


def lane_fold(x):
    folded = x[:, :TILE]
    for at in range(TILE, x.shape[1], TILE):
        folded = folded + x[:, at : at + TILE]
    return folded


def copy_all(moves, sem):
    copies = [pltpu.make_async_copy(a, b, sem.at[n]) for n, (a, b) in enumerate(moves)]
    for copy in copies:
        copy.start()
    for copy in copies:
        copy.wait()


def cut_kernel(
    lines, cols, cut, nadir, forward, backward, ends, first_part, near_first, near_last, side, sem
):
    body = pl.ds(LINE_RIM, lines - 2 * LINE_RIM)
    moves = [(backward.at[body, pl.ds(0, cut)], first_part)]
    for n, (begin, near) in enumerate(((0, near_first), (cols - TILE, near_last))):
        moves.append((nadir.at[:, pl.ds(begin, TILE)], near.at[pl.ds(0, lines), :]))
        for s, slab in enumerate((forward, backward)):
            moves.append((slab.at[:, pl.ds(begin, TILE)], side.at[s, n]))
    copy_all(moves, sem)
    for n, (row, near) in enumerate(((0, near_first), (TILE - EDGE, near_last))):
        for s in range(2):
            turned = side[s, n].astype(jnp.float32).T[row : row + EDGE].astype(jnp.bfloat16)
            for k in range(lines // TILE):
                at = lines + (s * (lines // TILE) + k) * EDGE
                near[at : at + EDGE, :] = turned[:, k * TILE : (k + 1) * TILE]


def ends_kernel(lines, backward, ends, sem):
    moves = []
    for n, row in enumerate((0, lines - LINE_RIM)):
        target = pl.ds(n * LINE_RIM, LINE_RIM)
        moves.append((backward.at[pl.ds(row, LINE_RIM), :], ends.at[target, :]))
    copy_all(moves, sem)


def nadir_lines_kernel(lines, cols, nadir, from_left, from_right, bands, first, last, sem):
    moves = []
    whole = cols + 2 * TILE
    for out, row, tile in ((first, 0, 0), (last, lines - NADIR_RIM, lines // TILE - 1)):
        span = pl.ds(row, NADIR_RIM)
        moves.append((from_left.at[span, :], out.at[:, pl.ds(0, TILE)]))
        moves.append((nadir.at[span, :], out.at[:, pl.ds(TILE, cols)]))
        moves.append((from_right.at[span, :], out.at[:, pl.ds(TILE + cols, TILE)]))
        for n, near in enumerate((from_left, from_right)):
            for s in range(2):
                at = lines + (s * (lines // TILE) + tile) * EDGE
                target = pl.ds(whole + (2 * n + s) * TILE, TILE)
                moves.append((near.at[pl.ds(at, EDGE), :], out.at[:, target]))
    copy_all(moves, sem)


def late_kernel(
    lines, cols, cuts, backward, from_left, from_right, above, below, second, third, sem
):
    height = lines - 2 * LINE_RIM
    whole = cols + 2 * TILE
    body = pl.ds(LINE_RIM, height)
    width = cuts[1] - cuts[0]
    moves = [
        (backward.at[body, pl.ds(cuts[0], width)], second.at[pl.ds(0, height), :]),
        (backward.at[body, pl.ds(cuts[1], cols - cuts[1])], third),
    ]
    lane = lax.broadcasted_iota(jnp.int32, (EDGE, TILE), 1)
    for k in range(4):
        row = height + k * EDGE
        near = (from_left, from_right)[k // 2]
        for tile in range(lines // TILE):
            at = lines + (k % 2 * (lines // TILE) + tile) * EDGE
            window = second.at[pl.ds(row, EDGE), pl.ds(tile * TILE, TILE)]
            moves.append((near.at[pl.ds(at, EDGE), :], window))
        here = slice(whole + k * TILE, whole + (k + 1) * TILE)
        ahead = above[:, here].astype(jnp.float32)
        behind = below[:, here].astype(jnp.float32)
        both = jnp.where(lane < TILE // 2, behind, ahead).astype(jnp.bfloat16)
        second[row : row + EDGE, lines : lines + TILE] = both
    if width > lines + TILE:
        second[height:, lines + TILE :] = jnp.zeros((4 * EDGE, width - lines - TILE), jnp.bfloat16)
    copy_all(moves, sem)


def lines_kernel(lines, half_ring, place, forward, backward, lead, ends, down, up, sem):
    in_half = lax.rem(place[0], half_ring)
    most, least = LINE_RIM, LINE_RIM // 2
    for out, counts, raw_place in ((down, (least, most), 0), (up, (most, least), half_ring - 1)):
        starts = (0, 0) if out is down else (lines - counts[0], lines - counts[1])
        ended = 0 if out is down else 2 * LINE_RIM - counts[1]
        tops = pl.ds(0, counts[0]), pl.ds(counts[0], counts[1])

        @pl.when(in_half == raw_place)
        def _(out=out, counts=counts, starts=starts, tops=tops):
            copy_all(
                [
                    (slab.at[pl.ds(start, count), :], out.at[top, :])
                    for slab, start, count, top in zip((forward, backward), starts, counts, tops)
                ],
                sem,
            )

        @pl.when(in_half != raw_place)
        def _(out=out, counts=counts, starts=starts, ended=ended, tops=tops):
            copy_all(
                [
                    (lead.at[pl.ds(starts[0], counts[0]), :], out.at[tops[0], :]),
                    (ends.at[pl.ds(ended, counts[1]), :], out.at[tops[1], :]),
                ],
                sem,
            )


def positions(place, cols, total_cols, at, span):
    column = lax.broadcasted_iota(jnp.int32, (1, span), 1) + (place[1] * cols + at)
    position = (column.astype(jnp.float32) + 0.5) / total_cols + 0.25
    return position, position * position


def prep_kernel(
    lines, cols, total_cols, place, nadir, left, right, above, below, down,
    slopes, center, inverse, lever, sums, framed,
):
    tall = lines + 2 * NADIR_RIM
    rows = lines + 16
    framed[0:NADIR_RIM, :] = above[:, 0 : cols + 2 * TILE]
    framed[NADIR_RIM + lines : tall, :] = below[:, 0 : cols + 2 * TILE]
    framed[NADIR_RIM : NADIR_RIM + lines, 0:TILE] = left[0:lines, :]
    framed[NADIR_RIM : NADIR_RIM + lines, TILE : TILE + cols] = nadir[...]
    framed[NADIR_RIM : NADIR_RIM + lines, TILE + cols :] = right[0:lines, :]
    row = lax.broadcasted_iota(jnp.int32, (2 * WIDE, WIDE), 0)
    col = lax.broadcasted_iota(jnp.int32, (2 * WIDE, WIDE), 1)
    gap = jnp.abs(row - TILE - col)
    smear = jnp.where(gap == 0, 2.0, jnp.where(gap == 1, 1.0, 0.0)).astype(jnp.bfloat16)
    totals = [jnp.zeros((lines, TILE), jnp.float32) for _ in range(3)]
    for at in range(0, cols, WIDE):
        across = jnp.dot(
            framed[:, at : at + 2 * WIDE], smear, preferred_element_type=jnp.float32
        )
        change = pltpu.roll(across, tall - 5, 0) - pltpu.roll(across, tall - 3, 0)
        slope = change[8 : 8 + rows] * 0.25
        slopes[:, at : at + WIDE] = slope
        middle = framed[:, TILE + at : TILE + at + WIDE].astype(jnp.float32)
        middle = pltpu.roll(middle, tall - 4, 0)[8 : 8 + rows]
        center[:, at : at + WIDE] = middle.astype(jnp.bfloat16)
        level = box_sum(slope * slope, lines) * (1.0 / (2 * BOX + 1))
        inverted = (-1.0 / (2 * BOX + 1)) / jnp.maximum(level, 0.4)
        inverse[:, at : at + WIDE] = inverted
        lever[:, at : at + WIDE] = level * inverted
        position, square = positions(place, cols, total_cols, at, WIDE)
        for k, power in enumerate((square, square * position, square * square)):
            totals[k] = totals[k] + lane_fold(level * power)
    lane = lax.broadcasted_iota(jnp.int32, (lines, TILE), 1)
    packed = jnp.zeros((lines, TILE), jnp.float32)
    for k in range(3):
        packed = jnp.where(lane == k, jnp.sum(totals[k], axis=1, keepdims=True), packed)
    sums[...] = packed.T[0:8, :] * (1.0 / (lines * total_cols))


def cosines(phases, sines):
    period = 4 * MODES
    turned = jnp.where(sines, phases + (period - MODES), phases) % period
    return jnp.cos(turned.astype(jnp.float32) * (2.0 * jnp.pi / period))


def bands_kernel(
    lines, cols, total_lines, total_cols, lag_floor, place, lag, offsets, weights, shifts, taps,
    line_bands, col_bands, levers, basis, rows_basis, upper, chosen,
):
    rows = lines + 16
    period = 4 * MODES
    for s in range(2):
        for n in range(cols // WIDE):
            here = slice(n * WIDE, (n + 1) * WIDE)
            row = lax.broadcasted_iota(jnp.int32, (WIDE + 2 * EDGE, WIDE), 0)
            col = lax.broadcasted_iota(jnp.int32, (WIDE + 2 * EDGE, WIDE), 1)
            distance = row - col - EDGE - shifts[s : s + 1, here]
            weight = taps[s, :, here].astype(jnp.float32)
            band = jnp.zeros((WIDE + 2 * EDGE, WIDE), jnp.float32)
            for tap in range(TAPS):
                band = jnp.where(distance == tap, weight[tap : tap + 1], band)
            col_bands[s, :, here] = band.astype(jnp.bfloat16)
    position, square = positions(place, cols, total_cols, 0, cols)
    levers[0:1, :] = position
    levers[1:2, :] = square
    levers[2:, :] = jnp.zeros((6, cols), jnp.float32)
    start = place[2] + place[0] * lines
    line = start + lax.broadcasted_iota(jnp.int32, (lines, 2 * MODES), 0)
    mode = lax.broadcasted_iota(jnp.int32, (lines, 2 * MODES), 1)
    basis[...] = cosines(line % period * (2 * (mode % MODES) + 1), mode >= MODES)
    count = rows_basis.shape[0]
    row_first = place[1] * count
    row_at = lax.rem(row_first, 2 * MODES)
    mode = row_at + lax.broadcasted_iota(jnp.int32, (count, lines), 0)
    line = start + lax.broadcasted_iota(jnp.int32, (count, lines), 1)
    rows_basis[...] = cosines(line % period * (2 * (mode % MODES) + 1), mode >= MODES)
    upper[...] = jnp.zeros_like(upper) + jnp.where(row_first >= 2 * MODES, 1.0, 0.0)
    own = row_at + lax.broadcasted_iota(jnp.int32, (2 * MODES, count), 1)
    mode = lax.broadcasted_iota(jnp.int32, (2 * MODES, count), 0)
    chosen[...] = jnp.where(own == mode, 1.0, 0.0)
    begin = place[0] * lines
    ahead = pl.multiple_of(lax.rem(begin + total_lines - TILE, total_lines), TILE)
    behind = pl.multiple_of(lax.rem(begin + lines, total_lines), TILE)
    begin = pl.multiple_of(begin, TILE)

    def window(ref, lead):
        parts = [
            ref[lead + (slice(None), pl.ds(start, size))].astype(jnp.float32)
            for start, size in ((ahead, TILE), (begin, lines), (behind, TILE))
        ]
        return jnp.concatenate(parts, axis=1)

    wide = lines + 2 * TILE
    lags = window(lag, ()) - float(lag_floor)
    shifts = window(offsets, ())
    stacked = jnp.concatenate(
        [
            jnp.broadcast_to(shifts[0:1] - lags, (8, wide)),
            jnp.broadcast_to(shifts[1:2] + lags, (8, wide)),
            window(weights, (0,)),
            window(weights, (1,)),
            jnp.zeros((TILE - 24, wide), jnp.float32),
        ],
        axis=0,
    )
    as_columns = pltpu.roll(stacked.T, wide - (TILE - BOX), 0)[0:rows]
    half = lines // 2
    depth = half + 2 * LINE_RIM
    for s in range(2):
        for first, last in ((0, half), (half, rows)):
            at = lax.broadcasted_iota(jnp.int32, (last - first, depth), 1)
            own = lax.broadcasted_iota(jnp.int32, (last - first, depth), 0)
            distance = (at - own - (LINE_RIM - BOX)).astype(jnp.float32)
            distance = distance - as_columns[first:last, 8 * s : 8 * s + 1]
            band = jnp.zeros((last - first, depth), jnp.float32)
            for tap in range(TAPS):
                weight = as_columns[first:last, 16 + 4 * s + tap : 17 + 4 * s + tap]
                band = jnp.where(distance == float(tap), weight, band)
            line_bands[s, first:last, :] = band.astype(jnp.bfloat16)


def slab_kernel(
    lines, cols, cuts, jobs, count, fresh, last,
    slopes, center, inverse, lever, line_bands, col_bands, levers, basis, above, below, ends, *rest,
):
    lead, first_part, second_part, third_part = (*rest[:count], None, None, None)[:4]
    rest = rest[count:]
    if not fresh:
        earlier, rest = rest[0], rest[2:]
    parallax, pulled, sem, *scratch = rest
    rows = lines + 16
    half = lines // 2
    depth = half + 2 * LINE_RIM
    height = lines - 2 * LINE_RIM
    most, least = LINE_RIM, LINE_RIM // 2
    writes = []
    if fresh:
        pulls = [jnp.zeros((lines, TILE), jnp.float32) for _ in range(2)]
    else:
        pulls = [earlier[k] for k in range(2)]
    for n, (s, first, width) in enumerate(jobs):
        ext, along, result = scratch[3 * n : 3 * n + 3]
        low, high = first - TILE, first + width + TILE
        over, under = ((most, least), (least, most))[s]
        pieces = [
            (above, (0, most)[s], LINE_RIM - over, over, 0, cols),
            (below, (0, least)[s], LINE_RIM + lines, under, 0, cols),
        ]
        if s == 0:
            pieces.append((lead, 0, LINE_RIM, lines, 0, cols))
        else:
            pieces.append((ends, 0, LINE_RIM, LINE_RIM, 0, cols))
            pieces.append((ends, LINE_RIM, lines, LINE_RIM, 0, cols))
            pieces.append((first_part, 0, 2 * LINE_RIM, height, 0, cuts[0]))
            pieces.append((second_part, 0, 2 * LINE_RIM, height, cuts[0], cuts[1]))
            pieces.append((third_part, 0, 2 * LINE_RIM, height, cuts[1], cols))
        for ref, row, target, tall, begin, end in pieces:
            a, b = max(low, begin), min(high, end)
            if a < b:
                ext[target : target + tall, a - low : b - low] = ref[
                    row : row + tall, a - begin : b - begin
                ]
        blank = jnp.zeros((least, width + 2 * TILE), jnp.bfloat16)
        if s == 0:
            ext[2 * LINE_RIM + lines - least :, :] = blank
        else:
            ext[:least, :] = blank
        for side in range(2):
            if (low < 0, high > cols)[side]:
                at = 0 if side == 0 else width + TILE
                row = height + (2 * side + s) * EDGE
                piece = second_part[row : row + EDGE, : lines + TILE].astype(jnp.float32)
                gap = jnp.zeros((TILE - EDGE, lines + TILE), jnp.float32)
                piece = jnp.concatenate([gap, piece] if side == 0 else [piece, gap], axis=0)
                turned = piece.T.astype(jnp.bfloat16)
                ext[LINE_RIM : LINE_RIM + lines, at : at + TILE] = turned[:lines]
                ext[LINE_RIM - over : LINE_RIM, at : at + TILE] = turned[lines + TILE - over :]
                ext[LINE_RIM + lines : LINE_RIM + lines + under, at : at + TILE] = turned[
                    lines : lines + under
                ]
        for at in range(0, width + 2 * TILE, WIDE):
            end = min(at + WIDE, width + 2 * TILE)
            for start, stop in ((0, half), (half, rows)):
                along[start:stop, at:end] = jnp.dot(
                    line_bands[s, start:stop, :],
                    ext[start : start + depth, at:end],
                    preferred_element_type=jnp.float32,
                ).astype(jnp.bfloat16)
        bounds = sorted({first, first + width, *range(-(-first // WIDE) * WIDE, first + width, WIDE)})
        for at, end in zip(bounds[:-1], bounds[1:]):
            at, span = at - first, end - at
            blank = jnp.zeros((TILE - EDGE, span), jnp.bfloat16)
            offset = first + at
            inner = offset % WIDE
            band = col_bands[s, inner : inner + span + 2 * EDGE, offset : offset + span]
            resampled = jnp.dot(
                along[:, at : at + span + 2 * TILE],
                jnp.concatenate([blank, band, blank], axis=0),
                preferred_element_type=jnp.float32,
            ).astype(jnp.bfloat16)
            for part in range(0, span, TILE):
                here = slice(at + part, at + part + TILE)
                there = slice(first + at + part, first + at + part + TILE)
                mismatch = resampled[:, part : part + TILE].astype(jnp.float32)
                mismatch = mismatch - center[:, there].astype(jnp.float32)
                boxed = box_sum(slopes[:, there] * mismatch, lines)
                result[:, here] = (boxed * inverse[:, there]).astype(jnp.bfloat16)
                weighted = boxed * lever[:, there]
                for k in range(2):
                    pulls[k] = pulls[k] + weighted * levers[k : k + 1, there]
        write = pltpu.make_async_copy(
            result, parallax.at[s, :, pl.ds(first, width)], sem.at[n]
        )
        write.start()
        writes.append(write)
    if last:
        pulled[...] = jnp.zeros_like(pulled)
        for k in range(2):
            per_line = jnp.sum(pulls[k], axis=1, keepdims=True)
            pulled[k : k + 1, :] = jnp.sum(basis[...] * per_line, axis=0, keepdims=True)
    else:
        for k in range(2):
            pulled[k] = pulls[k]
    for write in writes:
        write.wait()


def final_kernel(lines, scale_pull, basis, rows_basis, upper, chosen, *rest):
    shares, (gram, rhs) = rest[:-2], rest[-2:]
    total = shares[0][...]
    for share in shares[1:]:
        total = total + share[...]
    is_upper = upper[0:1, :] > 0.5
    sums = total[:, :lines]
    precision = lax.Precision.HIGHEST
    for n in range(2):
        coef = jnp.where(is_upper, sums[n + 1 : n + 2], sums[n : n + 1])
        gram[0, :, n * TILE : (n + 1) * TILE] = jnp.dot(
            rows_basis[...] * coef, basis[...], precision=precision, preferred_element_type=jnp.float32
        )
    pull = jnp.where(is_upper[:, :TILE], total[1:2, lines:], total[0:1, lines:]) * scale_pull
    rhs[...] = jnp.dot(
        jnp.broadcast_to(pull, (8, TILE)), chosen[...], precision=precision, preferred_element_type=jnp.float32
    )[0:1]


def local(
    nadir_view, forward, backward, along_weights, cross_weights, band_offsets, col_offsets,
    lag_lines, window_start,
):
    lines, cols = nadir_view.shape
    along_count = lax.axis_size("along")
    cross_count = lax.axis_size("cross")
    along_index = lax.axis_index("along")
    cross_index = lax.axis_index("cross")
    total_lines = lines * along_count
    total_cols = cols * cross_count
    half_ring = along_count // 2
    lag_floor = CAMERA_LAG // total_lines * total_lines + half_ring * lines
    rows = lines + 16
    whole = cols + 2 * TILE
    low_z, high_z = pairs_of(cross_count, -1), pairs_of(cross_count, 1)
    ring_down = [(i, (i - 1) % along_count) for i in range(along_count)]
    ring_up = [(i, (i + 1) % along_count) for i in range(along_count)]
    half_down, half_up = [], []
    for i in range(along_count):
        base = i // half_ring * half_ring
        half_down.append((i, base + (i - base - 1) % half_ring))
        half_up.append((i, base + (i - base + 1) % half_ring))
    across = [(i, (i + half_ring) % along_count) for i in range(along_count)]

    def over(value):
        return lax.ppermute(value, "along", across)

    def hbm(value):
        return pltpu.with_memory_space_constraint(value, pltpu.HBM)

    f32, bf16 = jnp.float32, jnp.bfloat16
    any_space = pl.BlockSpec(memory_space=pl.ANY)
    vmem = pl.BlockSpec(memory_space=pltpu.VMEM)
    smem = pl.BlockSpec(memory_space=pltpu.SMEM)
    limit = pltpu.CompilerParams(vmem_limit_bytes=24 * 1024 * 1024)

    def mover(kernel, name, shapes, operands, copies, scalars=0, scratch=()):
        return pl.pallas_call(
            kernel,
            out_shape=tuple(jax.ShapeDtypeStruct(shape, bf16) for shape in shapes),
            in_specs=[smem] * scalars + [any_space] * (len(operands) - scalars),
            out_specs=(vmem,) * len(shapes),
            scratch_shapes=[*scratch, pltpu.SemaphoreType.DMA((copies,))],
            compiler_params=limit,
            cost_estimate=pl.CostEstimate(
                flops=0, bytes_accessed=4 * sum(math.prod(s) for s in shapes), transcendentals=0
            ),
            name=name,
        )(*operands)

    place = jnp.stack([along_index, cross_index, window_start[0]]).astype(jnp.int32)

    lead = over(forward)
    (own_ends,) = mover(
        functools.partial(ends_kernel, lines),
        "ends",
        ((2 * LINE_RIM, cols),),
        (hbm(backward),),
        2,
    )
    ends = over(own_ends)
    cuts = (cols // 2, cols - lines - TILE)
    height = lines - 2 * LINE_RIM
    near = lines + 2 * EDGE * lines // TILE
    first_part, near_first, near_last = mover(
        functools.partial(cut_kernel, lines, cols, cuts[0]),
        "cut",
        ((height, cuts[0]), (near, TILE), (near, TILE)),
        (hbm(nadir_view), hbm(forward), hbm(backward), own_ends),
        7,
        scratch=[pltpu.VMEM((2, 2, lines, TILE), bf16)],
    )
    first_part = over(first_part)

    from_right = lax.ppermute(near_first, "cross", low_z)
    from_left = lax.ppermute(near_last, "cross", high_z)
    depth = lines // 2 + 2 * LINE_RIM
    row_count = 4 * MODES // cross_count
    assert 2 * MODES % row_count == 0
    bands = pl.pallas_call(
        functools.partial(bands_kernel, lines, cols, total_lines, total_cols, lag_floor),
        out_shape=(
            jax.ShapeDtypeStruct((2, rows, depth), bf16),
            jax.ShapeDtypeStruct((2, WIDE + 2 * EDGE, cols), bf16),
            jax.ShapeDtypeStruct((8, cols), f32),
            jax.ShapeDtypeStruct((lines, 2 * MODES), f32),
            jax.ShapeDtypeStruct((row_count, lines), f32),
            jax.ShapeDtypeStruct((8, lines), f32),
            jax.ShapeDtypeStruct((2 * MODES, row_count), f32),
        ),
        in_specs=[smem] + [vmem] * 5,
        out_specs=(vmem,) * 7,
        compiler_params=limit,
        cost_estimate=pl.CostEstimate(
            flops=20 * 300 * cols, bytes_accessed=4 * 300 * cols, transcendentals=0
        ),
        name="bands",
    )(
        place, lag_lines[None], hbm(band_offsets), hbm(along_weights), hbm(col_offsets),
        hbm(cross_weights),
    )
    line_bands, col_bands, levers, basis, rows_basis, upper, chosen = bands
    first_lines, last_lines = mover(
        functools.partial(nadir_lines_kernel, lines, cols),
        "nadir_lines",
        ((NADIR_RIM, whole + 4 * TILE), (NADIR_RIM, whole + 4 * TILE)),
        (hbm(nadir_view), from_left, from_right, line_bands),
        14,
    )
    nadir_below = lax.ppermute(first_lines, "along", ring_down)
    nadir_above = lax.ppermute(last_lines, "along", ring_up)

    down, up = mover(
        functools.partial(lines_kernel, lines, half_ring),
        "lines",
        ((3 * LINE_RIM // 2, cols), (3 * LINE_RIM // 2, cols)),
        (place, hbm(forward), hbm(backward), lead, ends),
        2,
        1,
    )
    slab_below = lax.ppermute(down, "along", half_down)
    slab_above = lax.ppermute(up, "along", half_up)

    second_part, third_part = pl.pallas_call(
        functools.partial(late_kernel, lines, cols, cuts),
        out_shape=(
            jax.ShapeDtypeStruct((height + 4 * EDGE, cuts[1] - cuts[0]), bf16),
            jax.ShapeDtypeStruct((height, cols - cuts[1]), bf16),
        ),
        in_specs=[any_space, any_space, any_space, vmem, vmem],
        out_specs=(vmem, vmem),
        scratch_shapes=[pltpu.SemaphoreType.DMA((2 + 4 * lines // TILE,))],
        compiler_params=limit,
        cost_estimate=pl.CostEstimate(flops=0, bytes_accessed=lines * cols, transcendentals=0),
        name="late_cut",
    )(hbm(backward), from_left, from_right, nadir_above, nadir_below)
    second_part, third_part = over(second_part), over(third_part)

    slopes, center, inverse, lever, sums = pl.pallas_call(
        functools.partial(prep_kernel, lines, cols, total_cols),
        out_shape=(
            jax.ShapeDtypeStruct((rows, cols), f32),
            jax.ShapeDtypeStruct((rows, cols), bf16),
            jax.ShapeDtypeStruct((lines, cols), f32),
            jax.ShapeDtypeStruct((lines, cols), f32),
            jax.ShapeDtypeStruct((8, lines), f32),
        ),
        in_specs=[smem] + [vmem] * 5 + [any_space],
        out_specs=(vmem,) * 5,
        scratch_shapes=[pltpu.VMEM((lines + 2 * NADIR_RIM, whole), bf16)],
        compiler_params=limit,
        cost_estimate=pl.CostEstimate(
            flops=2 * rows * cols * 512, bytes_accessed=12 * rows * cols, transcendentals=0
        ),
        name="prep",
    )(place, hbm(nadir_view), from_left, from_right, nadir_above, nadir_below, down)

    def run(name, jobs, crossed, so_far, last):
        fresh = so_far is None
        operands = [
            slopes, center, inverse, lever, line_bands, col_bands, levers, basis, slab_above, slab_below,
            ends, *crossed,
        ]
        specs = [vmem] * len(operands)
        aliases = {}
        if not fresh:
            aliases = {len(operands) + 1: 0}
            operands += [so_far[1], so_far[0]]
            specs += [vmem, any_space]
        scratch = []
        for _, _, width in jobs:
            scratch += [
                pltpu.VMEM((lines + 2 * LINE_RIM, width + 2 * TILE), bf16),
                pltpu.VMEM((rows, width + 2 * TILE), bf16),
                pltpu.VMEM((lines, width), bf16),
            ]
        done = sum(width for _, _, width in jobs)
        return pl.pallas_call(
            functools.partial(slab_kernel, lines, cols, cuts, jobs, len(crossed), fresh, last),
            out_shape=(
                pltpu.HBM((2, lines, cols), bf16),
                jax.ShapeDtypeStruct((8, TILE) if last else (2, lines, TILE), f32),
            ),
            in_specs=specs,
            out_specs=(any_space, vmem),
            scratch_shapes=[pltpu.SemaphoreType.DMA((len(jobs),)), *scratch],
            input_output_aliases=aliases,
            compiler_params=limit,
            cost_estimate=pl.CostEstimate(
                flops=2 * rows * (done + 256) * 900, bytes_accessed=20 * rows * done, transcendentals=0
            ),
            name=name,
        )(*operands)

    so_far = run("inner", [(0, TILE, cols - 2 * TILE)], [lead], None, False)
    jobs = [(1, 0, cuts[1] - TILE), (0, 0, TILE), (0, cols - TILE, TILE)]
    so_far = run("second", jobs, [lead, first_part, second_part], so_far, False)
    jobs = [(1, cuts[1] - TILE, cols - cuts[1] + TILE)]
    crossed = [lead, first_part, second_part, third_part]
    parallax, pulled = run("third", jobs, crossed, so_far, True)

    share = jnp.concatenate([sums, pulled], axis=1)
    shares = [share]
    for shift_by in range(1, cross_count):
        pairs = [(i, (i + shift_by) % cross_count) for i in range(cross_count)]
        shares.append(lax.ppermute(share, "cross", pairs))
    scale_pull = 1.0 / (lines * total_cols) ** 0.5
    normal_gram, normal_rhs = pl.pallas_call(
        functools.partial(final_kernel, lines, scale_pull),
        out_shape=(
            jax.ShapeDtypeStruct((1, row_count, 4 * MODES), f32),
            jax.ShapeDtypeStruct((1, row_count), f32),
        ),
        in_specs=[vmem] * (4 + len(shares)),
        out_specs=(vmem, vmem),
        compiler_params=limit,
        name="final",
    )(basis, rows_basis, upper, chosen, *shares)
    return parallax, normal_gram, normal_rhs


def solution(mesh):
    placed = (
        P("along", "cross"),
        P("along", "cross"),
        P("along", "cross"),
        P(),
        P(None, None, "cross"),
        P(),
        P(None, "cross"),
        P(),
        P(),
    )
    return jax.shard_map(
        local,
        mesh=mesh,
        in_specs=placed,
        out_specs=(P(None, "along", "cross"), P("along", "cross", None), P("along", "cross")),
        check_vma=False,
    )
```

```python
import functools
import math

import jax
import jax.numpy as jnp
from jax import lax
from jax.experimental import pallas as pl
from jax.experimental.pallas import tpu as pltpu
from jax.sharding import PartitionSpec as P

TAPS = 4
CAMERA_LAG = 20480
BOX = 4
MODES = 64
LINE_RIM = 32
NADIR_RIM = 16
TILE = 128
WIDE = 256
EDGE = 16


def box_sum(x, lines):
    rows = x.shape[0]
    two = x + pltpu.roll(x, rows - 1, 0)
    four = two + pltpu.roll(two, rows - 2, 0)
    eight = four + pltpu.roll(four, rows - 4, 0)
    return eight[:lines] + x[2 * BOX : lines + 2 * BOX]


def lane_fold(x):
    folded = x[:, :TILE]
    for at in range(TILE, x.shape[1], TILE):
        folded = folded + x[:, at : at + TILE]
    return folded


def copy_all(moves, sem):
    copies = [pltpu.make_async_copy(a, b, sem.at[n]) for n, (a, b) in enumerate(moves)]
    for copy in copies:
        copy.start()
    for copy in copies:
        copy.wait()


def cut_kernel(
    lines, cols, cut, nadir, forward, backward, ends, first_part, near_first, near_last, side, sem
):
    body = pl.ds(LINE_RIM, lines - 2 * LINE_RIM)
    moves = [(backward.at[body, pl.ds(0, cut)], first_part)]
    for n, (begin, near) in enumerate(((0, near_first), (cols - TILE, near_last))):
        moves.append((nadir.at[:, pl.ds(begin, TILE)], near.at[pl.ds(0, lines), :]))
        for s, slab in enumerate((forward, backward)):
            moves.append((slab.at[:, pl.ds(begin, TILE)], side.at[s, n]))
    copy_all(moves, sem)
    for n, (row, near) in enumerate(((0, near_first), (TILE - EDGE, near_last))):
        for s in range(2):
            turned = side[s, n].astype(jnp.float32).T[row : row + EDGE].astype(jnp.bfloat16)
            for k in range(lines // TILE):
                at = lines + (s * (lines // TILE) + k) * EDGE
                near[at : at + EDGE, :] = turned[:, k * TILE : (k + 1) * TILE]


def ends_kernel(lines, forward, backward, lead_ends, ends, sem):
    moves = []
    for slab, out in ((backward, ends), (forward, lead_ends)):
        for n, row in enumerate((0, lines - LINE_RIM)):
            target = pl.ds(n * LINE_RIM, LINE_RIM)
            moves.append((slab.at[pl.ds(row, LINE_RIM), :], out.at[target, :]))
    copy_all(moves, sem)


def nadir_lines_kernel(lines, cols, nadir, from_left, from_right, bands, first, last, sem):
    moves = []
    whole = cols + 2 * TILE
    for out, row, tile in ((first, 0, 0), (last, lines - NADIR_RIM, lines // TILE - 1)):
        span = pl.ds(row, NADIR_RIM)
        moves.append((from_left.at[span, :], out.at[:, pl.ds(0, TILE)]))
        moves.append((nadir.at[span, :], out.at[:, pl.ds(TILE, cols)]))
        moves.append((from_right.at[span, :], out.at[:, pl.ds(TILE + cols, TILE)]))
        for n, near in enumerate((from_left, from_right)):
            for s in range(2):
                at = lines + (s * (lines // TILE) + tile) * EDGE
                target = pl.ds(whole + (2 * n + s) * TILE, TILE)
                moves.append((near.at[pl.ds(at, EDGE), :], out.at[:, target]))
    copy_all(moves, sem)


def late_kernel(
    lines, cols, cuts, backward, from_left, from_right, above, below, second, third, sem
):
    height = lines - 2 * LINE_RIM
    whole = cols + 2 * TILE
    body = pl.ds(LINE_RIM, height)
    width = cuts[1] - cuts[0]
    moves = [
        (backward.at[body, pl.ds(cuts[0], width)], second.at[pl.ds(0, height), :]),
        (backward.at[body, pl.ds(cuts[1], cols - cuts[1])], third),
    ]
    lane = lax.broadcasted_iota(jnp.int32, (EDGE, TILE), 1)
    for k in range(4):
        row = height + k * EDGE
        near = (from_left, from_right)[k // 2]
        for tile in range(lines // TILE):
            at = lines + (k % 2 * (lines // TILE) + tile) * EDGE
            window = second.at[pl.ds(row, EDGE), pl.ds(tile * TILE, TILE)]
            moves.append((near.at[pl.ds(at, EDGE), :], window))
        here = slice(whole + k * TILE, whole + (k + 1) * TILE)
        ahead = above[:, here].astype(jnp.float32)
        behind = below[:, here].astype(jnp.float32)
        both = jnp.where(lane < TILE // 2, behind, ahead).astype(jnp.bfloat16)
        second[row : row + EDGE, lines : lines + TILE] = both
    if width > lines + TILE:
        second[height:, lines + TILE :] = jnp.zeros((4 * EDGE, width - lines - TILE), jnp.bfloat16)
    copy_all(moves, sem)


def lines_kernel(lines, flags, own_lead, own_ends, lead, ends, down, up):
    most, least = LINE_RIM, LINE_RIM // 2
    for out, flag, counts in ((down, 0, (least, most)), (up, 1, (most, least))):
        as_lies = flags[flag : flag + 1, :] > 0.5
        at = 0
        for own, crossed, tall, count in (
            (own_lead, lead, lines, counts[0]),
            (own_ends, ends, 2 * LINE_RIM, counts[1]),
        ):
            here = 0 if out is down else 2 * LINE_RIM - count
            there = 0 if out is down else tall - count
            lying = own[here : here + count, :].astype(jnp.float32)
            moved = crossed[there : there + count, :].astype(jnp.float32)
            out[at : at + count, :] = jnp.where(as_lies, lying, moved).astype(jnp.bfloat16)
            at += count


def positions(place, cols, total_cols, at, span):
    column = lax.broadcasted_iota(jnp.int32, (1, span), 1) + (place[1] * cols + at)
    position = (column.astype(jnp.float32) + 0.5) / total_cols + 0.25
    return position, position * position


def prep_kernel(
    lines, cols, total_cols, place, nadir, left, right, above, below, down,
    slopes, center, inverse, lever, sums, framed,
):
    tall = lines + 2 * NADIR_RIM
    rows = lines + 16
    framed[0:NADIR_RIM, :] = above[:, 0 : cols + 2 * TILE]
    framed[NADIR_RIM + lines : tall, :] = below[:, 0 : cols + 2 * TILE]
    framed[NADIR_RIM : NADIR_RIM + lines, 0:TILE] = left[0:lines, :]
    framed[NADIR_RIM : NADIR_RIM + lines, TILE : TILE + cols] = nadir[...]
    framed[NADIR_RIM : NADIR_RIM + lines, TILE + cols :] = right[0:lines, :]
    row = lax.broadcasted_iota(jnp.int32, (2 * WIDE, WIDE), 0)
    col = lax.broadcasted_iota(jnp.int32, (2 * WIDE, WIDE), 1)
    gap = jnp.abs(row - TILE - col)
    smear = jnp.where(gap == 0, 2.0, jnp.where(gap == 1, 1.0, 0.0)).astype(jnp.bfloat16)
    totals = [jnp.zeros((lines, TILE), jnp.float32) for _ in range(3)]
    for at in range(0, cols, WIDE):
        across = jnp.dot(
            framed[:, at : at + 2 * WIDE], smear, preferred_element_type=jnp.float32
        )
        change = pltpu.roll(across, tall - 5, 0) - pltpu.roll(across, tall - 3, 0)
        slope = change[8 : 8 + rows] * 0.25
        slopes[:, at : at + WIDE] = slope
        middle = framed[:, TILE + at : TILE + at + WIDE].astype(jnp.float32)
        middle = pltpu.roll(middle, tall - 4, 0)[8 : 8 + rows]
        center[:, at : at + WIDE] = middle.astype(jnp.bfloat16)
        level = box_sum(slope * slope, lines) * (1.0 / (2 * BOX + 1))
        inverted = (-1.0 / (2 * BOX + 1)) / jnp.maximum(level, 0.4)
        inverse[:, at : at + WIDE] = inverted
        lever[:, at : at + WIDE] = level * inverted
        position, square = positions(place, cols, total_cols, at, WIDE)
        for k, power in enumerate((square, square * position, square * square)):
            totals[k] = totals[k] + lane_fold(level * power)
    lane = lax.broadcasted_iota(jnp.int32, (lines, TILE), 1)
    packed = jnp.zeros((lines, TILE), jnp.float32)
    for k in range(3):
        packed = jnp.where(lane == k, jnp.sum(totals[k], axis=1, keepdims=True), packed)
    sums[...] = packed.T[0:8, :] * (1.0 / (lines * total_cols))


def cosines(phases, sines):
    period = 4 * MODES
    turned = jnp.where(sines, phases + (period - MODES), phases) % period
    return jnp.cos(turned.astype(jnp.float32) * (2.0 * jnp.pi / period))


def bands_kernel(
    lines, cols, total_lines, total_cols, half_ring, lag_floor, place, lag, offsets, weights, shifts,
    taps, line_bands, col_bands, levers, basis, rows_basis, upper, chosen, flags,
):
    rows = lines + 16
    period = 4 * MODES
    for s in range(2):
        for n in range(cols // WIDE):
            here = slice(n * WIDE, (n + 1) * WIDE)
            row = lax.broadcasted_iota(jnp.int32, (WIDE + 2 * EDGE, WIDE), 0)
            col = lax.broadcasted_iota(jnp.int32, (WIDE + 2 * EDGE, WIDE), 1)
            distance = row - col - EDGE - shifts[s : s + 1, here]
            weight = taps[s, :, here].astype(jnp.float32)
            band = jnp.zeros((WIDE + 2 * EDGE, WIDE), jnp.float32)
            for tap in range(TAPS):
                band = jnp.where(distance == tap, weight[tap : tap + 1], band)
            col_bands[s, :, here] = band.astype(jnp.bfloat16)
    position, square = positions(place, cols, total_cols, 0, cols)
    levers[0:1, :] = position
    levers[1:2, :] = square
    levers[2:, :] = jnp.zeros((6, cols), jnp.float32)
    start = place[2] + place[0] * lines
    line = start + lax.broadcasted_iota(jnp.int32, (lines, 2 * MODES), 0)
    mode = lax.broadcasted_iota(jnp.int32, (lines, 2 * MODES), 1)
    basis[...] = cosines(line % period * (2 * (mode % MODES) + 1), mode >= MODES)
    count = rows_basis.shape[0]
    row_first = place[1] * count
    row_at = lax.rem(row_first, 2 * MODES)
    mode = row_at + lax.broadcasted_iota(jnp.int32, (count, lines), 0)
    line = start + lax.broadcasted_iota(jnp.int32, (count, lines), 1)
    rows_basis[...] = cosines(line % period * (2 * (mode % MODES) + 1), mode >= MODES)
    upper[...] = jnp.zeros_like(upper) + jnp.where(row_first >= 2 * MODES, 1.0, 0.0)
    own = row_at + lax.broadcasted_iota(jnp.int32, (2 * MODES, count), 1)
    mode = lax.broadcasted_iota(jnp.int32, (2 * MODES, count), 0)
    chosen[...] = jnp.where(own == mode, 1.0, 0.0)
    in_half = lax.rem(place[0], half_ring)
    row = lax.broadcasted_iota(jnp.int32, flags.shape, 0)
    wanted = jnp.where(row == 0, 0, half_ring - 1)
    flags[...] = jnp.where(wanted == in_half, 1.0, 0.0)
    begin = place[0] * lines
    ahead = pl.multiple_of(lax.rem(begin + total_lines - TILE, total_lines), TILE)
    behind = pl.multiple_of(lax.rem(begin + lines, total_lines), TILE)
    begin = pl.multiple_of(begin, TILE)

    def window(ref, lead):
        parts = [
            ref[lead + (slice(None), pl.ds(start, size))].astype(jnp.float32)
            for start, size in ((ahead, TILE), (begin, lines), (behind, TILE))
        ]
        return jnp.concatenate(parts, axis=1)

    wide = lines + 2 * TILE
    lags = window(lag, ()) - float(lag_floor)
    shifts = window(offsets, ())
    stacked = jnp.concatenate(
        [
            jnp.broadcast_to(shifts[0:1] - lags, (8, wide)),
            jnp.broadcast_to(shifts[1:2] + lags, (8, wide)),
            window(weights, (0,)),
            window(weights, (1,)),
            jnp.zeros((TILE - 24, wide), jnp.float32),
        ],
        axis=0,
    )
    as_columns = pltpu.roll(stacked.T, wide - (TILE - BOX), 0)[0:rows]
    half = lines // 2
    depth = half + 2 * LINE_RIM
    for s in range(2):
        for first, last in ((0, half), (half, rows)):
            at = lax.broadcasted_iota(jnp.int32, (last - first, depth), 1)
            own = lax.broadcasted_iota(jnp.int32, (last - first, depth), 0)
            distance = (at - own - (LINE_RIM - BOX)).astype(jnp.float32)
            distance = distance - as_columns[first:last, 8 * s : 8 * s + 1]
            band = jnp.zeros((last - first, depth), jnp.float32)
            for tap in range(TAPS):
                weight = as_columns[first:last, 16 + 4 * s + tap : 17 + 4 * s + tap]
                band = jnp.where(distance == float(tap), weight, band)
            line_bands[s, first:last, :] = band.astype(jnp.bfloat16)


def slab_kernel(
    lines, cols, cuts, jobs, count, fresh, last,
    slopes, center, inverse, lever, line_bands, col_bands, levers, basis, above, below, ends, *rest,
):
    lead, first_part, second_part, third_part = (*rest[:count], None, None, None)[:4]
    rest = rest[count:]
    if not fresh:
        earlier, rest = rest[0], rest[1:]
    if fresh:
        parallax, pulled, sem, *scratch = rest
    else:
        kept, (pulled, *scratch) = rest[: len(jobs)], rest[len(jobs) :]
        scratch[2::3] = kept
    rows = lines + 16
    half = lines // 2
    depth = half + 2 * LINE_RIM
    height = lines - 2 * LINE_RIM
    most, least = LINE_RIM, LINE_RIM // 2
    writes = []
    if fresh:
        pulls = [jnp.zeros((lines, TILE), jnp.float32) for _ in range(2)]
    else:
        pulls = [earlier[k] for k in range(2)]
    for n, (s, first, width) in enumerate(jobs):
        ext, along, result = scratch[3 * n : 3 * n + 3]
        low, high = first - TILE, first + width + TILE
        over, under = ((most, least), (least, most))[s]
        pieces = [
            (above, (0, most)[s], LINE_RIM - over, over, 0, cols),
            (below, (0, least)[s], LINE_RIM + lines, under, 0, cols),
        ]
        if s == 0:
            pieces.append((lead, 0, LINE_RIM, lines, 0, cols))
        else:
            pieces.append((ends, 0, LINE_RIM, LINE_RIM, 0, cols))
            pieces.append((ends, LINE_RIM, lines, LINE_RIM, 0, cols))
            pieces.append((first_part, 0, 2 * LINE_RIM, height, 0, cuts[0]))
            pieces.append((second_part, 0, 2 * LINE_RIM, height, cuts[0], cuts[1]))
            pieces.append((third_part, 0, 2 * LINE_RIM, height, cuts[1], cols))
        for ref, row, target, tall, begin, end in pieces:
            a, b = max(low, begin), min(high, end)
            if a < b:
                ext[target : target + tall, a - low : b - low] = ref[
                    row : row + tall, a - begin : b - begin
                ]
        blank = jnp.zeros((least, width + 2 * TILE), jnp.bfloat16)
        if s == 0:
            ext[2 * LINE_RIM + lines - least :, :] = blank
        else:
            ext[:least, :] = blank
        for side in range(2):
            if (low < 0, high > cols)[side]:
                at = 0 if side == 0 else width + TILE
                row = height + (2 * side + s) * EDGE
                piece = second_part[row : row + EDGE, : lines + TILE].astype(jnp.float32)
                gap = jnp.zeros((TILE - EDGE, lines + TILE), jnp.float32)
                piece = jnp.concatenate([gap, piece] if side == 0 else [piece, gap], axis=0)
                turned = piece.T.astype(jnp.bfloat16)
                ext[LINE_RIM : LINE_RIM + lines, at : at + TILE] = turned[:lines]
                ext[LINE_RIM - over : LINE_RIM, at : at + TILE] = turned[lines + TILE - over :]
                ext[LINE_RIM + lines : LINE_RIM + lines + under, at : at + TILE] = turned[
                    lines : lines + under
                ]
        for at in range(0, width + 2 * TILE, WIDE):
            end = min(at + WIDE, width + 2 * TILE)
            for start, stop in ((0, half), (half, rows)):
                along[start:stop, at:end] = jnp.dot(
                    line_bands[s, start:stop, :],
                    ext[start : start + depth, at:end],
                    preferred_element_type=jnp.float32,
                ).astype(jnp.bfloat16)
        bounds = sorted({first, first + width, *range(-(-first // WIDE) * WIDE, first + width, WIDE)})
        for at, end in zip(bounds[:-1], bounds[1:]):
            at, span = at - first, end - at
            blank = jnp.zeros((TILE - EDGE, span), jnp.bfloat16)
            offset = first + at
            inner = offset % WIDE
            band = col_bands[s, inner : inner + span + 2 * EDGE, offset : offset + span]
            resampled = jnp.dot(
                along[:, at : at + span + 2 * TILE],
                jnp.concatenate([blank, band, blank], axis=0),
                preferred_element_type=jnp.float32,
            ).astype(jnp.bfloat16)
            for part in range(0, span, TILE):
                here = slice(at + part, at + part + TILE)
                there = slice(first + at + part, first + at + part + TILE)
                mismatch = resampled[:, part : part + TILE].astype(jnp.float32)
                mismatch = mismatch - center[:, there].astype(jnp.float32)
                boxed = box_sum(slopes[:, there] * mismatch, lines)
                result[:, here] = (boxed * inverse[:, there]).astype(jnp.bfloat16)
                weighted = boxed * lever[:, there]
                for k in range(2):
                    pulls[k] = pulls[k] + weighted * levers[k : k + 1, there]
        if fresh:
            write = pltpu.make_async_copy(
                result, parallax.at[s, :, pl.ds(first, width)], sem.at[n]
            )
            write.start()
            writes.append(write)
    if last:
        pulled[...] = jnp.zeros_like(pulled)
        for k in range(2):
            per_line = jnp.sum(pulls[k], axis=1, keepdims=True)
            pulled[k : k + 1, :] = jnp.sum(basis[...] * per_line, axis=0, keepdims=True)
    else:
        for k in range(2):
            pulled[k] = pulls[k]
    for write in writes:
        write.wait()


def store_kernel(jobs, *rest):
    parallax, sem = rest[-2:]
    copy_all(
        [
            (kept, parallax.at[s, :, pl.ds(first, width)])
            for kept, (s, first, width) in zip(rest, jobs)
        ],
        sem,
    )


def final_kernel(lines, scale_pull, basis, rows_basis, upper, chosen, *rest):
    shares, (gram, rhs) = rest[:-2], rest[-2:]
    total = shares[0][...]
    for share in shares[1:]:
        total = total + share[...]
    is_upper = upper[0:1, :] > 0.5
    sums = total[:, :lines]
    precision = lax.Precision.HIGHEST
    for n in range(2):
        coef = jnp.where(is_upper, sums[n + 1 : n + 2], sums[n : n + 1])
        gram[0, :, n * TILE : (n + 1) * TILE] = jnp.dot(
            rows_basis[...] * coef, basis[...], precision=precision, preferred_element_type=jnp.float32
        )
    pull = jnp.where(is_upper[:, :TILE], total[1:2, lines:], total[0:1, lines:]) * scale_pull
    rhs[...] = jnp.dot(
        jnp.broadcast_to(pull, (8, TILE)), chosen[...], precision=precision, preferred_element_type=jnp.float32
    )[0:1]


def local(
    nadir_view, forward, backward, along_weights, cross_weights, band_offsets, col_offsets,
    lag_lines, window_start,
):
    lines, cols = nadir_view.shape
    along_count = lax.axis_size("along")
    cross_count = lax.axis_size("cross")
    along_index = lax.axis_index("along")
    cross_index = lax.axis_index("cross")
    total_lines = lines * along_count
    total_cols = cols * cross_count
    half_ring = along_count // 2
    lag_floor = CAMERA_LAG // total_lines * total_lines + half_ring * lines
    rows = lines + 16
    whole = cols + 2 * TILE
    assert cross_count % 2 == 0 and half_ring % 2 == 0
    even_along, even_cross = along_index % 2 == 0, cross_index % 2 == 0
    across = [(i, (i + half_ring) % along_count) for i in range(along_count)]

    def swap(axis, pairs, even, to_before, to_behind):
        count = lax.axis_size(axis)
        inside = [(i, i ^ 1) for i in range(count)]
        both = [*pairs, *((j, i) for i, j in pairs)]
        near = lax.ppermute(jnp.where(even, to_behind, to_before), axis, inside)
        far = lax.ppermute(jnp.where(even, to_before, to_behind), axis, both)
        return jnp.where(even, far, near), jnp.where(even, near, far)

    whole_ring = [(i, (i + 1) % along_count) for i in range(1, along_count, 2)]
    half_rings = [
        (i, i // half_ring * half_ring + (i + 1) % half_ring) for i in range(1, along_count, 2)
    ]
    line = [(i, i + 1) for i in range(1, cross_count - 1, 2)]

    def over(value):
        return lax.ppermute(value, "along", across)

    def hbm(value):
        return pltpu.with_memory_space_constraint(value, pltpu.HBM)

    f32, bf16 = jnp.float32, jnp.bfloat16
    any_space = pl.BlockSpec(memory_space=pl.ANY)
    vmem = pl.BlockSpec(memory_space=pltpu.VMEM)
    smem = pl.BlockSpec(memory_space=pltpu.SMEM)
    limit = pltpu.CompilerParams(vmem_limit_bytes=24 * 1024 * 1024)

    def mover(kernel, name, shapes, operands, copies, scalars=0, scratch=()):
        return pl.pallas_call(
            kernel,
            out_shape=tuple(jax.ShapeDtypeStruct(shape, bf16) for shape in shapes),
            in_specs=[smem] * scalars + [any_space] * (len(operands) - scalars),
            out_specs=(vmem,) * len(shapes),
            scratch_shapes=[*scratch, pltpu.SemaphoreType.DMA((copies,))],
            compiler_params=limit,
            cost_estimate=pl.CostEstimate(
                flops=0, bytes_accessed=4 * sum(math.prod(s) for s in shapes), transcendentals=0
            ),
            name=name,
        )(*operands)

    place = jnp.stack([along_index, cross_index, window_start[0]]).astype(jnp.int32)

    lead = over(forward)
    own_lead, own_ends = mover(
        functools.partial(ends_kernel, lines),
        "ends",
        ((2 * LINE_RIM, cols), (2 * LINE_RIM, cols)),
        (hbm(forward), hbm(backward)),
        4,
    )
    ends = over(own_ends)
    cuts = (cols // 2, cols - lines - TILE)
    height = lines - 2 * LINE_RIM
    near = lines + 2 * EDGE * lines // TILE
    first_part, near_first, near_last = mover(
        functools.partial(cut_kernel, lines, cols, cuts[0]),
        "cut",
        ((height, cuts[0]), (near, TILE), (near, TILE)),
        (hbm(nadir_view), hbm(forward), hbm(backward), own_ends),
        7,
        scratch=[pltpu.VMEM((2, 2, lines, TILE), bf16)],
    )
    first_part = over(first_part)

    from_left, from_right = swap("cross", line, even_cross, near_first, near_last)
    depth = lines // 2 + 2 * LINE_RIM
    row_count = 4 * MODES // cross_count
    assert 2 * MODES % row_count == 0
    bands = pl.pallas_call(
        functools.partial(
            bands_kernel, lines, cols, total_lines, total_cols, half_ring, lag_floor
        ),
        out_shape=(
            jax.ShapeDtypeStruct((2, rows, depth), bf16),
            jax.ShapeDtypeStruct((2, WIDE + 2 * EDGE, cols), bf16),
            jax.ShapeDtypeStruct((8, cols), f32),
            jax.ShapeDtypeStruct((lines, 2 * MODES), f32),
            jax.ShapeDtypeStruct((row_count, lines), f32),
            jax.ShapeDtypeStruct((8, lines), f32),
            jax.ShapeDtypeStruct((2 * MODES, row_count), f32),
            jax.ShapeDtypeStruct((8, cols), f32),
        ),
        in_specs=[smem] + [vmem] * 5,
        out_specs=(vmem,) * 8,
        compiler_params=limit,
        cost_estimate=pl.CostEstimate(
            flops=20 * 300 * cols, bytes_accessed=4 * 300 * cols, transcendentals=0
        ),
        name="bands",
    )(
        place, lag_lines[None], hbm(band_offsets), hbm(along_weights), hbm(col_offsets),
        hbm(cross_weights),
    )
    line_bands, col_bands, levers, basis, rows_basis, upper, chosen, flags = bands
    first_lines, last_lines = mover(
        functools.partial(nadir_lines_kernel, lines, cols),
        "nadir_lines",
        ((NADIR_RIM, whole + 4 * TILE), (NADIR_RIM, whole + 4 * TILE)),
        (hbm(nadir_view), from_left, from_right, line_bands),
        14,
    )
    nadir_above, nadir_below = swap("along", whole_ring, even_along, first_lines, last_lines)

    most_lines = 3 * LINE_RIM // 2
    down, up = pl.pallas_call(
        functools.partial(lines_kernel, lines),
        out_shape=(jax.ShapeDtypeStruct((most_lines, cols), bf16),) * 2,
        in_specs=[vmem] * 5,
        out_specs=(vmem, vmem),
        compiler_params=limit,
        cost_estimate=pl.CostEstimate(
            flops=0, bytes_accessed=16 * most_lines * cols, transcendentals=0
        ),
        name="lines",
    )(flags, own_lead, own_ends, lead, ends)
    slab_above, slab_below = swap("along", half_rings, even_along, down, up)

    second_part, third_part = pl.pallas_call(
        functools.partial(late_kernel, lines, cols, cuts),
        out_shape=(
            jax.ShapeDtypeStruct((height + 4 * EDGE, cuts[1] - cuts[0]), bf16),
            jax.ShapeDtypeStruct((height, cols - cuts[1]), bf16),
        ),
        in_specs=[any_space, any_space, any_space, vmem, vmem],
        out_specs=(vmem, vmem),
        scratch_shapes=[pltpu.SemaphoreType.DMA((2 + 4 * lines // TILE,))],
        compiler_params=limit,
        cost_estimate=pl.CostEstimate(flops=0, bytes_accessed=lines * cols, transcendentals=0),
        name="late_cut",
    )(hbm(backward), from_left, from_right, nadir_above, nadir_below)
    second_part, third_part = over(second_part), over(third_part)

    slopes, center, inverse, lever, sums = pl.pallas_call(
        functools.partial(prep_kernel, lines, cols, total_cols),
        out_shape=(
            jax.ShapeDtypeStruct((rows, cols), f32),
            jax.ShapeDtypeStruct((rows, cols), bf16),
            jax.ShapeDtypeStruct((lines, cols), f32),
            jax.ShapeDtypeStruct((lines, cols), f32),
            jax.ShapeDtypeStruct((8, lines), f32),
        ),
        in_specs=[smem] + [vmem] * 5 + [any_space],
        out_specs=(vmem,) * 5,
        scratch_shapes=[pltpu.VMEM((lines + 2 * NADIR_RIM, whole), bf16)],
        compiler_params=limit,
        cost_estimate=pl.CostEstimate(
            flops=2 * rows * cols * 512, bytes_accessed=12 * rows * cols, transcendentals=0
        ),
        name="prep",
    )(place, hbm(nadir_view), from_left, from_right, nadir_above, nadir_below, down)

    def run(name, jobs, crossed, so_far, last):
        fresh = so_far is None
        operands = [
            slopes, center, inverse, lever, line_bands, col_bands, levers, basis, slab_above, slab_below,
            ends, *crossed,
        ]
        specs = [vmem] * len(operands)
        if not fresh:
            operands.append(so_far)
            specs.append(vmem)
        scratch = []
        for _, _, width in jobs:
            scratch += [
                pltpu.VMEM((lines + 2 * LINE_RIM, width + 2 * TILE), bf16),
                pltpu.VMEM((rows, width + 2 * TILE), bf16),
                pltpu.VMEM((lines, width), bf16),
            ]
        done = sum(width for _, _, width in jobs)
        return pl.pallas_call(
            functools.partial(slab_kernel, lines, cols, cuts, jobs, len(crossed), fresh, last),
            out_shape=(
                *(
                    (pltpu.HBM((2, lines, cols), bf16),)
                    if fresh
                    else (jax.ShapeDtypeStruct((lines, width), bf16) for _, _, width in jobs)
                ),
                jax.ShapeDtypeStruct((8, TILE) if last else (2, lines, TILE), f32),
            ),
            in_specs=specs,
            out_specs=(any_space, vmem) if fresh else (vmem,) * (len(jobs) + 1),
            scratch_shapes=[pltpu.SemaphoreType.DMA((len(jobs),)), *scratch] if fresh else scratch,
            compiler_params=limit,
            cost_estimate=pl.CostEstimate(
                flops=2 * rows * (done + 256) * 900, bytes_accessed=20 * rows * done, transcendentals=0
            ),
            name=name,
        )(*operands)

    split = cuts[0] - TILE
    jobs = [(0, TILE, cols - 2 * TILE), (1, TILE, split - TILE)]
    parallax, pulls = run("inner", jobs, [lead, first_part], None, False)
    jobs = [(1, split, cuts[1] - TILE - split), (0, 0, TILE), (0, cols - TILE, TILE), (1, 0, TILE)]
    *kept, pulls = run("second", jobs, [lead, first_part, second_part], pulls, False)
    last_jobs = [(1, cuts[1] - TILE, cols - cuts[1] + TILE)]
    crossed = [lead, first_part, second_part, third_part]
    *last_kept, pulled = run("third", last_jobs, crossed, pulls, True)
    kept, jobs = [*kept, *last_kept], jobs + last_jobs
    parallax = pl.pallas_call(
        functools.partial(store_kernel, jobs),
        out_shape=pltpu.HBM((2, lines, cols), bf16),
        in_specs=[vmem] * len(kept) + [any_space],
        out_specs=any_space,
        scratch_shapes=[pltpu.SemaphoreType.DMA((len(kept),))],
        input_output_aliases={len(kept): 0},
        compiler_params=limit,
        cost_estimate=pl.CostEstimate(flops=0, bytes_accessed=2 * lines * cols, transcendentals=0),
        name="store",
    )(*kept, parallax)

    share = jnp.concatenate([sums, pulled], axis=1)
    shares = [share]
    assert cross_count & (cross_count - 1) == 0
    for shift_by in range(1, cross_count):
        pairs = [(i, (i + shift_by) % cross_count) for i in range(cross_count)]
        shares.append(lax.ppermute(share, "cross", pairs))
    scale_pull = 1.0 / (lines * total_cols) ** 0.5
    normal_gram, normal_rhs = pl.pallas_call(
        functools.partial(final_kernel, lines, scale_pull),
        out_shape=(
            jax.ShapeDtypeStruct((1, row_count, 4 * MODES), f32),
            jax.ShapeDtypeStruct((1, row_count), f32),
        ),
        in_specs=[vmem] * (4 + len(shares)),
        out_specs=(vmem, vmem),
        compiler_params=limit,
        name="final",
    )(basis, rows_basis, upper, chosen, *shares)
    return parallax, normal_gram, normal_rhs


def solution(mesh):
    placed = (
        P("along", "cross"),
        P("along", "cross"),
        P("along", "cross"),
        P(),
        P(None, None, "cross"),
        P(),
        P(None, "cross"),
        P(),
        P(),
    )
    return jax.shard_map(
        local,
        mesh=mesh,
        in_specs=placed,
        out_specs=(P(None, "along", "cross"), P("along", "cross", None), P("along", "cross")),
        check_vma=False,
    )
```

```python
import functools
import math

import jax
import jax.numpy as jnp
from jax import lax
from jax.experimental import pallas as pl
from jax.experimental.pallas import tpu as pltpu
from jax.sharding import PartitionSpec as P

TAPS = 4
CAMERA_LAG = 20480
BOX = 4
MODES = 64
LINE_RIM = 32
NADIR_RIM = 16
TILE = 128
WIDE = 256
EDGE = 16
LESS = 8


def box_sum(x, lines):
    rows = x.shape[0]
    two = x + pltpu.roll(x, rows - 1, 0)
    four = two + pltpu.roll(two, rows - 2, 0)
    eight = four + pltpu.roll(four, rows - 4, 0)
    return eight[:lines] + x[2 * BOX : lines + 2 * BOX]


def lane_fold(x):
    folded = x[:, :TILE]
    for at in range(TILE, x.shape[1], TILE):
        folded = folded + x[:, at : at + TILE]
    return folded


def copy_all(moves, sem):
    copies = [pltpu.make_async_copy(a, b, sem.at[n]) for n, (a, b) in enumerate(moves)]
    for copy in copies:
        copy.start()
    for copy in copies:
        copy.wait()


def cut_kernel(
    lines, cols, cut, nadir, forward, backward, ends, first_part, near_first, near_last, side, sem
):
    body = pl.ds(LINE_RIM, lines - 2 * LINE_RIM)
    moves = [(backward.at[body, pl.ds(0, cut)], first_part)]
    for n, (begin, near) in enumerate(((0, near_first), (cols - TILE, near_last))):
        moves.append((nadir.at[:, pl.ds(begin, TILE)], near.at[pl.ds(0, lines), :]))
        for s, slab in enumerate((forward, backward)):
            moves.append((slab.at[:, pl.ds(begin, TILE)], side.at[s, n]))
    copy_all(moves, sem)
    for n, (row, near) in enumerate(((0, near_first), (TILE - EDGE, near_last))):
        for s in range(2):
            turned = side[s, n].astype(jnp.float32).T[row : row + EDGE].astype(jnp.bfloat16)
            for k in range(lines // TILE):
                at = lines + (s * (lines // TILE) + k) * EDGE
                near[at : at + EDGE, :] = turned[:, k * TILE : (k + 1) * TILE]


def ends_kernel(lines, forward, backward, lead_ends, ends, sem):
    moves = []
    for slab, out in ((backward, ends), (forward, lead_ends)):
        for n, row in enumerate((0, lines - LINE_RIM)):
            target = pl.ds(n * LINE_RIM, LINE_RIM)
            moves.append((slab.at[pl.ds(row, LINE_RIM), :], out.at[target, :]))
    copy_all(moves, sem)


def nadir_lines_kernel(lines, cols, nadir, from_left, from_right, bands, first, last, sem):
    moves = []
    whole = cols + 2 * TILE
    for out, row, tile in ((first, 0, 0), (last, lines - NADIR_RIM, lines // TILE - 1)):
        span = pl.ds(row, NADIR_RIM)
        moves.append((from_left.at[span, :], out.at[:, pl.ds(0, TILE)]))
        moves.append((nadir.at[span, :], out.at[:, pl.ds(TILE, cols)]))
        moves.append((from_right.at[span, :], out.at[:, pl.ds(TILE + cols, TILE)]))
        for n, near in enumerate((from_left, from_right)):
            for s in range(2):
                at = lines + (s * (lines // TILE) + tile) * EDGE
                target = pl.ds(whole + (2 * n + s) * TILE, TILE)
                moves.append((near.at[pl.ds(at, EDGE), :], out.at[:, target]))
    copy_all(moves, sem)


def late_kernel(
    lines, cols, cuts, backward, from_left, from_right, above, below, second, third, sem
):
    height = lines - 2 * LINE_RIM
    whole = cols + 2 * TILE
    body = pl.ds(LINE_RIM, height)
    width = cuts[1] - cuts[0]
    moves = [
        (backward.at[body, pl.ds(cuts[0], width)], second.at[pl.ds(0, height), :]),
        (backward.at[body, pl.ds(cuts[1], cols - cuts[1])], third),
    ]
    lane = lax.broadcasted_iota(jnp.int32, (EDGE, TILE), 1)
    kinds = []
    for k in range(4):
        near = (from_left, from_right)[k // 2]
        tiles = []
        for tile in range(lines // TILE):
            at = lines + (k % 2 * (lines // TILE) + tile) * EDGE
            tiles.append(near[at : at + EDGE, :].astype(jnp.float32))
        here = slice(whole + k * TILE, whole + (k + 1) * TILE)
        ahead = above[:, here].astype(jnp.float32)
        behind = below[:, here].astype(jnp.float32)
        tiles.append(jnp.where(lane < TILE // 2, behind, ahead))
        kinds.append(jnp.concatenate(tiles, axis=1))
    left = jnp.concatenate([kind[EDGE - LESS :] for kind in kinds[:2]], axis=0)
    for n, block in enumerate((left, *kinds[2:])):
        row = height + n * EDGE
        second[row : row + EDGE, : lines + TILE] = block.astype(jnp.bfloat16)
    if width > lines + TILE:
        second[height:, lines + TILE :] = jnp.zeros((3 * EDGE, width - lines - TILE), jnp.bfloat16)
    copy_all(moves, sem)


def lines_kernel(lines, flags, own_lead, own_ends, lead, ends, down, up):
    most, least = LINE_RIM, LINE_RIM // 2
    for out, flag, counts in ((down, 0, (least, most)), (up, 1, (most, least))):
        as_lies = flags[flag : flag + 1, :] > 0.5
        at = 0
        for own, crossed, tall, count in (
            (own_lead, lead, lines, counts[0]),
            (own_ends, ends, 2 * LINE_RIM, counts[1]),
        ):
            here = 0 if out is down else 2 * LINE_RIM - count
            there = 0 if out is down else tall - count
            lying = own[here : here + count, :].astype(jnp.float32)
            moved = crossed[there : there + count, :].astype(jnp.float32)
            out[at : at + count, :] = jnp.where(as_lies, lying, moved).astype(jnp.bfloat16)
            at += count


def positions(place, cols, total_cols, at, span):
    column = lax.broadcasted_iota(jnp.int32, (1, span), 1) + (place[1] * cols + at)
    position = (column.astype(jnp.float32) + 0.5) / total_cols + 0.25
    return position, position * position


def prep_kernel(
    lines, cols, total_cols, place, nadir, left, right, above, below, down,
    slopes, center, inverse, lever, sums, framed,
):
    tall = lines + 2 * NADIR_RIM
    rows = lines + 16
    framed[0:NADIR_RIM, :] = above[:, 0 : cols + 2 * TILE]
    framed[NADIR_RIM + lines : tall, :] = below[:, 0 : cols + 2 * TILE]
    framed[NADIR_RIM : NADIR_RIM + lines, 0:TILE] = left[0:lines, :]
    framed[NADIR_RIM : NADIR_RIM + lines, TILE : TILE + cols] = nadir[...]
    framed[NADIR_RIM : NADIR_RIM + lines, TILE + cols :] = right[0:lines, :]
    row = lax.broadcasted_iota(jnp.int32, (2 * WIDE, WIDE), 0)
    col = lax.broadcasted_iota(jnp.int32, (2 * WIDE, WIDE), 1)
    gap = jnp.abs(row - TILE - col)
    smear = jnp.where(gap == 0, 2.0, jnp.where(gap == 1, 1.0, 0.0)).astype(jnp.bfloat16)
    totals = [jnp.zeros((lines, TILE), jnp.float32) for _ in range(3)]
    for at in range(0, cols, WIDE):
        across = jnp.dot(
            framed[:, at : at + 2 * WIDE], smear, preferred_element_type=jnp.float32
        )
        change = pltpu.roll(across, tall - 5, 0) - pltpu.roll(across, tall - 3, 0)
        slope = change[8 : 8 + rows] * 0.25
        slopes[:, at : at + WIDE] = slope
        middle = framed[:, TILE + at : TILE + at + WIDE].astype(jnp.float32)
        middle = pltpu.roll(middle, tall - 4, 0)[8 : 8 + rows]
        center[:, at : at + WIDE] = middle.astype(jnp.bfloat16)
        level = box_sum(slope * slope, lines) * (1.0 / (2 * BOX + 1))
        inverted = (-1.0 / (2 * BOX + 1)) / jnp.maximum(level, 0.4)
        inverse[:, at : at + WIDE] = inverted
        lever[:, at : at + WIDE] = level * inverted
        position, square = positions(place, cols, total_cols, at, WIDE)
        for k, power in enumerate((square, square * position, square * square)):
            totals[k] = totals[k] + lane_fold(level * power)
    lane = lax.broadcasted_iota(jnp.int32, (lines, TILE), 1)
    packed = jnp.zeros((lines, TILE), jnp.float32)
    for k in range(3):
        packed = jnp.where(lane == k, jnp.sum(totals[k], axis=1, keepdims=True), packed)
    sums[...] = packed.T[0:8, :] * (1.0 / (lines * total_cols))


def cosines(phases, sines):
    period = 4 * MODES
    turned = jnp.where(sines, phases + (period - MODES), phases) % period
    return jnp.cos(turned.astype(jnp.float32) * (2.0 * jnp.pi / period))


def bands_kernel(
    lines, cols, total_lines, total_cols, half_ring, lag_floor, place, lag, offsets, weights, shifts,
    taps, line_bands, col_bands, levers, basis, rows_basis, upper, chosen, flags,
):
    rows = lines + 16
    period = 4 * MODES
    for s in range(2):
        for n in range(cols // WIDE):
            here = slice(n * WIDE, (n + 1) * WIDE)
            row = lax.broadcasted_iota(jnp.int32, (WIDE + 2 * EDGE, WIDE), 0)
            col = lax.broadcasted_iota(jnp.int32, (WIDE + 2 * EDGE, WIDE), 1)
            distance = row - col - EDGE - shifts[s : s + 1, here]
            weight = taps[s, :, here].astype(jnp.float32)
            band = jnp.zeros((WIDE + 2 * EDGE, WIDE), jnp.float32)
            for tap in range(TAPS):
                band = jnp.where(distance == tap, weight[tap : tap + 1], band)
            col_bands[s, :, here] = band.astype(jnp.bfloat16)
    position, square = positions(place, cols, total_cols, 0, cols)
    levers[0:1, :] = position
    levers[1:2, :] = square
    levers[2:, :] = jnp.zeros((6, cols), jnp.float32)
    start = place[2] + place[0] * lines
    line = start + lax.broadcasted_iota(jnp.int32, (lines, 2 * MODES), 0)
    mode = lax.broadcasted_iota(jnp.int32, (lines, 2 * MODES), 1)
    basis[...] = cosines(line % period * (2 * (mode % MODES) + 1), mode >= MODES)
    count = rows_basis.shape[0]
    row_first = place[1] * count
    row_at = lax.rem(row_first, 2 * MODES)
    mode = row_at + lax.broadcasted_iota(jnp.int32, (count, lines), 0)
    line = start + lax.broadcasted_iota(jnp.int32, (count, lines), 1)
    rows_basis[...] = cosines(line % period * (2 * (mode % MODES) + 1), mode >= MODES)
    upper[...] = jnp.zeros_like(upper) + jnp.where(row_first >= 2 * MODES, 1.0, 0.0)
    own = row_at + lax.broadcasted_iota(jnp.int32, (2 * MODES, count), 1)
    mode = lax.broadcasted_iota(jnp.int32, (2 * MODES, count), 0)
    chosen[...] = jnp.where(own == mode, 1.0, 0.0)
    in_half = lax.rem(place[0], half_ring)
    row = lax.broadcasted_iota(jnp.int32, flags.shape, 0)
    wanted = jnp.where(row == 0, 0, half_ring - 1)
    flags[...] = jnp.where(wanted == in_half, 1.0, 0.0)
    begin = place[0] * lines
    ahead = pl.multiple_of(lax.rem(begin + total_lines - TILE, total_lines), TILE)
    behind = pl.multiple_of(lax.rem(begin + lines, total_lines), TILE)
    begin = pl.multiple_of(begin, TILE)

    def window(ref, lead):
        parts = [
            ref[lead + (slice(None), pl.ds(start, size))].astype(jnp.float32)
            for start, size in ((ahead, TILE), (begin, lines), (behind, TILE))
        ]
        return jnp.concatenate(parts, axis=1)

    wide = lines + 2 * TILE
    lags = window(lag, ()) - float(lag_floor)
    shifts = window(offsets, ())
    stacked = jnp.concatenate(
        [
            jnp.broadcast_to(shifts[0:1] - lags, (8, wide)),
            jnp.broadcast_to(shifts[1:2] + lags, (8, wide)),
            window(weights, (0,)),
            window(weights, (1,)),
            jnp.zeros((TILE - 24, wide), jnp.float32),
        ],
        axis=0,
    )
    as_columns = pltpu.roll(stacked.T, wide - (TILE - BOX), 0)[0:rows]
    half = lines // 2
    depth = half + 2 * LINE_RIM
    for s in range(2):
        for first, last in ((0, half), (half, rows)):
            at = lax.broadcasted_iota(jnp.int32, (last - first, depth), 1)
            own = lax.broadcasted_iota(jnp.int32, (last - first, depth), 0)
            distance = (at - own - (LINE_RIM - BOX)).astype(jnp.float32)
            distance = distance - as_columns[first:last, 8 * s : 8 * s + 1]
            band = jnp.zeros((last - first, depth), jnp.float32)
            for tap in range(TAPS):
                weight = as_columns[first:last, 16 + 4 * s + tap : 17 + 4 * s + tap]
                band = jnp.where(distance == float(tap), weight, band)
            line_bands[s, first:last, :] = band.astype(jnp.bfloat16)


def slab_kernel(
    lines, cols, cuts, jobs, count, fresh, last,
    slopes, center, inverse, lever, line_bands, col_bands, levers, basis, above, below, ends, *rest,
):
    lead, first_part, second_part, third_part = (*rest[:count], None, None, None)[:4]
    rest = rest[count:]
    if not fresh:
        earlier, rest = rest[0], rest[1:]
    if fresh:
        parallax, pulled, sem, *scratch = rest
    else:
        kept, (pulled, *scratch) = rest[: len(jobs)], rest[len(jobs) :]
        scratch[2::3] = kept
    rows = lines + 16
    half = lines // 2
    depth = half + 2 * LINE_RIM
    height = lines - 2 * LINE_RIM
    most, least = LINE_RIM, LINE_RIM // 2
    writes = []
    if fresh:
        pulls = [jnp.zeros((lines, TILE), jnp.float32) for _ in range(2)]
    else:
        pulls = [earlier[k] for k in range(2)]
    for n, (s, first, width) in enumerate(jobs):
        ext, along, result = scratch[3 * n : 3 * n + 3]
        low, high = first - TILE, first + width + TILE
        over, under = ((most, least), (least, most))[s]
        pieces = [
            (above, (0, most)[s], LINE_RIM - over, over, 0, cols),
            (below, (0, least)[s], LINE_RIM + lines, under, 0, cols),
        ]
        if s == 0:
            pieces.append((lead, 0, LINE_RIM, lines, 0, cols))
        else:
            pieces.append((ends, 0, LINE_RIM, LINE_RIM, 0, cols))
            pieces.append((ends, LINE_RIM, lines, LINE_RIM, 0, cols))
            pieces.append((first_part, 0, 2 * LINE_RIM, height, 0, cuts[0]))
            pieces.append((second_part, 0, 2 * LINE_RIM, height, cuts[0], cuts[1]))
            pieces.append((third_part, 0, 2 * LINE_RIM, height, cuts[1], cols))
        for ref, row, target, tall, begin, end in pieces:
            a, b = max(low, begin), min(high, end)
            if a < b:
                ext[target : target + tall, a - low : b - low] = ref[
                    row : row + tall, a - begin : b - begin
                ]
        blank = jnp.zeros((least, width + 2 * TILE), jnp.bfloat16)
        if s == 0:
            ext[2 * LINE_RIM + lines - least :, :] = blank
        else:
            ext[:least, :] = blank
        for side in range(2):
            if (low < 0, high > cols)[side]:
                at = 0 if side == 0 else width + TILE
                row = height + (0 if side == 0 else (1 + s) * EDGE)
                piece = second_part[row : row + EDGE, : lines + TILE].astype(jnp.float32)
                if side == 0:
                    piece = piece[s * LESS : (s + 1) * LESS]
                gap = jnp.zeros((TILE - piece.shape[0], lines + TILE), jnp.float32)
                piece = jnp.concatenate([gap, piece] if side == 0 else [piece, gap], axis=0)
                turned = piece.T.astype(jnp.bfloat16)
                ext[LINE_RIM : LINE_RIM + lines, at : at + TILE] = turned[:lines]
                ext[LINE_RIM - over : LINE_RIM, at : at + TILE] = turned[lines + TILE - over :]
                ext[LINE_RIM + lines : LINE_RIM + lines + under, at : at + TILE] = turned[
                    lines : lines + under
                ]
        for at in range(0, width + 2 * TILE, WIDE):
            end = min(at + WIDE, width + 2 * TILE)
            for start, stop in ((0, half), (half, rows)):
                along[start:stop, at:end] = jnp.dot(
                    line_bands[s, start:stop, :],
                    ext[start : start + depth, at:end],
                    preferred_element_type=jnp.float32,
                ).astype(jnp.bfloat16)
        bounds = sorted({first, first + width, *range(-(-first // WIDE) * WIDE, first + width, WIDE)})
        for at, end in zip(bounds[:-1], bounds[1:]):
            at, span = at - first, end - at
            blank = jnp.zeros((TILE - EDGE, span), jnp.bfloat16)
            offset = first + at
            inner = offset % WIDE
            band = col_bands[s, inner : inner + span + 2 * EDGE, offset : offset + span]
            resampled = jnp.dot(
                along[:, at : at + span + 2 * TILE],
                jnp.concatenate([blank, band, blank], axis=0),
                preferred_element_type=jnp.float32,
            ).astype(jnp.bfloat16)
            for part in range(0, span, TILE):
                here = slice(at + part, at + part + TILE)
                there = slice(first + at + part, first + at + part + TILE)
                mismatch = resampled[:, part : part + TILE].astype(jnp.float32)
                mismatch = mismatch - center[:, there].astype(jnp.float32)
                boxed = box_sum(slopes[:, there] * mismatch, lines)
                result[:, here] = (boxed * inverse[:, there]).astype(jnp.bfloat16)
                weighted = boxed * lever[:, there]
                for k in range(2):
                    pulls[k] = pulls[k] + weighted * levers[k : k + 1, there]
        if fresh:
            write = pltpu.make_async_copy(
                result, parallax.at[s, :, pl.ds(first, width)], sem.at[n]
            )
            write.start()
            writes.append(write)
    if last:
        pulled[...] = jnp.zeros_like(pulled)
        for k in range(2):
            per_line = jnp.sum(pulls[k], axis=1, keepdims=True)
            pulled[k : k + 1, :] = jnp.sum(basis[...] * per_line, axis=0, keepdims=True)
    else:
        for k in range(2):
            pulled[k] = pulls[k]
    for write in writes:
        write.wait()


def store_kernel(jobs, *rest):
    parallax, sem = rest[-2:]
    copy_all(
        [
            (kept, parallax.at[s, :, pl.ds(first, width)])
            for kept, (s, first, width) in zip(rest, jobs)
        ],
        sem,
    )


def final_kernel(lines, scale_pull, basis, rows_basis, upper, chosen, *rest):
    shares, (gram, rhs) = rest[:-2], rest[-2:]
    total = shares[0][...]
    for share in shares[1:]:
        total = total + share[...]
    is_upper = upper[0:1, :] > 0.5
    sums = total[:, :lines]
    count = rows_basis.shape[0]
    rows = [
        rows_basis[...] * jnp.where(is_upper, sums[n + 1 : n + 2], sums[n : n + 1]) for n in range(2)
    ]
    both = jnp.dot(
        jnp.concatenate(rows, axis=0),
        basis[...],
        precision=lax.Precision.HIGHEST,
        preferred_element_type=jnp.float32,
    )
    gram[0, :, :TILE] = both[:count]
    gram[0, :, TILE:] = both[count:]
    pull = jnp.where(is_upper[:, :TILE], total[1:2, lines:], total[0:1, lines:]) * scale_pull
    own = jnp.zeros((1, count), jnp.float32)
    for at in range(0, TILE, count):
        own = jnp.where(chosen[at : at + 1, 0:1] > 0.5, pull[:, at : at + count], own)
    rhs[...] = own


def local(
    nadir_view, forward, backward, along_weights, cross_weights, band_offsets, col_offsets,
    lag_lines, window_start,
):
    lines, cols = nadir_view.shape
    along_count = lax.axis_size("along")
    cross_count = lax.axis_size("cross")
    along_index = lax.axis_index("along")
    cross_index = lax.axis_index("cross")
    total_lines = lines * along_count
    total_cols = cols * cross_count
    half_ring = along_count // 2
    lag_floor = CAMERA_LAG // total_lines * total_lines + half_ring * lines
    rows = lines + 16
    whole = cols + 2 * TILE
    assert cross_count % 2 == 0 and half_ring % 2 == 0
    even_along, even_cross = along_index % 2 == 0, cross_index % 2 == 0
    across = [(i, (i + half_ring) % along_count) for i in range(along_count)]

    def swap(axis, pairs, even, to_before, to_behind):
        count = lax.axis_size(axis)
        inside = [(i, i ^ 1) for i in range(count)]
        both = [*pairs, *((j, i) for i, j in pairs)]
        near = lax.ppermute(jnp.where(even, to_behind, to_before), axis, inside)
        far = lax.ppermute(jnp.where(even, to_before, to_behind), axis, both)
        return jnp.where(even, far, near), jnp.where(even, near, far)

    whole_ring = [(i, (i + 1) % along_count) for i in range(1, along_count, 2)]
    half_rings = [
        (i, i // half_ring * half_ring + (i + 1) % half_ring) for i in range(1, along_count, 2)
    ]
    line = [(i, i + 1) for i in range(1, cross_count - 1, 2)]

    def over(value):
        return lax.ppermute(value, "along", across)

    def hbm(value):
        return pltpu.with_memory_space_constraint(value, pltpu.HBM)

    f32, bf16 = jnp.float32, jnp.bfloat16
    any_space = pl.BlockSpec(memory_space=pl.ANY)
    vmem = pl.BlockSpec(memory_space=pltpu.VMEM)
    smem = pl.BlockSpec(memory_space=pltpu.SMEM)
    limit = pltpu.CompilerParams(vmem_limit_bytes=24 * 1024 * 1024)

    def mover(kernel, name, shapes, operands, copies, scalars=0, scratch=()):
        return pl.pallas_call(
            kernel,
            out_shape=tuple(jax.ShapeDtypeStruct(shape, bf16) for shape in shapes),
            in_specs=[smem] * scalars + [any_space] * (len(operands) - scalars),
            out_specs=(vmem,) * len(shapes),
            scratch_shapes=[*scratch, pltpu.SemaphoreType.DMA((copies,))],
            compiler_params=limit,
            cost_estimate=pl.CostEstimate(
                flops=0, bytes_accessed=4 * sum(math.prod(s) for s in shapes), transcendentals=0
            ),
            name=name,
        )(*operands)

    place = jnp.stack([along_index, cross_index, window_start[0]]).astype(jnp.int32)

    lead = over(forward)
    own_lead, own_ends = mover(
        functools.partial(ends_kernel, lines),
        "ends",
        ((2 * LINE_RIM, cols), (2 * LINE_RIM, cols)),
        (hbm(forward), hbm(backward)),
        4,
    )
    ends = over(own_ends)
    cuts = (cols // 2, cols - lines - TILE)
    height = lines - 2 * LINE_RIM
    near = lines + 2 * EDGE * lines // TILE
    first_part, near_first, near_last = mover(
        functools.partial(cut_kernel, lines, cols, cuts[0]),
        "cut",
        ((height, cuts[0]), (near, TILE), (near, TILE)),
        (hbm(nadir_view), hbm(forward), hbm(backward), own_ends),
        7,
        scratch=[pltpu.VMEM((2, 2, lines, TILE), bf16)],
    )
    first_part = over(first_part)

    from_left, from_right = swap("cross", line, even_cross, near_first, near_last)
    depth = lines // 2 + 2 * LINE_RIM
    row_count = 4 * MODES // cross_count
    assert 2 * MODES % row_count == 0
    bands = pl.pallas_call(
        functools.partial(
            bands_kernel, lines, cols, total_lines, total_cols, half_ring, lag_floor
        ),
        out_shape=(
            jax.ShapeDtypeStruct((2, rows, depth), bf16),
            jax.ShapeDtypeStruct((2, WIDE + 2 * EDGE, cols), bf16),
            jax.ShapeDtypeStruct((8, cols), f32),
            jax.ShapeDtypeStruct((lines, 2 * MODES), f32),
            jax.ShapeDtypeStruct((row_count, lines), f32),
            jax.ShapeDtypeStruct((8, lines), f32),
            jax.ShapeDtypeStruct((2 * MODES, row_count), f32),
            jax.ShapeDtypeStruct((8, cols), f32),
        ),
        in_specs=[smem] + [vmem] * 5,
        out_specs=(vmem,) * 8,
        compiler_params=limit,
        cost_estimate=pl.CostEstimate(
            flops=20 * 300 * cols, bytes_accessed=4 * 300 * cols, transcendentals=0
        ),
        name="bands",
    )(
        place, lag_lines[None], hbm(band_offsets), hbm(along_weights), hbm(col_offsets),
        hbm(cross_weights),
    )
    line_bands, col_bands, levers, basis, rows_basis, upper, chosen, flags = bands
    first_lines, last_lines = mover(
        functools.partial(nadir_lines_kernel, lines, cols),
        "nadir_lines",
        ((NADIR_RIM, whole + 4 * TILE), (NADIR_RIM, whole + 4 * TILE)),
        (hbm(nadir_view), from_left, from_right, line_bands),
        14,
    )
    nadir_above, nadir_below = swap("along", whole_ring, even_along, first_lines, last_lines)

    most_lines = 3 * LINE_RIM // 2
    down, up = pl.pallas_call(
        functools.partial(lines_kernel, lines),
        out_shape=(jax.ShapeDtypeStruct((most_lines, cols), bf16),) * 2,
        in_specs=[vmem] * 5,
        out_specs=(vmem, vmem),
        compiler_params=limit,
        cost_estimate=pl.CostEstimate(
            flops=0, bytes_accessed=16 * most_lines * cols, transcendentals=0
        ),
        name="lines",
    )(flags, own_lead, own_ends, lead, ends)
    slab_above, slab_below = swap("along", half_rings, even_along, down, up)

    second_part, third_part = pl.pallas_call(
        functools.partial(late_kernel, lines, cols, cuts),
        out_shape=(
            jax.ShapeDtypeStruct((height + 3 * EDGE, cuts[1] - cuts[0]), bf16),
            jax.ShapeDtypeStruct((height, cols - cuts[1]), bf16),
        ),
        in_specs=[any_space, vmem, vmem, vmem, vmem],
        out_specs=(vmem, vmem),
        scratch_shapes=[pltpu.SemaphoreType.DMA((2,))],
        compiler_params=limit,
        cost_estimate=pl.CostEstimate(flops=0, bytes_accessed=lines * cols, transcendentals=0),
        name="late_cut",
    )(hbm(backward), from_left, from_right, nadir_above, nadir_below)
    second_part, third_part = over(second_part), over(third_part)

    slopes, center, inverse, lever, sums = pl.pallas_call(
        functools.partial(prep_kernel, lines, cols, total_cols),
        out_shape=(
            jax.ShapeDtypeStruct((rows, cols), f32),
            jax.ShapeDtypeStruct((rows, cols), bf16),
            jax.ShapeDtypeStruct((lines, cols), f32),
            jax.ShapeDtypeStruct((lines, cols), f32),
            jax.ShapeDtypeStruct((8, lines), f32),
        ),
        in_specs=[smem] + [vmem] * 5 + [any_space],
        out_specs=(vmem,) * 5,
        scratch_shapes=[pltpu.VMEM((lines + 2 * NADIR_RIM, whole), bf16)],
        compiler_params=limit,
        cost_estimate=pl.CostEstimate(
            flops=2 * rows * cols * 512, bytes_accessed=12 * rows * cols, transcendentals=0
        ),
        name="prep",
    )(place, hbm(nadir_view), from_left, from_right, nadir_above, nadir_below, down)

    def run(name, jobs, crossed, so_far, last):
        fresh = so_far is None
        operands = [
            slopes, center, inverse, lever, line_bands, col_bands, levers, basis, slab_above, slab_below,
            ends, *crossed,
        ]
        specs = [vmem] * len(operands)
        if not fresh:
            operands.append(so_far)
            specs.append(vmem)
        scratch = []
        for _, _, width in jobs:
            scratch += [
                pltpu.VMEM((lines + 2 * LINE_RIM, width + 2 * TILE), bf16),
                pltpu.VMEM((rows, width + 2 * TILE), bf16),
                pltpu.VMEM((lines, width), bf16),
            ]
        done = sum(width for _, _, width in jobs)
        return pl.pallas_call(
            functools.partial(slab_kernel, lines, cols, cuts, jobs, len(crossed), fresh, last),
            out_shape=(
                *(
                    (pltpu.HBM((2, lines, cols), bf16),)
                    if fresh
                    else (jax.ShapeDtypeStruct((lines, width), bf16) for _, _, width in jobs)
                ),
                jax.ShapeDtypeStruct((8, TILE) if last else (2, lines, TILE), f32),
            ),
            in_specs=specs,
            out_specs=(any_space, vmem) if fresh else (vmem,) * (len(jobs) + 1),
            scratch_shapes=[pltpu.SemaphoreType.DMA((len(jobs),)), *scratch] if fresh else scratch,
            compiler_params=limit,
            cost_estimate=pl.CostEstimate(
                flops=2 * rows * (done + 256) * 900, bytes_accessed=20 * rows * done, transcendentals=0
            ),
            name=name,
        )(*operands)

    split = cuts[0] - TILE
    jobs = [(0, TILE, cols - 2 * TILE), (1, TILE, split - TILE)]
    parallax, pulls = run("inner", jobs, [lead, first_part], None, False)
    jobs = [(1, split, cuts[1] - TILE - split), (0, 0, TILE), (0, cols - TILE, TILE), (1, 0, TILE)]
    *kept, pulls = run("second", jobs, [lead, first_part, second_part], pulls, False)
    last_jobs = [(1, cuts[1] - TILE, cols - cuts[1] + TILE)]
    crossed = [lead, first_part, second_part, third_part]
    *last_kept, pulled = run("third", last_jobs, crossed, pulls, True)
    kept, jobs = [*kept, *last_kept], jobs + last_jobs
    parallax = pl.pallas_call(
        functools.partial(store_kernel, jobs),
        out_shape=pltpu.HBM((2, lines, cols), bf16),
        in_specs=[vmem] * len(kept) + [any_space],
        out_specs=any_space,
        scratch_shapes=[pltpu.SemaphoreType.DMA((len(kept),))],
        input_output_aliases={len(kept): 0},
        compiler_params=limit,
        cost_estimate=pl.CostEstimate(flops=0, bytes_accessed=2 * lines * cols, transcendentals=0),
        name="store",
    )(*kept, parallax)

    share = jnp.concatenate([sums, pulled], axis=1)
    shares = [share]
    assert cross_count & (cross_count - 1) == 0
    for shift_by in range(1, cross_count):
        pairs = [(i, (i + shift_by) % cross_count) for i in range(cross_count)]
        shares.append(lax.ppermute(share, "cross", pairs))
    scale_pull = 1.0 / (lines * total_cols) ** 0.5
    normal_gram, normal_rhs = pl.pallas_call(
        functools.partial(final_kernel, lines, scale_pull),
        out_shape=(
            jax.ShapeDtypeStruct((1, row_count, 4 * MODES), f32),
            jax.ShapeDtypeStruct((1, row_count), f32),
        ),
        in_specs=[vmem] * (4 + len(shares)),
        out_specs=(vmem, vmem),
        compiler_params=limit,
        name="final",
    )(basis, rows_basis, upper, chosen, *shares)
    return parallax, normal_gram, normal_rhs


def solution(mesh):
    placed = (
        P("along", "cross"),
        P("along", "cross"),
        P("along", "cross"),
        P(),
        P(None, None, "cross"),
        P(),
        P(None, "cross"),
        P(),
        P(),
    )
    return jax.shard_map(
        local,
        mesh=mesh,
        in_specs=placed,
        out_specs=(P(None, "along", "cross"), P("along", "cross", None), P("along", "cross")),
        check_vma=False,
    )
```

```python
import functools
import math

import jax
import jax.numpy as jnp
from jax import lax
from jax.experimental import pallas as pl
from jax.experimental.pallas import tpu as pltpu
from jax.sharding import PartitionSpec as P

TAPS = 4
CAMERA_LAG = 20480
BOX = 4
MODES = 64
LINE_RIM = 32
NADIR_RIM = 16
TILE = 128
WIDE = 256
EDGE = 16
LESS = 8


def box_sum(x, lines):
    rows = x.shape[0]
    two = x + pltpu.roll(x, rows - 1, 0)
    four = two + pltpu.roll(two, rows - 2, 0)
    eight = four + pltpu.roll(four, rows - 4, 0)
    return eight[:lines] + x[2 * BOX : lines + 2 * BOX]


def lane_fold(x):
    folded = x[:, :TILE]
    for at in range(TILE, x.shape[1], TILE):
        folded = folded + x[:, at : at + TILE]
    return folded


def copy_all(moves, sem):
    copies = [pltpu.make_async_copy(a, b, sem.at[n]) for n, (a, b) in enumerate(moves)]
    for copy in copies:
        copy.start()
    for copy in copies:
        copy.wait()


def cut_kernel(
    lines, cols, cut, nadir, forward, backward, ends, first_part, near_first, near_last, side, sem
):
    body = pl.ds(LINE_RIM, lines - 2 * LINE_RIM)
    moves = [(backward.at[body, pl.ds(0, cut)], first_part)]
    for n, (begin, near) in enumerate(((0, near_first), (cols - TILE, near_last))):
        moves.append((nadir.at[:, pl.ds(begin, TILE)], near.at[pl.ds(0, lines), :]))
        for s, slab in enumerate((forward, backward)):
            moves.append((slab.at[:, pl.ds(begin, TILE)], side.at[s, n]))
    copy_all(moves, sem)
    for n, (row, near) in enumerate(((0, near_first), (TILE - EDGE, near_last))):
        for s in range(2):
            turned = side[s, n].astype(jnp.float32).T[row : row + EDGE].astype(jnp.bfloat16)
            for k in range(lines // TILE):
                at = lines + (s * (lines // TILE) + k) * EDGE
                near[at : at + EDGE, :] = turned[:, k * TILE : (k + 1) * TILE]


def ends_kernel(lines, forward, backward, lead_ends, ends, sem):
    moves = []
    for slab, out in ((backward, ends), (forward, lead_ends)):
        for n, row in enumerate((0, lines - LINE_RIM)):
            target = pl.ds(n * LINE_RIM, LINE_RIM)
            moves.append((slab.at[pl.ds(row, LINE_RIM), :], out.at[target, :]))
    copy_all(moves, sem)


def nadir_lines_kernel(
    lines, cols, nadir, from_left, from_right, bands, first, last, stage, sem
):
    starts = (0, lines - NADIR_RIM)
    copy_all(
        [(nadir.at[pl.ds(row, NADIR_RIM), :], stage.at[n]) for n, row in enumerate(starts)], sem
    )
    fold = (cols + 2 * TILE) // 2
    for n, (out, row) in enumerate(zip((first, last), starts)):
        span = slice(row, row + NADIR_RIM)
        long = jnp.concatenate([from_left[span, :], stage[n], from_right[span, :]], axis=1)
        long = long.astype(jnp.float32)
        long = long[:LESS] if n == 0 else long[NADIR_RIM - LESS :]
        tile = n * (lines // TILE - 1)
        parts = []
        for near in (from_left, from_right):
            for s in range(2):
                at = lines + (s * (lines // TILE) + tile) * EDGE
                parts.append(near[at : at + EDGE, :].astype(jnp.float32))
        upper = [long[:, :fold], parts[0][EDGE - LESS :], parts[2][:LESS], parts[3][:LESS]]
        lower = [long[:, fold:], parts[1][EDGE - LESS :], parts[2][LESS:], parts[3][LESS:]]
        both = [jnp.concatenate(half, axis=1) for half in (upper, lower)]
        out[...] = jnp.concatenate(both, axis=0).astype(jnp.bfloat16)


def late_kernel(
    lines, cols, cuts, backward, from_left, from_right, above, below, second, third, sem
):
    height = lines - 2 * LINE_RIM
    whole = cols + 2 * TILE
    body = pl.ds(LINE_RIM, height)
    width = cuts[1] - cuts[0]
    moves = [
        (backward.at[body, pl.ds(cuts[0], width)], second.at[pl.ds(0, height), :]),
        (backward.at[body, pl.ds(cuts[1], cols - cuts[1])], third),
    ]
    fold = whole // 2
    lane = lax.broadcasted_iota(jnp.int32, (EDGE, TILE), 1)
    blocks = []
    for n in range(3):
        here = slice(fold + n * TILE, fold + (n + 1) * TILE)
        ahead, behind = (ref[:, here].astype(jnp.float32) for ref in (above, below))
        tiles = []
        for tile in range(lines // TILE):
            at = lines + tile * EDGE
            if n == 0:
                pair = [at + EDGE - LESS, at + lines // TILE * EDGE + EDGE - LESS]
                held = [from_left[k - LESS : k + LESS, :].astype(jnp.float32)[LESS:] for k in pair]
                tiles.append(jnp.concatenate(held, axis=0))
            else:
                at += (n - 1) * (lines // TILE) * EDGE
                tiles.append(from_right[at : at + EDGE, :].astype(jnp.float32))
        tiles.append(jnp.where(lane < TILE // 2, behind, ahead))
        blocks.append(jnp.concatenate(tiles, axis=1))
    for n, block in enumerate(blocks):
        row = height + n * EDGE
        second[row : row + EDGE, : lines + TILE] = block.astype(jnp.bfloat16)
    if width > lines + TILE:
        second[height:, lines + TILE :] = jnp.zeros((3 * EDGE, width - lines - TILE), jnp.bfloat16)
    copy_all(moves, sem)


def lines_kernel(lines, flags, own_lead, own_ends, lead, ends, down, up):
    most, least = LINE_RIM, LINE_RIM // 2
    for out, flag, counts in ((down, 0, (least, most)), (up, 1, (most, least))):
        as_lies = flags[flag : flag + 1, :] > 0.5
        at = 0
        for own, crossed, tall, count in (
            (own_lead, lead, lines, counts[0]),
            (own_ends, ends, 2 * LINE_RIM, counts[1]),
        ):
            here = 0 if out is down else 2 * LINE_RIM - count
            there = 0 if out is down else tall - count
            lying = own[here : here + count, :].astype(jnp.float32)
            moved = crossed[there : there + count, :].astype(jnp.float32)
            out[at : at + count, :] = jnp.where(as_lies, lying, moved).astype(jnp.bfloat16)
            at += count


def positions(place, cols, total_cols, at, span):
    column = lax.broadcasted_iota(jnp.int32, (1, span), 1) + (place[1] * cols + at)
    position = (column.astype(jnp.float32) + 0.5) / total_cols + 0.25
    return position, position * position


def prep_kernel(
    lines, cols, total_cols, place, nadir, left, right, above, below, down,
    slopes, center, inverse, lever, sums, framed,
):
    tall = lines + 2 * NADIR_RIM
    rows = lines + 16
    fold = (cols + 2 * TILE) // 2
    blank = jnp.zeros((NADIR_RIM - LESS, 2 * fold), jnp.float32)
    before, behind = (
        jnp.concatenate([held[:LESS, :fold], held[LESS:, :fold]], axis=1)
        for held in (above[...].astype(jnp.float32), below[...].astype(jnp.float32))
    )
    framed[0:NADIR_RIM, :] = jnp.concatenate([blank, before], axis=0).astype(jnp.bfloat16)
    framed[NADIR_RIM + lines : tall, :] = jnp.concatenate([behind, blank], axis=0).astype(jnp.bfloat16)
    framed[NADIR_RIM : NADIR_RIM + lines, 0:TILE] = left[0:lines, :]
    framed[NADIR_RIM : NADIR_RIM + lines, TILE : TILE + cols] = nadir[...]
    framed[NADIR_RIM : NADIR_RIM + lines, TILE + cols :] = right[0:lines, :]
    row = lax.broadcasted_iota(jnp.int32, (2 * WIDE, WIDE), 0)
    col = lax.broadcasted_iota(jnp.int32, (2 * WIDE, WIDE), 1)
    gap = jnp.abs(row - TILE - col)
    smear = jnp.where(gap == 0, 2.0, jnp.where(gap == 1, 1.0, 0.0)).astype(jnp.bfloat16)
    totals = [jnp.zeros((lines, TILE), jnp.float32) for _ in range(3)]
    for at in range(0, cols, WIDE):
        across = jnp.dot(
            framed[:, at : at + 2 * WIDE], smear, preferred_element_type=jnp.float32
        )
        change = pltpu.roll(across, tall - 5, 0) - pltpu.roll(across, tall - 3, 0)
        slope = change[8 : 8 + rows] * 0.25
        slopes[:, at : at + WIDE] = slope
        middle = framed[:, TILE + at : TILE + at + WIDE].astype(jnp.float32)
        middle = pltpu.roll(middle, tall - 4, 0)[8 : 8 + rows]
        center[:, at : at + WIDE] = middle.astype(jnp.bfloat16)
        level = box_sum(slope * slope, lines) * (1.0 / (2 * BOX + 1))
        inverted = (-1.0 / (2 * BOX + 1)) / jnp.maximum(level, 0.4)
        inverse[:, at : at + WIDE] = inverted
        lever[:, at : at + WIDE] = level * inverted
        position, square = positions(place, cols, total_cols, at, WIDE)
        for k, power in enumerate((square, square * position, square * square)):
            totals[k] = totals[k] + lane_fold(level * power)
    lane = lax.broadcasted_iota(jnp.int32, (lines, TILE), 1)
    packed = jnp.zeros((lines, TILE), jnp.float32)
    for k in range(3):
        packed = jnp.where(lane == k, jnp.sum(totals[k], axis=1, keepdims=True), packed)
    sums[...] = packed.T[0:8, :] * (1.0 / (lines * total_cols))


def cosines(phases, sines):
    period = 4 * MODES
    turned = jnp.where(sines, phases + (period - MODES), phases) % period
    return jnp.cos(turned.astype(jnp.float32) * (2.0 * jnp.pi / period))


def bands_kernel(
    lines, cols, total_lines, total_cols, half_ring, lag_floor, place, lag, offsets, weights, shifts,
    taps, line_bands, col_bands, levers, basis, rows_basis, upper, chosen, flags,
):
    rows = lines + 16
    period = 4 * MODES
    for s in range(2):
        for n in range(cols // WIDE):
            here = slice(n * WIDE, (n + 1) * WIDE)
            row = lax.broadcasted_iota(jnp.int32, (WIDE + 2 * EDGE, WIDE), 0)
            col = lax.broadcasted_iota(jnp.int32, (WIDE + 2 * EDGE, WIDE), 1)
            distance = row - col - EDGE - shifts[s : s + 1, here]
            weight = taps[s, :, here].astype(jnp.float32)
            band = jnp.zeros((WIDE + 2 * EDGE, WIDE), jnp.float32)
            for tap in range(TAPS):
                band = jnp.where(distance == tap, weight[tap : tap + 1], band)
            col_bands[s, :, here] = band.astype(jnp.bfloat16)
    position, square = positions(place, cols, total_cols, 0, cols)
    levers[0:1, :] = position
    levers[1:2, :] = square
    levers[2:, :] = jnp.zeros((6, cols), jnp.float32)
    start = place[2] + place[0] * lines
    line = start + lax.broadcasted_iota(jnp.int32, (lines, 2 * MODES), 0)
    mode = lax.broadcasted_iota(jnp.int32, (lines, 2 * MODES), 1)
    basis[...] = cosines(line % period * (2 * (mode % MODES) + 1), mode >= MODES)
    count = rows_basis.shape[0]
    row_first = place[1] * count
    row_at = lax.rem(row_first, 2 * MODES)
    mode = row_at + lax.broadcasted_iota(jnp.int32, (count, lines), 0)
    line = start + lax.broadcasted_iota(jnp.int32, (count, lines), 1)
    rows_basis[...] = cosines(line % period * (2 * (mode % MODES) + 1), mode >= MODES)
    upper[...] = jnp.zeros_like(upper) + jnp.where(row_first >= 2 * MODES, 1.0, 0.0)
    own = row_at + lax.broadcasted_iota(jnp.int32, (2 * MODES, count), 1)
    mode = lax.broadcasted_iota(jnp.int32, (2 * MODES, count), 0)
    chosen[...] = jnp.where(own == mode, 1.0, 0.0)
    in_half = lax.rem(place[0], half_ring)
    row = lax.broadcasted_iota(jnp.int32, flags.shape, 0)
    wanted = jnp.where(row == 0, 0, half_ring - 1)
    flags[...] = jnp.where(wanted == in_half, 1.0, 0.0)
    begin = place[0] * lines
    ahead = pl.multiple_of(lax.rem(begin + total_lines - TILE, total_lines), TILE)
    behind = pl.multiple_of(lax.rem(begin + lines, total_lines), TILE)
    begin = pl.multiple_of(begin, TILE)

    def window(ref, lead):
        parts = [
            ref[lead + (slice(None), pl.ds(start, size))].astype(jnp.float32)
            for start, size in ((ahead, TILE), (begin, lines), (behind, TILE))
        ]
        return jnp.concatenate(parts, axis=1)

    wide = lines + 2 * TILE
    lags = window(lag, ()) - float(lag_floor)
    shifts = window(offsets, ())
    stacked = jnp.concatenate(
        [
            jnp.broadcast_to(shifts[0:1] - lags, (8, wide)),
            jnp.broadcast_to(shifts[1:2] + lags, (8, wide)),
            window(weights, (0,)),
            window(weights, (1,)),
            jnp.zeros((TILE - 24, wide), jnp.float32),
        ],
        axis=0,
    )
    as_columns = pltpu.roll(stacked.T, wide - (TILE - BOX), 0)[0:rows]
    half = lines // 2
    depth = half + 2 * LINE_RIM
    for s in range(2):
        for first, last in ((0, half), (half, rows)):
            at = lax.broadcasted_iota(jnp.int32, (last - first, depth), 1)
            own = lax.broadcasted_iota(jnp.int32, (last - first, depth), 0)
            distance = (at - own - (LINE_RIM - BOX)).astype(jnp.float32)
            distance = distance - as_columns[first:last, 8 * s : 8 * s + 1]
            band = jnp.zeros((last - first, depth), jnp.float32)
            for tap in range(TAPS):
                weight = as_columns[first:last, 16 + 4 * s + tap : 17 + 4 * s + tap]
                band = jnp.where(distance == float(tap), weight, band)
            line_bands[s, first:last, :] = band.astype(jnp.bfloat16)


def slab_kernel(
    lines, cols, cuts, jobs, count, fresh, last,
    slopes, center, inverse, lever, line_bands, col_bands, levers, basis, above, below, ends, *rest,
):
    lead, first_part, second_part, third_part = (*rest[:count], None, None, None)[:4]
    rest = rest[count:]
    if not fresh:
        earlier, rest = rest[0], rest[1:]
    if fresh:
        parallax, pulled, sem, *scratch = rest
    else:
        kept, (pulled, *scratch) = rest[: len(jobs)], rest[len(jobs) :]
        scratch[2::3] = kept
    rows = lines + 16
    half = lines // 2
    depth = half + 2 * LINE_RIM
    height = lines - 2 * LINE_RIM
    most, least = LINE_RIM, LINE_RIM // 2
    writes = []
    if fresh:
        pulls = [jnp.zeros((lines, TILE), jnp.float32) for _ in range(2)]
    else:
        pulls = [earlier[k] for k in range(2)]
    for n, (s, first, width) in enumerate(jobs):
        ext, along, result = scratch[3 * n : 3 * n + 3]
        low, high = first - TILE, first + width + TILE
        over, under = ((most, least), (least, most))[s]
        pieces = [
            (above, (0, most)[s], LINE_RIM - over, over, 0, cols),
            (below, (0, least)[s], LINE_RIM + lines, under, 0, cols),
        ]
        if s == 0:
            pieces.append((lead, 0, LINE_RIM, lines, 0, cols))
        else:
            pieces.append((ends, 0, LINE_RIM, LINE_RIM, 0, cols))
            pieces.append((ends, LINE_RIM, lines, LINE_RIM, 0, cols))
            pieces.append((first_part, 0, 2 * LINE_RIM, height, 0, cuts[0]))
            pieces.append((second_part, 0, 2 * LINE_RIM, height, cuts[0], cuts[1]))
            pieces.append((third_part, 0, 2 * LINE_RIM, height, cuts[1], cols))
        for ref, row, target, tall, begin, end in pieces:
            a, b = max(low, begin), min(high, end)
            if a < b:
                ext[target : target + tall, a - low : b - low] = ref[
                    row : row + tall, a - begin : b - begin
                ]
        blank = jnp.zeros((least, width + 2 * TILE), jnp.bfloat16)
        if s == 0:
            ext[2 * LINE_RIM + lines - least :, :] = blank
        else:
            ext[:least, :] = blank
        for side in range(2):
            if (low < 0, high > cols)[side]:
                at = 0 if side == 0 else width + TILE
                row = height + (0 if side == 0 else (1 + s) * EDGE)
                piece = second_part[row : row + EDGE, : lines + TILE].astype(jnp.float32)
                if side == 0:
                    piece = piece[s * LESS : (s + 1) * LESS]
                gap = jnp.zeros((TILE - piece.shape[0], lines + TILE), jnp.float32)
                piece = jnp.concatenate([gap, piece] if side == 0 else [piece, gap], axis=0)
                turned = piece.T.astype(jnp.bfloat16)
                ext[LINE_RIM : LINE_RIM + lines, at : at + TILE] = turned[:lines]
                ext[LINE_RIM - over : LINE_RIM, at : at + TILE] = turned[lines + TILE - over :]
                ext[LINE_RIM + lines : LINE_RIM + lines + under, at : at + TILE] = turned[
                    lines : lines + under
                ]
        for at in range(0, width + 2 * TILE, WIDE):
            end = min(at + WIDE, width + 2 * TILE)
            for start, stop in ((0, half), (half, rows)):
                along[start:stop, at:end] = jnp.dot(
                    line_bands[s, start:stop, :],
                    ext[start : start + depth, at:end],
                    preferred_element_type=jnp.float32,
                ).astype(jnp.bfloat16)
        bounds = sorted({first, first + width, *range(-(-first // WIDE) * WIDE, first + width, WIDE)})
        for at, end in zip(bounds[:-1], bounds[1:]):
            at, span = at - first, end - at
            blank = jnp.zeros((TILE - EDGE, span), jnp.bfloat16)
            offset = first + at
            inner = offset % WIDE
            band = col_bands[s, inner : inner + span + 2 * EDGE, offset : offset + span]
            resampled = jnp.dot(
                along[:, at : at + span + 2 * TILE],
                jnp.concatenate([blank, band, blank], axis=0),
                preferred_element_type=jnp.float32,
            ).astype(jnp.bfloat16)
            for part in range(0, span, TILE):
                here = slice(at + part, at + part + TILE)
                there = slice(first + at + part, first + at + part + TILE)
                mismatch = resampled[:, part : part + TILE].astype(jnp.float32)
                mismatch = mismatch - center[:, there].astype(jnp.float32)
                boxed = box_sum(slopes[:, there] * mismatch, lines)
                result[:, here] = (boxed * inverse[:, there]).astype(jnp.bfloat16)
                weighted = boxed * lever[:, there]
                for k in range(2):
                    pulls[k] = pulls[k] + weighted * levers[k : k + 1, there]
        if fresh:
            write = pltpu.make_async_copy(
                result, parallax.at[s, :, pl.ds(first, width)], sem.at[n]
            )
            write.start()
            writes.append(write)
    if last:
        pulled[...] = jnp.zeros_like(pulled)
        for k in range(2):
            per_line = jnp.sum(pulls[k], axis=1, keepdims=True)
            pulled[k : k + 1, :] = jnp.sum(basis[...] * per_line, axis=0, keepdims=True)
    else:
        for k in range(2):
            pulled[k] = pulls[k]
    for write in writes:
        write.wait()


def store_kernel(jobs, *rest):
    parallax, sem = rest[-2:]
    copy_all(
        [
            (kept, parallax.at[s, :, pl.ds(first, width)])
            for kept, (s, first, width) in zip(rest, jobs)
        ],
        sem,
    )


def final_kernel(lines, scale_pull, basis, rows_basis, upper, chosen, *rest):
    shares, (gram, rhs) = rest[:-2], rest[-2:]
    total = shares[0][...]
    for share in shares[1:]:
        total = total + share[...]
    is_upper = upper[0:1, :] > 0.5
    sums = total[:, :lines]
    count = rows_basis.shape[0]
    rows = [
        rows_basis[...] * jnp.where(is_upper, sums[n + 1 : n + 2], sums[n : n + 1]) for n in range(2)
    ]
    both = jnp.dot(
        jnp.concatenate(rows, axis=0),
        basis[...],
        precision=lax.Precision.HIGHEST,
        preferred_element_type=jnp.float32,
    )
    gram[0, :, :TILE] = both[:count]
    gram[0, :, TILE:] = both[count:]
    pull = jnp.where(is_upper[:, :TILE], total[1:2, lines:], total[0:1, lines:]) * scale_pull
    own = jnp.zeros((1, count), jnp.float32)
    for at in range(0, TILE, count):
        own = jnp.where(chosen[at : at + 1, 0:1] > 0.5, pull[:, at : at + count], own)
    rhs[...] = own


def local(
    nadir_view, forward, backward, along_weights, cross_weights, band_offsets, col_offsets,
    lag_lines, window_start,
):
    lines, cols = nadir_view.shape
    along_count = lax.axis_size("along")
    cross_count = lax.axis_size("cross")
    along_index = lax.axis_index("along")
    cross_index = lax.axis_index("cross")
    total_lines = lines * along_count
    total_cols = cols * cross_count
    half_ring = along_count // 2
    lag_floor = CAMERA_LAG // total_lines * total_lines + half_ring * lines
    rows = lines + 16
    whole = cols + 2 * TILE
    assert cross_count % 2 == 0 and half_ring % 2 == 0
    even_along, even_cross = along_index % 2 == 0, cross_index % 2 == 0
    across = [(i, (i + half_ring) % along_count) for i in range(along_count)]

    def swap(axis, pairs, even, to_before, to_behind):
        count = lax.axis_size(axis)
        inside = [(i, i ^ 1) for i in range(count)]
        both = [*pairs, *((j, i) for i, j in pairs)]
        near = lax.ppermute(jnp.where(even, to_behind, to_before), axis, inside)
        far = lax.ppermute(jnp.where(even, to_before, to_behind), axis, both)
        return jnp.where(even, far, near), jnp.where(even, near, far)

    whole_ring = [(i, (i + 1) % along_count) for i in range(1, along_count, 2)]
    half_rings = [
        (i, i // half_ring * half_ring + (i + 1) % half_ring) for i in range(1, along_count, 2)
    ]
    line = [(i, i + 1) for i in range(1, cross_count - 1, 2)]

    def over(value):
        return lax.ppermute(value, "along", across)

    def hbm(value):
        return pltpu.with_memory_space_constraint(value, pltpu.HBM)

    f32, bf16 = jnp.float32, jnp.bfloat16
    any_space = pl.BlockSpec(memory_space=pl.ANY)
    vmem = pl.BlockSpec(memory_space=pltpu.VMEM)
    smem = pl.BlockSpec(memory_space=pltpu.SMEM)
    limit = pltpu.CompilerParams(vmem_limit_bytes=24 * 1024 * 1024)

    def mover(kernel, name, shapes, operands, copies, scalars=0, scratch=()):
        return pl.pallas_call(
            kernel,
            out_shape=tuple(jax.ShapeDtypeStruct(shape, bf16) for shape in shapes),
            in_specs=[smem] * scalars + [any_space] * (len(operands) - scalars),
            out_specs=(vmem,) * len(shapes),
            scratch_shapes=[*scratch, pltpu.SemaphoreType.DMA((copies,))],
            compiler_params=limit,
            cost_estimate=pl.CostEstimate(
                flops=0, bytes_accessed=4 * sum(math.prod(s) for s in shapes), transcendentals=0
            ),
            name=name,
        )(*operands)

    place = jnp.stack([along_index, cross_index, window_start[0]]).astype(jnp.int32)

    lead = over(forward)
    own_lead, own_ends = mover(
        functools.partial(ends_kernel, lines),
        "ends",
        ((2 * LINE_RIM, cols), (2 * LINE_RIM, cols)),
        (hbm(forward), hbm(backward)),
        4,
    )
    ends = over(own_ends)
    cuts = (cols // 2, cols - lines - TILE)
    height = lines - 2 * LINE_RIM
    near = lines + 2 * EDGE * lines // TILE
    first_part, near_first, near_last = mover(
        functools.partial(cut_kernel, lines, cols, cuts[0]),
        "cut",
        ((height, cuts[0]), (near, TILE), (near, TILE)),
        (hbm(nadir_view), hbm(forward), hbm(backward), own_ends),
        7,
        scratch=[pltpu.VMEM((2, 2, lines, TILE), bf16)],
    )
    first_part = over(first_part)

    from_left, from_right = swap("cross", line, even_cross, near_first, near_last)
    depth = lines // 2 + 2 * LINE_RIM
    row_count = 4 * MODES // cross_count
    assert 2 * MODES % row_count == 0
    bands = pl.pallas_call(
        functools.partial(
            bands_kernel, lines, cols, total_lines, total_cols, half_ring, lag_floor
        ),
        out_shape=(
            jax.ShapeDtypeStruct((2, rows, depth), bf16),
            jax.ShapeDtypeStruct((2, WIDE + 2 * EDGE, cols), bf16),
            jax.ShapeDtypeStruct((8, cols), f32),
            jax.ShapeDtypeStruct((lines, 2 * MODES), f32),
            jax.ShapeDtypeStruct((row_count, lines), f32),
            jax.ShapeDtypeStruct((8, lines), f32),
            jax.ShapeDtypeStruct((2 * MODES, row_count), f32),
            jax.ShapeDtypeStruct((8, cols), f32),
        ),
        in_specs=[smem] + [vmem] * 5,
        out_specs=(vmem,) * 8,
        compiler_params=limit,
        cost_estimate=pl.CostEstimate(
            flops=20 * 300 * cols, bytes_accessed=4 * 300 * cols, transcendentals=0
        ),
        name="bands",
    )(
        place, lag_lines[None], hbm(band_offsets), hbm(along_weights), hbm(col_offsets),
        hbm(cross_weights),
    )
    line_bands, col_bands, levers, basis, rows_basis, upper, chosen, flags = bands
    folded = (NADIR_RIM, whole // 2 + 3 * TILE)
    first_lines, last_lines = pl.pallas_call(
        functools.partial(nadir_lines_kernel, lines, cols),
        out_shape=(jax.ShapeDtypeStruct(folded, bf16),) * 2,
        in_specs=[any_space, vmem, vmem, any_space],
        out_specs=(vmem, vmem),
        scratch_shapes=[pltpu.VMEM((2, NADIR_RIM, cols), bf16), pltpu.SemaphoreType.DMA((2,))],
        compiler_params=limit,
        cost_estimate=pl.CostEstimate(
            flops=0, bytes_accessed=16 * NADIR_RIM * cols, transcendentals=0
        ),
        name="nadir_lines",
    )(hbm(nadir_view), from_left, from_right, line_bands)
    nadir_above, nadir_below = swap("along", whole_ring, even_along, first_lines, last_lines)

    most_lines = 3 * LINE_RIM // 2
    down, up = pl.pallas_call(
        functools.partial(lines_kernel, lines),
        out_shape=(jax.ShapeDtypeStruct((most_lines, cols), bf16),) * 2,
        in_specs=[vmem] * 5,
        out_specs=(vmem, vmem),
        compiler_params=limit,
        cost_estimate=pl.CostEstimate(
            flops=0, bytes_accessed=16 * most_lines * cols, transcendentals=0
        ),
        name="lines",
    )(flags, own_lead, own_ends, lead, ends)
    slab_above, slab_below = swap("along", half_rings, even_along, down, up)

    second_part, third_part = pl.pallas_call(
        functools.partial(late_kernel, lines, cols, cuts),
        out_shape=(
            jax.ShapeDtypeStruct((height + 3 * EDGE, cuts[1] - cuts[0]), bf16),
            jax.ShapeDtypeStruct((height, cols - cuts[1]), bf16),
        ),
        in_specs=[any_space, vmem, vmem, vmem, vmem],
        out_specs=(vmem, vmem),
        scratch_shapes=[pltpu.SemaphoreType.DMA((2,))],
        compiler_params=limit,
        cost_estimate=pl.CostEstimate(flops=0, bytes_accessed=lines * cols, transcendentals=0),
        name="late_cut",
    )(hbm(backward), from_left, from_right, nadir_above, nadir_below)
    second_part, third_part = over(second_part), over(third_part)

    slopes, center, inverse, lever, sums = pl.pallas_call(
        functools.partial(prep_kernel, lines, cols, total_cols),
        out_shape=(
            jax.ShapeDtypeStruct((rows, cols), f32),
            jax.ShapeDtypeStruct((rows, cols), bf16),
            jax.ShapeDtypeStruct((lines, cols), f32),
            jax.ShapeDtypeStruct((lines, cols), f32),
            jax.ShapeDtypeStruct((8, lines), f32),
        ),
        in_specs=[smem] + [vmem] * 5 + [any_space],
        out_specs=(vmem,) * 5,
        scratch_shapes=[pltpu.VMEM((lines + 2 * NADIR_RIM, whole), bf16)],
        compiler_params=limit,
        cost_estimate=pl.CostEstimate(
            flops=2 * rows * cols * 512, bytes_accessed=12 * rows * cols, transcendentals=0
        ),
        name="prep",
    )(place, hbm(nadir_view), from_left, from_right, nadir_above, nadir_below, down)

    def run(name, jobs, crossed, so_far, last):
        fresh = so_far is None
        operands = [
            slopes, center, inverse, lever, line_bands, col_bands, levers, basis, slab_above, slab_below,
            ends, *crossed,
        ]
        specs = [vmem] * len(operands)
        if not fresh:
            operands.append(so_far)
            specs.append(vmem)
        scratch = []
        for _, _, width in jobs:
            scratch += [
                pltpu.VMEM((lines + 2 * LINE_RIM, width + 2 * TILE), bf16),
                pltpu.VMEM((rows, width + 2 * TILE), bf16),
                pltpu.VMEM((lines, width), bf16),
            ]
        done = sum(width for _, _, width in jobs)
        return pl.pallas_call(
            functools.partial(slab_kernel, lines, cols, cuts, jobs, len(crossed), fresh, last),
            out_shape=(
                *(
                    (pltpu.HBM((2, lines, cols), bf16),)
                    if fresh
                    else (jax.ShapeDtypeStruct((lines, width), bf16) for _, _, width in jobs)
                ),
                jax.ShapeDtypeStruct((8, TILE) if last else (2, lines, TILE), f32),
            ),
            in_specs=specs,
            out_specs=(any_space, vmem) if fresh else (vmem,) * (len(jobs) + 1),
            scratch_shapes=[pltpu.SemaphoreType.DMA((len(jobs),)), *scratch] if fresh else scratch,
            compiler_params=limit,
            cost_estimate=pl.CostEstimate(
                flops=2 * rows * (done + 256) * 900, bytes_accessed=20 * rows * done, transcendentals=0
            ),
            name=name,
        )(*operands)

    split = cuts[0] - TILE
    jobs = [(0, TILE, cols - 2 * TILE), (1, TILE, split - TILE)]
    parallax, pulls = run("inner", jobs, [lead, first_part], None, False)
    jobs = [(1, split, cuts[1] - TILE - split), (0, 0, TILE), (0, cols - TILE, TILE), (1, 0, TILE)]
    *kept, pulls = run("second", jobs, [lead, first_part, second_part], pulls, False)
    last_jobs = [(1, cuts[1] - TILE, cols - cuts[1] + TILE)]
    crossed = [lead, first_part, second_part, third_part]
    *last_kept, pulled = run("third", last_jobs, crossed, pulls, True)
    kept, jobs = [*kept, *last_kept], jobs + last_jobs
    parallax = pl.pallas_call(
        functools.partial(store_kernel, jobs),
        out_shape=pltpu.HBM((2, lines, cols), bf16),
        in_specs=[vmem] * len(kept) + [any_space],
        out_specs=any_space,
        scratch_shapes=[pltpu.SemaphoreType.DMA((len(kept),))],
        input_output_aliases={len(kept): 0},
        compiler_params=limit,
        cost_estimate=pl.CostEstimate(flops=0, bytes_accessed=2 * lines * cols, transcendentals=0),
        name="store",
    )(*kept, parallax)

    share = jnp.concatenate([sums, pulled], axis=1)
    shares = [share]
    assert cross_count & (cross_count - 1) == 0
    for shift_by in range(1, cross_count):
        pairs = [(i, (i + shift_by) % cross_count) for i in range(cross_count)]
        shares.append(lax.ppermute(share, "cross", pairs))
    scale_pull = 1.0 / (lines * total_cols) ** 0.5
    normal_gram, normal_rhs = pl.pallas_call(
        functools.partial(final_kernel, lines, scale_pull),
        out_shape=(
            jax.ShapeDtypeStruct((1, row_count, 4 * MODES), f32),
            jax.ShapeDtypeStruct((1, row_count), f32),
        ),
        in_specs=[vmem] * (4 + len(shares)),
        out_specs=(vmem, vmem),
        compiler_params=limit,
        name="final",
    )(basis, rows_basis, upper, chosen, *shares)
    return parallax, normal_gram, normal_rhs


def solution(mesh):
    placed = (
        P("along", "cross"),
        P("along", "cross"),
        P("along", "cross"),
        P(),
        P(None, None, "cross"),
        P(),
        P(None, "cross"),
        P(),
        P(),
    )
    return jax.shard_map(
        local,
        mesh=mesh,
        in_specs=placed,
        out_specs=(P(None, "along", "cross"), P("along", "cross", None), P("along", "cross")),
        check_vma=False,
    )
```
